32 devices in a mesh: rep: 4 (over z), fsdp: 8 (over y, x, core).
Axes of the slice: x: 2, y: 2, z: 4, core: 2. Of those that a mesh axis runs over, the one named last changes fastest.
Arguments:
- block_input: bfloat16 [65536, 768], P(('rep', 'fsdp')), may hold values from -6 to 6
- lengths: int32 [512, 4], P(('rep', 'fsdp')), may hold values from 8 to 40, as said below
- segments: int32 [65536], P(('rep', 'fsdp')), may hold values from 0 to 4, as said below
- gain_attn: bfloat16 [768], P('fsdp'), may hold values from 0.099609375 to 1.8984375
- w_qkv: bfloat16 [768, 2304], P('fsdp'), may hold values from -0.21875 to 0.21875
- w_attn_out: bfloat16 [768, 768], P('fsdp'), may hold values from -0.875 to 0.875
- gain_mlp: bfloat16 [768], P('fsdp'), may hold values from 0.099609375 to 1.8984375
- w_mlp_in: bfloat16 [768, 3072], P('fsdp'), may hold values from -0.21875 to 0.21875
- w_mlp_out: bfloat16 [3072, 768], P('fsdp'), may hold values from -0.15625 to 0.15625
- cotangent: bfloat16 [65536, 768], P(('rep', 'fsdp')), may hold values from -6 to 6
Outputs:
- block_output: bfloat16 [65536, 768], P(('rep', 'fsdp'))
- grad_input: bfloat16 [65536, 768], P(('rep', 'fsdp'))
- grad_gain_attn: float32 [768], P('fsdp')
- grad_qkv: float32 [768, 2304], P('fsdp')
- grad_attn_out: float32 [768, 768], P('fsdp')
- grad_gain_mlp: float32 [768], P('fsdp')
- grad_mlp_in: float32 [768, 3072], P('fsdp')
- grad_mlp_out: float32 [3072, 768], P('fsdp')
The draws below stay inside these ranges and needn't reach their ends.
Inputs may be any that keep to these rules, and one draw needn't show every extreme that they name: `lengths`: each packed row holds 4 sentences in order; one has exactly 40 tokens and the next one (cyclically) exactly 8; the rest of the row after them is padding. `segments`: within a packed row, token p has the number of sentences that end at or before p, so padding has 4; consistent with lengths.
All inputs are finite; a program needn't handle non-finite values.
Results may differ from the reference program's by a relative error of at most 0.01.
Values may be sent and summed in bfloat16 or wider, within the bound.
A program may use at most 192 MiB of HBM per device.

```python
import math
from functools import partial
import jax
import jax.numpy as jnp
from jax import lax

D = 768
HEADS = 12
HEAD = 64
FF = 3072
L = 128
NSEG = 4
LEAST = 8
MOST = 40
ROWS = 512
TOKENS = 65536


def sentence_lengths(key):
    key_fill, key_long = jax.random.split(key, 2)
    filler = jax.random.randint(key_fill, (ROWS, NSEG), LEAST, MOST + 1)
    longest_at = jax.random.randint(key_long, (ROWS, 1), 0, NSEG)
    place = jnp.arange(NSEG, dtype=jnp.int32)[None, :]
    filler = jnp.where(place == longest_at, MOST, filler)
    filler = jnp.where(place == (longest_at + 1) % NSEG, LEAST, filler)
    return filler.astype(jnp.int32)


def draw_lengths(key, part):
    shared = sentence_lengths(key)
    return shared


def draw_segments(key, part):
    shared = sentence_lengths(key)
    endings = jnp.cumsum(shared, axis=1)
    place = jnp.arange(L, dtype=jnp.int32)
    labels = jnp.sum((place[None, :, None] >= endings[:, None, :]).astype(jnp.int32), axis=2)
    return labels.reshape(ROWS * L).astype(jnp.int32)


def shard_levels(own_key, extent, cuts, least, top_value):
    factor_of, own = 1.0, jax.random.fold_in(own_key, 6)
    for dim, blocks in cuts:
        draws = jnp.exp(jax.random.uniform(jax.random.fold_in(own, dim), (blocks,), jnp.float32, least / len(cuts), top_value / len(cuts)))
        factor_of = factor_of * jnp.repeat(draws, extent[dim] // blocks).reshape([-1 if axis == dim else 1 for axis in range(len(extent))])
    return factor_of


def scatter_about(own_key, dims, deviation, reach, cuts=(), kind=jnp.bfloat16):
    level = shard_levels(own_key, dims, cuts, -0.22, 0.18) if cuts else 1.0
    result = jax.random.normal(own_key, dims, jnp.float32) * deviation * level
    return jnp.minimum(jnp.maximum(result, -reach), reach).astype(kind)


def setup_inputs(seed: int = 0) -> dict:
    arg_keys = jax.random.split(jax.random.key(seed), 11)
    block_input = scatter_about(arg_keys[0], (TOKENS, D), 1.0, 6.0, ((0, 32),))
    lengths = draw_lengths(jax.random.fold_in(arg_keys[10], 71), 0)
    segments = draw_segments(jax.random.fold_in(arg_keys[10], 71), 0)
    gain_attn = jnp.clip(1.0 + 0.18 * jax.random.normal(arg_keys[3], (D,), jnp.float32), 0.099609375, 1.8984375).astype(jnp.bfloat16)
    w_qkv = scatter_about(arg_keys[4], (D, 3 * D), D ** -0.5, 0.21875, ((0, 8),))
    w_attn_out = scatter_about(arg_keys[5], (D, D), (D // 16) ** -0.5, 0.875, ((0, 8),))
    gain_mlp = jnp.clip(1.0 + 0.18 * jax.random.normal(arg_keys[6], (D,), jnp.float32), 0.099609375, 1.8984375).astype(jnp.bfloat16)
    w_mlp_in = scatter_about(arg_keys[7], (D, FF), D ** -0.5, 0.21875, ((0, 8),))
    w_mlp_out = scatter_about(arg_keys[8], (FF, D), (FF // 2) ** -0.5, 0.15625, ((0, 8),))
    cotangent = scatter_about(arg_keys[9], (TOKENS, D), 1.0, 6.0, ((0, 32),))
    return {"block_input": block_input, "lengths": lengths, "segments": segments, "gain_attn": gain_attn, "w_qkv": w_qkv, "w_attn_out": w_attn_out, "gain_mlp": gain_mlp, "w_mlp_in": w_mlp_in, "w_mlp_out": w_mlp_out, "cotangent": cotangent}


@jax.custom_vjp
def low(v):
    return lax.optimization_barrier(v.astype(jnp.bfloat16)).astype(jnp.float32)

@jax.custom_vjp
def low_back(v):
    return v

def low_keep(v):
    return (low(v), None)

def low_pass(kept, grad):
    return (grad,)

def back_keep(v):
    return (v, None)

def back_low(kept, grad):
    return (low(grad),)
low.defvjp(low_keep, low_pass)
low_back.defvjp(back_keep, back_low)
EPS = 1e-05
NEGATIVE = -1e+30
HIGHEST = lax.Precision.HIGHEST

def product(left, right):
    return jnp.dot(left, right, precision=HIGHEST, preferred_element_type=jnp.float32)

def normalize(values, gain):
    middle = lax.optimization_barrier(jnp.mean(values, axis=-1, keepdims=True))
    centred = values - middle
    spread = lax.optimization_barrier(jnp.mean(centred * centred, axis=-1, keepdims=True))
    return centred * lax.rsqrt(spread + EPS) * gain

def permitted(lengths, segments):
    row_count = lengths.shape[0]
    row_span = segments.shape[0] // row_count
    labels = segments.reshape(row_count, row_span)
    filled = lax.optimization_barrier(jnp.sum(lengths, axis=1))
    place = jnp.arange(row_span, dtype=jnp.int32)
    real_key = place[None, :] < filled[:, None]
    same = labels[:, :, None] == labels[:, None, :]
    itself = place[:, None] == place[None, :]
    return same & (real_key[:, None, :] | itself[None])

def attend(block):
    stacked, allowed = block
    queries = stacked[:, :, 0]
    key_rows = stacked[:, :, 1]
    value_rows = stacked[:, :, 2]
    raw_scores = low_back(jnp.einsum('gqhd,gkhd->ghqk', queries, key_rows, precision=HIGHEST))
    scores = jnp.where(allowed[:, None], raw_scores * HEAD ** (-0.5), NEGATIVE)
    highest = lax.optimization_barrier(jnp.max(scores, axis=-1, keepdims=True))
    raised = jnp.exp(scores - highest)
    weights = low(raised / lax.optimization_barrier(jnp.sum(raised, axis=-1, keepdims=True)))
    return jnp.einsum('ghqk,gkhd->gqhd', weights, value_rows, precision=HIGHEST)

def forward(allowed, block_input, gain_attn, w_qkv, w_attn_out, gain_mlp, w_mlp_in, w_mlp_out):
    token_count, width = block_input.shape
    normed = low(normalize(block_input, gain_attn))
    projected = low(low_back(product(normed, w_qkv)))
    row_count = allowed.shape[0]
    group = math.gcd(row_count, max(1, 4096 // L))
    stacked = projected.reshape(row_count // group, group, L, 3, HEADS, HEAD)
    mixed = lax.map(jax.checkpoint(attend), (stacked, allowed.reshape(row_count // group, group, L, L)))
    mixed = low(low_back(mixed.reshape(token_count, width)))
    middle = block_input + low_back(product(mixed, w_attn_out))
    normed_mlp = low(normalize(middle, gain_mlp))
    hidden = low_back(product(normed_mlp, w_mlp_in))
    active = low(jax.nn.gelu(hidden, approximate=True))
    return middle + low_back(product(active, w_mlp_out))

def reference(block_input, lengths, segments, gain_attn, w_qkv, w_attn_out, gain_mlp, w_mlp_in, w_mlp_out, cotangent):
    allowed = permitted(lengths, segments)
    inputs = tuple((array.astype(jnp.float32) for array in (block_input, gain_attn, w_qkv, w_attn_out, gain_mlp, w_mlp_in, w_mlp_out)))
    output, pullback = jax.vjp(partial(forward, allowed), *inputs)
    grads = pullback(cotangent.astype(jnp.float32))
    return (output.astype(jnp.bfloat16), grads[0].astype(jnp.bfloat16), grads[1], grads[2], grads[3], grads[4], grads[5], grads[6])
```

```python
import functools, math
import jax, jax.numpy as jnp
from jax import lax
from jax.experimental import pallas as pl
from jax.experimental.pallas import tpu as pltpu
from jax.sharding import PartitionSpec as P
bf = jnp.bfloat16
f32 = jnp.float32
EPS = 1e-05
NEG = -1e30
SPAN = 128
TILE = 256
VMEM = 60 * 1024 * 1024
SCALE = 64 ** -0.5
LOG2E = math.log2(math.e)
GC = math.sqrt(2.0 / math.pi)
GK = 0.044715


def nn(a, b):
    return lax.dot_general(a, b, (((1,), (0,)), ((), ())), preferred_element_type=f32)


def nt(a, b):
    return lax.dot_general(a, b, (((1,), (1,)), ((), ())), preferred_element_type=f32)


def tn(a, b):
    return lax.dot_general(a, b, (((0,), (0,)), ((), ())), preferred_element_type=f32)


def moments(v):
    c = v - jnp.mean(v, axis=-1, keepdims=True)
    r = lax.rsqrt(jnp.mean(c * c, axis=-1, keepdims=True) + EPS)
    return c * r, r


def norm_back(e, n, r, g):
    s = e * g
    inner = s - jnp.mean(s, axis=-1, keepdims=True) - n * jnp.mean(s * n, axis=-1, keepdims=True)
    return inner * r


def split_heads(t):
    low = lax.broadcasted_iota(jnp.int32, t.shape, 1) < 64
    zero = jnp.zeros_like(t)
    return jnp.concatenate([jnp.where(low, t, zero), jnp.where(low, zero, t)], axis=0)


def stack_lanes(t):
    return jnp.concatenate([t[:, :SPAN], t[:, SPAN:]], axis=0)


def permitted(lengths, row):
    ends = []
    total = 0
    for k in range(4):
        total = total + lengths[row, k]
        ends.append(total)
    key = lax.broadcasted_iota(jnp.int32, (SPAN, SPAN), 0)
    query = lax.broadcasted_iota(jnp.int32, (SPAN, SPAN), 1)
    one, zero = jnp.int32(1), jnp.int32(0)
    seg_key = sum(jnp.where(key >= e, one, zero) for e in ends)
    seg_query = sum(jnp.where(query >= e, one, zero) for e in ends)
    return (seg_key == seg_query) & ((key < total) | (key == query))


def attend(qkv, mask):
    mask2 = jnp.concatenate([mask, mask], axis=1)
    probs, mixed = [], []
    for p in range(6):
        q2, k2, v2 = qkv(p * 128), qkv(768 + p * 128), qkv(1536 + p * 128)
        s = jnp.where(mask2, nt(k2, split_heads(q2)), NEG)
        top = jnp.max(s, axis=0, keepdims=True)
        e = jnp.exp2((s - top) * (SCALE * LOG2E))
        w = (e * (1.0 / jnp.sum(e, axis=0, keepdims=True))).astype(bf)
        probs.append(w)
        mixed.append(tn(stack_lanes(w), split_heads(v2)).astype(bf))
    return probs, mixed


def attend_back(qkv, w, do2, p):
    q2, k2, v2 = qkv(p * 128), qkv(768 + p * 128), qkv(1536 + p * 128)
    do_bd = split_heads(do2)
    dv = nn(w, do_bd)
    dp = nt(v2, do_bd)
    pf = w.astype(f32)
    pd = pf * dp
    inner = jnp.sum(pd, axis=0, keepdims=True)
    draw = ((pd - pf * inner) * SCALE).astype(bf)
    dq = tn(stack_lanes(draw), split_heads(k2))
    dk = nn(draw, split_heads(q2))
    return dq.astype(bf), dk.astype(bf), dv.astype(bf)


def kernel_ab(lengths, x, gain, w_qkv, qkv_out, probs_out, o_out):
    i = pl.program_id(0)
    n, _ = moments(x[...].astype(f32))
    u = (n * gain[...]).astype(bf)
    qkv_out[...] = nn(u, w_qkv[...]).astype(bf)
    for rr in range(TILE // SPAN):
        rows = slice(rr * SPAN, (rr + 1) * SPAN)
        mask = permitted(lengths, i * (TILE // SPAN) + rr)
        probs, mixed = attend(lambda c: qkv_out[rows, c : c + 128], mask)
        for p in range(6):
            probs_out[rr, p] = probs[p]
            o_out[rows, p * 128 : (p + 1) * 128] = mixed[p]


def gelu_both(t):
    t2 = t * t
    th = jnp.tanh(t * (GC + (GC * GK) * t2))
    half = 0.5 + 0.5 * th
    a = t * half
    slope = half + (0.5 * t) * (1.0 - th * th) * (GC + (3.0 * GC * GK) * t2)
    return a, slope


FC = 768


def kernel_c(x, o, dy, gain, w_ao, w_in, w_out, y_out, wn_out, a_out, dz_out, dh_out, do_out, gg_out):
    i = pl.program_id(0)
    h = x[...].astype(f32) + nn(o[...], w_ao[...])
    n, r = moments(h)
    g = gain[...]
    wn = (n * g).astype(bf)
    wn_out[...] = wn
    dm = dy[...]
    y = h
    dw = None
    for j in range(w_in.shape[1] // FC):
        cols = slice(j * FC, (j + 1) * FC)
        a, slope = gelu_both(nn(wn, w_in[:, cols]))
        a = a.astype(bf)
        a_out[:, cols] = a
        y = y + nn(a, w_out[cols, :])
        dz = (nt(dm, w_out[cols, :]) * slope).astype(bf)
        dz_out[:, cols] = dz
        t = nt(dz, w_in[:, cols])
        dw = t if dw is None else dw + t
    y_out[...] = y.astype(bf)
    dh = dm.astype(f32) + norm_back(dw, n, r, g)
    dh_out[...] = dh
    do_out[...] = nt(dh.astype(bf), w_ao[...]).astype(bf)
    part = jnp.sum((dw * n).reshape(-1, 8, dw.shape[1]), axis=0)

    @pl.when(i == 0)
    def _():
        gg_out[...] = part

    @pl.when(i > 0)
    def _():
        gg_out[...] += part


def kernel_d1(wn, dz, g):
    g[...] = tn(wn[...], dz[...]).astype(g.dtype)


def kernel_e(qkv, probs, do, dqkv):
    for rr in range(TILE // SPAN):
        rows = slice(rr * SPAN, (rr + 1) * SPAN)
        for p in range(6):
            cols = slice(p * 128, (p + 1) * 128)
            dq, dk, dv = attend_back(lambda c: qkv[rows, c : c + 128], probs[rr, p], do[rows, cols], p)
            dqkv[rows, p * 128 : p * 128 + 128] = dq
            dqkv[rows, 768 + p * 128 : 768 + p * 128 + 128] = dk
            dqkv[rows, 1536 + p * 128 : 1536 + p * 128 + 128] = dv


def kernel_f(x, dqkv, dh, gain, w_qkv, dx_out, gg_out):
    i = pl.program_id(0)
    n, r = moments(x[...].astype(f32))
    du = nt(dqkv[...], w_qkv[...])
    dx_out[...] = (dh[...] + norm_back(du, n, r, gain[...])).astype(bf)
    part = jnp.sum((du * n).reshape(-1, 8, du.shape[1]), axis=0)

    @pl.when(i == 0)
    def _():
        gg_out[...] = part

    @pl.when(i > 0)
    def _():
        gg_out[...] += part


def kernel_gq(x, gain, dqkv, g, u):
    @pl.when(pl.program_id(0) == 0)
    def _():
        for t in range(x.shape[0] // TILE):
            rows = slice(t * TILE, (t + 1) * TILE)
            n, _ = moments(x[rows].astype(f32))
            u[rows] = (n * gain[...]).astype(bf)

    g[...] = tn(u[...], dqkv[...]).astype(g.dtype)


def whole(shape):
    return pl.BlockSpec(shape, lambda i: (0,) * len(shape), pipeline_mode=pl.Buffered(1))


def rows_of(cols, tile=TILE):
    return pl.BlockSpec((tile, cols), lambda i: (i, 0))


def call(body, name, grid, in_specs, out_specs, out_shape, flops, nbytes, scratch=()):
    return pl.pallas_call(
        body,
        name=name,
        grid=grid,
        in_specs=in_specs,
        out_specs=out_specs,
        out_shape=out_shape,
        scratch_shapes=scratch,
        cost_estimate=pl.CostEstimate(flops=flops, bytes_accessed=nbytes, transcendentals=0),
        compiler_params=pltpu.CompilerParams(vmem_limit_bytes=VMEM),
    )


def sds(*shape, dtype=bf):
    return jax.ShapeDtypeStruct(shape, dtype)


def forward_attention(x, lengths, g1, w_qkv):
    T, D = x.shape
    rows = T // SPAN
    per = TILE // SPAN
    return call(
        kernel_ab, "attention_forward", (T // TILE,),
        [pl.BlockSpec(memory_space=pltpu.SMEM), rows_of(D), whole((1, D)), whole(w_qkv.shape)],
        [rows_of(3 * D), pl.BlockSpec((per, 6, SPAN, 2 * SPAN), lambda i: (i, 0, 0, 0)), rows_of(D)],
        [sds(T, 3 * D), sds(rows, 6, SPAN, 2 * SPAN), sds(T, D)],
        12 * T * D * D, 30 << 20,
    )(lengths, x, g1, w_qkv)


def mlp_both(x, o, dy, g2, w_ao, w_in, w_out):
    T, D = x.shape
    F = w_in.shape[1]
    return call(
        kernel_c, "mlp_both", (T // TILE,),
        [rows_of(D), rows_of(D), rows_of(D), whole((1, D)), whole(w_ao.shape), whole(w_in.shape), whole(w_out.shape)],
        [rows_of(D), rows_of(D), rows_of(F), rows_of(F), rows_of(D), rows_of(D), pl.BlockSpec((8, D), lambda i: (0, 0))],
        [sds(T, D), sds(T, D), sds(T, F), sds(T, F), sds(T, D, dtype=f32), sds(T, D), sds(8, D, dtype=f32)],
        8 * T * D * F + 4 * T * D * D, 60 << 20,
    )(x, o, dy, g2, w_ao, w_in, w_out)


def weight_grad(left, right, name, tile, out=bf, by="right"):
    T, M = left.shape
    N = right.shape[1]
    if by == "right":
        ins = [whole((T, M)), pl.BlockSpec((T, tile), lambda i: (0, i))]
        outs = pl.BlockSpec((M, tile), lambda i: (0, i))
        grid = (N // tile,)
    else:
        ins = [pl.BlockSpec((T, tile), lambda i: (0, i)), whole((T, N))]
        outs = pl.BlockSpec((tile, N), lambda i: (i, 0))
        grid = (M // tile,)
    return call(kernel_d1, name, grid, ins, outs, sds(M, N, dtype=out), 2 * T * M * N, 2 * (T * M + T * N + M * N))(left, right)


def attention_back(qkv, probs, do):
    T, D = do.shape
    per = TILE // SPAN
    return call(
        kernel_e, "attention_backward", (T // TILE,),
        [rows_of(3 * D), pl.BlockSpec((per, 6, SPAN, 2 * SPAN), lambda i: (i, 0, 0, 0)), rows_of(D)],
        rows_of(3 * D), sds(T, 3 * D), 8 * T * D * D, 30 << 20,
    )(qkv, probs, do)


def input_grad(x, dqkv, dh, g1, w_qkv):
    T, D = x.shape
    return call(
        kernel_f, "input_grad", (T // TILE,),
        [rows_of(D), rows_of(3 * D), rows_of(D), whole((1, D)), whole(w_qkv.shape)],
        [rows_of(D), pl.BlockSpec((8, D), lambda i: (0, 0))],
        [sds(T, D), sds(8, D, dtype=f32)],
        6 * T * D * D, 30 << 20,
    )(x, dqkv, dh, g1, w_qkv)


def qkv_grad(x, g1, dqkv, tile=768, out=bf):
    T, D = x.shape
    N = dqkv.shape[1]
    return call(
        kernel_gq, "qkv_grad", (N // tile,),
        [whole((T, D)), whole((1, D)), pl.BlockSpec((T, tile), lambda i: (0, i))],
        pl.BlockSpec((D, tile), lambda i: (0, i)), sds(D, N, dtype=out), 2 * T * D * N, 20 << 20,
        scratch=[pltpu.VMEM((T, D), bf)],
    )(x, g1, dqkv)


def shards(x, lengths, segments, gain_attn, w_qkv, w_attn_out, gain_mlp, w_mlp_in, w_mlp_out, dy):
    D = x.shape[1]
    gains = jnp.stack([gain_attn, gain_mlp], axis=1)
    packed = jnp.concatenate([w_qkv, jnp.pad(gains, ((0, 0), (0, 126)))], axis=1)
    gather = lambda v: lax.all_gather(v, "fsdp", axis=0, tiled=True)
    packed = gather(packed)
    wq = packed[:, : 3 * D]
    g1 = packed[:, 3 * D].astype(f32)[None]
    g2 = packed[:, 3 * D + 1].astype(f32)[None]
    wo, wi, wt = gather(w_attn_out), gather(w_mlp_in), gather(w_mlp_out)
    qkv, probs, o = forward_attention(x, lengths, g1, wq)
    y, wn, a, dz, dh, do, gg2 = mlp_both(x, o, dy, g2, wo, wi, wt)
    scatter = lambda v: lax.psum_scatter(v, "fsdp", scatter_dimension=0, tiled=True)
    gwt = scatter(weight_grad(a, dy, "mlp_out_grad", 768, bf, "left"))
    gwi = scatter(weight_grad(wn, dz, "mlp_in_grad", 768))
    gwo = scatter(weight_grad(o, dh.astype(bf), "attn_out_grad", 768))
    dqkv = attention_back(qkv, probs, do)
    gq = qkv_grad(x, g1, dqkv)
    dx, gg1 = input_grad(x, dqkv, dh, g1, wq)
    ends = jnp.stack([gg1.sum(0), gg2.sum(0)], axis=1).astype(bf)
    gq = scatter(jnp.concatenate([gq, jnp.pad(ends, ((0, 0), (0, 126)))], axis=1))
    gwt, gwi, gwo, gq = lax.psum((gwt, gwi, gwo, gq), "rep")
    gwt, gwi, gwo, gq = (v.astype(f32) for v in (gwt, gwi, gwo, gq))
    return y, dx, gq[:, 3 * D], gq[:, : 3 * D], gwo, gq[:, 3 * D + 1], gwi, gwt


def solution(mesh):
    tokens, cut, vec = P(("rep", "fsdp"), None), P("fsdp", None), P("fsdp")
    return jax.shard_map(
        shards,
        mesh=mesh,
        in_specs=(tokens, tokens, P(("rep", "fsdp")), vec, cut, cut, vec, cut, cut, tokens),
        out_specs=(tokens, tokens, vec, cut, cut, vec, cut, cut),
        check_vma=False,
    )
```

```python
import functools, math
import jax, jax.numpy as jnp
from jax import lax
from jax.experimental import pallas as pl
from jax.experimental.pallas import tpu as pltpu
from jax.sharding import PartitionSpec as P
bf = jnp.bfloat16
f32 = jnp.float32
EPS = 1e-05
NEG = -1e30
SPAN = 128
TILE = 256
VMEM = 60 * 1024 * 1024
SCALE = 64 ** -0.5
LOG2E = math.log2(math.e)
GC = math.sqrt(2.0 / math.pi)
GK = 0.044715


def nn(a, b):
    return lax.dot_general(a, b, (((1,), (0,)), ((), ())), preferred_element_type=f32)


def nt(a, b):
    return lax.dot_general(a, b, (((1,), (1,)), ((), ())), preferred_element_type=f32)


def tn(a, b):
    return lax.dot_general(a, b, (((0,), (0,)), ((), ())), preferred_element_type=f32)


def moments(v):
    c = v - jnp.mean(v, axis=-1, keepdims=True)
    r = lax.rsqrt(jnp.mean(c * c, axis=-1, keepdims=True) + EPS)
    return c * r, r


def norm_back(e, n, r, g):
    s = e * g
    inner = s - jnp.mean(s, axis=-1, keepdims=True) - n * jnp.mean(s * n, axis=-1, keepdims=True)
    return inner * r


def split_heads(t):
    low = lax.broadcasted_iota(jnp.int32, t.shape, 1) < 64
    zero = jnp.zeros_like(t)
    return jnp.concatenate([jnp.where(low, t, zero), jnp.where(low, zero, t)], axis=0)


def stack_lanes(t):
    return jnp.concatenate([t[:, :SPAN], t[:, SPAN:]], axis=0)


def permitted(lengths, row):
    ends = []
    total = 0
    for k in range(4):
        total = total + lengths[row, k]
        ends.append(total)
    key = lax.broadcasted_iota(jnp.int32, (SPAN, SPAN), 0)
    query = lax.broadcasted_iota(jnp.int32, (SPAN, SPAN), 1)
    one, zero = jnp.int32(1), jnp.int32(0)
    seg_key = sum(jnp.where(key >= e, one, zero) for e in ends)
    seg_query = sum(jnp.where(query >= e, one, zero) for e in ends)
    return (seg_key == seg_query) & ((key < total) | (key == query))


def attend(qkv, mask):
    mask2 = jnp.concatenate([mask, mask], axis=1)
    probs, mixed = [], []
    for p in range(6):
        q2, k2, v2 = qkv(p * 128), qkv(768 + p * 128), qkv(1536 + p * 128)
        s = jnp.where(mask2, nt(k2, split_heads(q2)), NEG)
        top = jnp.max(s, axis=0, keepdims=True)
        e = jnp.exp2((s - top) * (SCALE * LOG2E))
        w = (e * (1.0 / jnp.sum(e, axis=0, keepdims=True))).astype(bf)
        probs.append(w)
        mixed.append(tn(stack_lanes(w), split_heads(v2)).astype(bf))
    return probs, mixed


def attend_back(qkv, w, do2, p):
    q2, k2, v2 = qkv(p * 128), qkv(768 + p * 128), qkv(1536 + p * 128)
    do_bd = split_heads(do2)
    dv = nn(w, do_bd)
    dp = nt(v2, do_bd)
    pf = w.astype(f32)
    pd = pf * dp
    inner = jnp.sum(pd, axis=0, keepdims=True)
    draw = ((pd - pf * inner) * SCALE).astype(bf)
    dq = tn(stack_lanes(draw), split_heads(k2))
    dk = nn(draw, split_heads(q2))
    return dq.astype(bf), dk.astype(bf), dv.astype(bf)


def kernel_ab(lengths, x, gain, w_qkv, qkv_out, probs_out, o_out):
    i = pl.program_id(0)
    n, _ = moments(x[...].astype(f32))
    u = (n * gain[...]).astype(bf)
    qkv_out[...] = nn(u, w_qkv[...]).astype(bf)
    for rr in range(TILE // SPAN):
        rows = slice(rr * SPAN, (rr + 1) * SPAN)
        mask = permitted(lengths, i * (TILE // SPAN) + rr)
        probs, mixed = attend(lambda c: qkv_out[rows, c : c + 128], mask)
        for p in range(6):
            probs_out[rr, p] = probs[p]
            o_out[rows, p * 128 : (p + 1) * 128] = mixed[p]


def gelu_both(t):
    t2 = t * t
    th = jnp.tanh(t * (GC + (GC * GK) * t2))
    half = 0.5 + 0.5 * th
    a = t * half
    slope = half + (0.5 * t) * (1.0 - th * th) * (GC + (3.0 * GC * GK) * t2)
    return a, slope


FC = 768


def kernel_c(x, o, dy, gain, w_ao, w_in, w_out, y_out, wn_out, a_out, dz_out, dh_out, do_out, gg_out):
    i = pl.program_id(0)
    h = x[...].astype(f32) + nn(o[...], w_ao[...])
    n, r = moments(h)
    g = gain[...]
    wn = (n * g).astype(bf)
    wn_out[...] = wn
    dm = dy[...]
    y = h
    dw = None
    for j in range(w_in.shape[1] // FC):
        cols = slice(j * FC, (j + 1) * FC)
        a, slope = gelu_both(nn(wn, w_in[:, cols]))
        a = a.astype(bf)
        a_out[:, cols] = a
        y = y + nn(a, w_out[cols, :])
        dz = (nt(dm, w_out[cols, :]) * slope).astype(bf)
        dz_out[:, cols] = dz
        t = nt(dz, w_in[:, cols])
        dw = t if dw is None else dw + t
    y_out[...] = y.astype(bf)
    dh = dm.astype(f32) + norm_back(dw, n, r, g)
    dh_out[...] = dh
    do_out[...] = nt(dh.astype(bf), w_ao[...]).astype(bf)
    part = jnp.sum((dw * n).reshape(-1, 8, dw.shape[1]), axis=0)

    @pl.when(i == 0)
    def _():
        gg_out[...] = part

    @pl.when(i > 0)
    def _():
        gg_out[...] += part


def kernel_d1(wn, dz, g):
    g[...] = tn(wn[...], dz[...]).astype(g.dtype)


def kernel_e(qkv, probs, do, dqkv):
    for rr in range(TILE // SPAN):
        rows = slice(rr * SPAN, (rr + 1) * SPAN)
        for p in range(6):
            cols = slice(p * 128, (p + 1) * 128)
            dq, dk, dv = attend_back(lambda c: qkv[rows, c : c + 128], probs[rr, p], do[rows, cols], p)
            dqkv[rows, p * 128 : p * 128 + 128] = dq
            dqkv[rows, 768 + p * 128 : 768 + p * 128 + 128] = dk
            dqkv[rows, 1536 + p * 128 : 1536 + p * 128 + 128] = dv


def kernel_f(x, dqkv, dh, gain, w_qkv, dx_out, gg_out):
    i = pl.program_id(0)
    n, r = moments(x[...].astype(f32))
    du = nt(dqkv[...], w_qkv[...])
    dx_out[...] = (dh[...] + norm_back(du, n, r, gain[...])).astype(bf)
    part = jnp.sum((du * n).reshape(-1, 8, du.shape[1]), axis=0)

    @pl.when(i == 0)
    def _():
        gg_out[...] = part

    @pl.when(i > 0)
    def _():
        gg_out[...] += part


def kernel_gq(x, gain, dqkv, g, u):
    @pl.when(pl.program_id(0) == 0)
    def _():
        for t in range(x.shape[0] // TILE):
            rows = slice(t * TILE, (t + 1) * TILE)
            n, _ = moments(x[rows].astype(f32))
            u[rows] = (n * gain[...]).astype(bf)

    g[...] = tn(u[...], dqkv[...]).astype(g.dtype)


def whole(shape):
    return pl.BlockSpec(shape, lambda i: (0,) * len(shape), pipeline_mode=pl.Buffered(1))


def rows_of(cols, tile=TILE):
    return pl.BlockSpec((tile, cols), lambda i: (i, 0))


def call(body, name, grid, in_specs, out_specs, out_shape, flops, nbytes, scratch=()):
    return pl.pallas_call(
        body,
        name=name,
        grid=grid,
        in_specs=in_specs,
        out_specs=out_specs,
        out_shape=out_shape,
        scratch_shapes=scratch,
        cost_estimate=pl.CostEstimate(flops=flops, bytes_accessed=nbytes, transcendentals=0),
        compiler_params=pltpu.CompilerParams(vmem_limit_bytes=VMEM),
    )


def sds(*shape, dtype=bf):
    return jax.ShapeDtypeStruct(shape, dtype)


def forward_attention(x, lengths, g1, w_qkv):
    T, D = x.shape
    rows = T // SPAN
    per = TILE // SPAN
    return call(
        kernel_ab, "attention_forward", (T // TILE,),
        [pl.BlockSpec(memory_space=pltpu.SMEM), rows_of(D), whole((1, D)), whole(w_qkv.shape)],
        [rows_of(3 * D), pl.BlockSpec((per, 6, SPAN, 2 * SPAN), lambda i: (i, 0, 0, 0)), rows_of(D)],
        [sds(T, 3 * D), sds(rows, 6, SPAN, 2 * SPAN), sds(T, D)],
        12 * T * D * D, 30 << 20,
    )(lengths, x, g1, w_qkv)


def mlp_both(x, o, dy, g2, w_ao, w_in, w_out):
    T, D = x.shape
    F = w_in.shape[1]
    return call(
        kernel_c, "mlp_both", (T // TILE,),
        [rows_of(D), rows_of(D), rows_of(D), whole((1, D)), whole(w_ao.shape), whole(w_in.shape), whole(w_out.shape)],
        [rows_of(D), rows_of(D), rows_of(F), rows_of(F), rows_of(D), rows_of(D), pl.BlockSpec((8, D), lambda i: (0, 0))],
        [sds(T, D), sds(T, D), sds(T, F), sds(T, F), sds(T, D, dtype=f32), sds(T, D), sds(8, D, dtype=f32)],
        8 * T * D * F + 4 * T * D * D, 60 << 20,
    )(x, o, dy, g2, w_ao, w_in, w_out)


def weight_grad(left, right, name, tile, out=bf, by="right"):
    T, M = left.shape
    N = right.shape[1]
    if by == "right":
        ins = [whole((T, M)), pl.BlockSpec((T, tile), lambda i: (0, i))]
        outs = pl.BlockSpec((M, tile), lambda i: (0, i))
        grid = (N // tile,)
    else:
        ins = [pl.BlockSpec((T, tile), lambda i: (0, i)), whole((T, N))]
        outs = pl.BlockSpec((tile, N), lambda i: (i, 0))
        grid = (M // tile,)
    return call(kernel_d1, name, grid, ins, outs, sds(M, N, dtype=out), 2 * T * M * N, 2 * (T * M + T * N + M * N))(left, right)


def attention_back(qkv, probs, do):
    T, D = do.shape
    per = TILE // SPAN
    return call(
        kernel_e, "attention_backward", (T // TILE,),
        [rows_of(3 * D), pl.BlockSpec((per, 6, SPAN, 2 * SPAN), lambda i: (i, 0, 0, 0)), rows_of(D)],
        rows_of(3 * D), sds(T, 3 * D), 8 * T * D * D, 30 << 20,
    )(qkv, probs, do)


def input_grad(x, dqkv, dh, g1, w_qkv):
    T, D = x.shape
    return call(
        kernel_f, "input_grad", (T // TILE,),
        [rows_of(D), rows_of(3 * D), rows_of(D), whole((1, D)), whole(w_qkv.shape)],
        [rows_of(D), pl.BlockSpec((8, D), lambda i: (0, 0))],
        [sds(T, D), sds(8, D, dtype=f32)],
        6 * T * D * D, 30 << 20,
    )(x, dqkv, dh, g1, w_qkv)


def qkv_grad(x, g1, dqkv, tile=768, out=bf):
    T, D = x.shape
    N = dqkv.shape[1]
    return call(
        kernel_gq, "qkv_grad", (N // tile,),
        [whole((T, D)), whole((1, D)), pl.BlockSpec((T, tile), lambda i: (0, i))],
        pl.BlockSpec((D, tile), lambda i: (0, i)), sds(D, N, dtype=out), 2 * T * D * N, 20 << 20,
        scratch=[pltpu.VMEM((T, D), bf)],
    )(x, g1, dqkv)
MESH = pl.DeviceIdType.MESH
MESSAGES = {
    "c0": (1, 0, None), "x0": (2, 0, None), "y0": (4, 0, None),
    "xc": (1, 2, None), "yc": (1, 4, None), "xf": (4, 2, 0), "yf": (2, 4, 1),
    "dA": (1, 6, 0), "dB": (1, 6, 1),
}
ORDER = list(MESSAGES)


def halves(n):
    left = (n // 256) * 128
    return (left, n - left)


class Gather:
    def __init__(self, shard, full, send, recv, local, me, rep):
        self.shard, self.full, self.send, self.recv, self.local, self.me, self.rep = shard, full, send, recv, local, me, rep

    def copy(self, name):
        k = ORDER.index(name)
        partner, whose, part = MESSAGES[name]
        piece = self.me ^ whose
        src, dst = self.full.at[piece], self.full.at[piece]
        if whose == 0:
            src = self.shard
        if part is not None:
            left, right = halves(self.full.shape[2])
            cols = pl.ds(0, left) if part == 0 else pl.ds(left, right)
            src, dst = src.at[:, cols], dst.at[:, cols]
        return pltpu.make_async_remote_copy(
            src_ref=src, dst_ref=dst, send_sem=self.send.at[k], recv_sem=self.recv.at[k],
            device_id=(self.rep, self.me ^ partner), device_id_type=MESH,
        )

    def own(self):
        return pltpu.make_async_copy(self.shard, self.full.at[self.me], self.local)

    def start(self, *names):
        for name in names:
            self.copy(name).start()

    def arrived(self, *names):
        for name in names:
            self.copy(name).wait_recv()

    def begin(self):
        self.start("x0", "y0", "c0")
        self.own().start()

    def relay(self):
        self.arrived("x0")
        self.start("xf", "xc")
        self.arrived("y0")
        self.start("yf", "yc")

    def last(self):
        self.arrived("xf")
        self.start("dA")
        self.arrived("yf")
        self.start("dB")

    def complete(self):
        self.own().wait()
        self.arrived("c0", "xc", "yc", "dA", "dB")

    def finish(self):
        for name in ORDER:
            self.copy(name).wait_send()


class Local:
    def __init__(self, whole_ref, full, local):
        self.copy = pltpu.make_async_copy(whole_ref, full, local)

    def begin(self):
        self.copy.start()

    def complete(self):
        self.copy.wait()

    def relay(self):
        pass

    last = finish = relay


def flat(t):
    return t.reshape(t.shape[0] * t.shape[1], t.shape[2])


def kernel_one(
    remote, lengths, x, dy, q_in, o_in, i_in, t_in,
    qkv_out, probs_out, o_out, u_out, y_out, wn_out, a_out, dz_out, dh_out, do_out, gg_out, gains_out, gwo_out, wq_out,
    wq, wo, wi, wt, mixed_all, gwo, gains, send, recv, local, wq_sem,
):
    step = pl.program_id(0)
    tiles = pl.num_programs(0) // 2
    D = x.shape[1]
    refs = ((q_in, wq), (o_in, wo), (i_in, wi), (t_in, wt))
    if remote:
        me, rep = lax.axis_index("fsdp"), lax.axis_index("rep")
        gq, go, gi, gt = (Gather(s, f, send.at[k], recv.at[k], local.at[k], me, rep) for k, (s, f) in enumerate(refs))
    else:
        gq, go, gi, gt = (Local(s, f, local.at[k]) for k, (s, f) in enumerate(refs))
    export = pltpu.make_async_copy(wq, wq_out, wq_sem)

    @pl.when(step == 0)
    def _():
        if remote:
            barrier = pltpu.get_barrier_semaphore()
            for partner in (1, 2, 4):
                pl.semaphore_signal(barrier, inc=1, device_id=(rep, me ^ partner), device_id_type=MESH)
            pl.semaphore_wait(barrier, 3)
        gq.begin()
        gq.relay()
        go.begin()
        gi.begin()
        gq.last()
        gq.complete()
        export.start()
        gains[...] = flat(wq[:, :, 3 * D :]).astype(f32).T[:8]
        gains_out[...] = gains[...]

    @pl.when(step == 1)
    def _():
        go.relay()

    @pl.when(step == 3)
    def _():
        go.last()

    @pl.when(step == 5)
    def _():
        gi.relay()
        gt.begin()

    @pl.when(step == 7)
    def _():
        gi.last()

    @pl.when(step < tiles)
    def _():
        n, _ = moments(x[...].astype(f32))
        u = (n * gains[0:1]).astype(bf)
        u_out[...] = u
        qkv_out[...] = nn(u, flat(wq[:, :, : 3 * D])).astype(bf)
        for rr in range(TILE // SPAN):
            rows = slice(rr * SPAN, (rr + 1) * SPAN)
            mask = permitted(lengths, step * (TILE // SPAN) + rr)
            probs, mixed = attend(lambda c: qkv_out[rows, c : c + 128], mask)
            for p in range(6):
                probs_out[rr, p] = probs[p]
                o_out[rows, p * 128 : (p + 1) * 128] = mixed[p]
        mixed_all[step] = o_out[...]

    @pl.when(step == tiles)
    def _():
        go.complete()
        gi.complete()
        gt.relay()
        gt.last()
        gt.complete()

    @pl.when(step >= tiles)
    def _():
        o = mixed_all[step - tiles]
        h = x[...].astype(f32) + nn(o, flat(wo[...]))
        n, r = moments(h)
        g = gains[1:2]
        wn = (n * g).astype(bf)
        wn_out[...] = wn
        dm = dy[...]
        y = h
        dw = None
        per = FC // wt.shape[1]
        for j in range(wi.shape[2] // FC):
            cols = slice(j * FC, (j + 1) * FC)
            w_in, w_out = flat(wi[:, :, cols]), flat(wt[j * per : (j + 1) * per])
            a, slope = gelu_both(nn(wn, w_in))
            a = a.astype(bf)
            a_out[:, cols] = a
            y = y + nn(a, w_out)
            dz = (nt(dm, w_out) * slope).astype(bf)
            dz_out[:, cols] = dz
            t = nt(dz, w_in)
            dw = t if dw is None else dw + t
        y_out[...] = y.astype(bf)
        dh = dm.astype(f32) + norm_back(dw, n, r, g)
        dh_out[...] = dh
        dt = dh.astype(bf)
        do_out[...] = nt(dt, flat(wo[...])).astype(bf)
        part = jnp.sum((dw * n).reshape(-1, 8, D), axis=0)
        gw = tn(o, dt)

        @pl.when(step == tiles)
        def _():
            gg_out[...] = part
            gwo[...] = gw

        @pl.when(step > tiles)
        def _():
            gg_out[...] += part
            gwo[...] += gw

    @pl.when(step == 2 * tiles - 1)
    def _():
        gwo_out[...] = gwo[...].astype(bf)
        export.wait()
        for g in (gq, go, gi, gt):
            g.finish()


def forward_and_mlp(remote, x, lengths, dy, packed, w_ao, w_in, w_out):
    T, D = x.shape
    tiles = T // TILE
    per = TILE // SPAN
    F = w_in.shape[-1]
    rows = D // 8
    early = lambda *shape: pl.BlockSpec(shape, lambda i: (jnp.minimum(i, tiles - 1),) + (0,) * (len(shape) - 1))
    late = lambda *shape: pl.BlockSpec(shape, lambda i: (jnp.maximum(i - tiles, 0),) + (0,) * (len(shape) - 1))
    both = lambda *shape: pl.BlockSpec(shape, lambda i: (lax.rem(i, tiles),) + (0,) * (len(shape) - 1))
    fixed = lambda *shape: pl.BlockSpec(shape, lambda i: (0,) * len(shape))
    hbm = pl.BlockSpec(memory_space=pl.ANY)
    return pl.pallas_call(
        functools.partial(kernel_one, remote),
        name="forward_and_mlp",
        grid=(2 * tiles,),
        in_specs=[pl.BlockSpec(memory_space=pltpu.SMEM), both(TILE, D), late(TILE, D), hbm, hbm, hbm, hbm],
        out_specs=[
            early(TILE, 3 * D), early(per, 6, SPAN, 2 * SPAN), early(TILE, D), early(TILE, D),
            late(TILE, D), late(TILE, D), late(TILE, F), late(TILE, F), late(TILE, D), late(TILE, D),
            fixed(8, D), fixed(8, D), fixed(D, D), hbm,
        ],
        out_shape=[
            sds(T, 3 * D), sds(T // SPAN, 6, SPAN, 2 * SPAN), sds(T, D), sds(T, D),
            sds(T, D), sds(T, D), sds(T, F), sds(T, F), sds(T, D, dtype=f32), sds(T, D),
            sds(8, D, dtype=f32), sds(8, D, dtype=f32), sds(D, D), sds(8, rows, packed.shape[-1]),
        ],
        scratch_shapes=[
            pltpu.VMEM((8, rows, packed.shape[-1]), bf), pltpu.VMEM((8, rows, D), bf), pltpu.VMEM((8, rows, F), bf),
            pltpu.VMEM((8, F // 8, D), bf), pltpu.VMEM((tiles, TILE, D), bf), pltpu.VMEM((D, D), f32), pltpu.VMEM((8, D), f32),
            pltpu.SemaphoreType.DMA((4, len(ORDER))), pltpu.SemaphoreType.DMA((4, len(ORDER))), pltpu.SemaphoreType.DMA((4,)),
            pltpu.SemaphoreType.DMA,
        ],
        cost_estimate=pl.CostEstimate(flops=12 * T * D * D + 8 * T * D * F + 6 * T * D * D, bytes_accessed=90 << 20, transcendentals=0),
        compiler_params=pltpu.CompilerParams(
            vmem_limit_bytes=VMEM, has_side_effects=remote, collective_id=1 if remote else None
        ),
    )(lengths, x, dy, packed, w_ao, w_in, w_out)


def pack(w_qkv, gain_attn, gain_mlp):
    gains = jnp.stack([gain_attn, gain_mlp], axis=1)
    return jnp.concatenate([w_qkv, jnp.pad(gains, ((0, 0), (0, 126)))], axis=1)


def shards(x, lengths, segments, gain_attn, w_qkv, w_attn_out, gain_mlp, w_mlp_in, w_mlp_out, dy):
    D = x.shape[1]
    remote = lax.axis_size("fsdp") == 8
    weights = (pack(w_qkv, gain_attn, gain_mlp), w_attn_out, w_mlp_in, w_mlp_out)
    if not remote:
        weights = tuple(lax.all_gather(v, "fsdp", axis=0, tiled=True) for v in weights)
        weights = tuple(v.reshape(8, v.shape[0] // 8, v.shape[1]) for v in weights)
    qkv, probs, o, u, y, wn, a, dz, dh, do, gg2, gains, gwo, wq = forward_and_mlp(remote, x, lengths, dy, *weights)
    g1 = gains[0:1]
    wq = wq.reshape(D, wq.shape[2])[:, : 3 * D]
    scatter = lambda v: lax.psum_scatter(v, "fsdp", scatter_dimension=0, tiled=True)
    gwt = scatter(weight_grad(a, dy, "mlp_out_grad", 768, bf, "left"))
    gwi = scatter(weight_grad(wn, dz, "mlp_in_grad", 768))
    gwo = scatter(gwo)
    dqkv = attention_back(qkv, probs, do)
    gq = weight_grad(u, dqkv, "qkv_grad", 768)
    dx, gg1 = input_grad(x, dqkv, dh, g1, wq)
    ends = jnp.stack([gg1.sum(0), gg2.sum(0)], axis=1).astype(bf)
    gq = scatter(jnp.concatenate([gq, jnp.pad(ends, ((0, 0), (0, 126)))], axis=1))
    gwt, gwi, gwo, gq = lax.psum((gwt, gwi, gwo, gq), "rep")
    gwt, gwi, gwo, gq = (v.astype(f32) for v in (gwt, gwi, gwo, gq))
    return y, dx, gq[:, 3 * D], gq[:, : 3 * D], gwo, gq[:, 3 * D + 1], gwi, gwt


def solution(mesh):
    tokens, cut, vec = P(("rep", "fsdp"), None), P("fsdp", None), P("fsdp")
    return jax.shard_map(
        shards,
        mesh=mesh,
        in_specs=(tokens, tokens, P(("rep", "fsdp")), vec, cut, cut, vec, cut, cut, tokens),
        out_specs=(tokens, tokens, vec, cut, cut, vec, cut, cut),
        check_vma=False,
    )
```

```python
import functools, math
import jax, jax.numpy as jnp
from jax import lax
from jax.experimental import pallas as pl
from jax.experimental.pallas import tpu as pltpu
from jax.sharding import PartitionSpec as P
bf = jnp.bfloat16
f32 = jnp.float32
EPS = 1e-05
NEG = -1e30
SPAN = 128
TILE = 256
VMEM = 60 * 1024 * 1024
SCALE = 64 ** -0.5
LOG2E = math.log2(math.e)
GC = math.sqrt(2.0 / math.pi)
GK = 0.044715


def nn(a, b):
    return lax.dot_general(a, b, (((1,), (0,)), ((), ())), preferred_element_type=f32)


def nt(a, b):
    return lax.dot_general(a, b, (((1,), (1,)), ((), ())), preferred_element_type=f32)


def tn(a, b):
    return lax.dot_general(a, b, (((0,), (0,)), ((), ())), preferred_element_type=f32)


def moments(v):
    c = v - jnp.mean(v, axis=-1, keepdims=True)
    r = lax.rsqrt(jnp.mean(c * c, axis=-1, keepdims=True) + EPS)
    return c * r, r


def norm_back(e, n, r, g):
    s = e * g
    inner = s - jnp.mean(s, axis=-1, keepdims=True) - n * jnp.mean(s * n, axis=-1, keepdims=True)
    return inner * r


def split_heads(t):
    low = lax.broadcasted_iota(jnp.int32, t.shape, 1) < 64
    zero = jnp.zeros_like(t)
    return jnp.concatenate([jnp.where(low, t, zero), jnp.where(low, zero, t)], axis=0)


def stack_lanes(t):
    return jnp.concatenate([t[:, :SPAN], t[:, SPAN:]], axis=0)


def permitted(lengths, row):
    ends = []
    total = 0
    for k in range(4):
        total = total + lengths[row, k]
        ends.append(total)
    key = lax.broadcasted_iota(jnp.int32, (SPAN, SPAN), 0)
    query = lax.broadcasted_iota(jnp.int32, (SPAN, SPAN), 1)
    one, zero = jnp.int32(1), jnp.int32(0)
    seg_key = sum(jnp.where(key >= e, one, zero) for e in ends)
    seg_query = sum(jnp.where(query >= e, one, zero) for e in ends)
    return (seg_key == seg_query) & ((key < total) | (key == query))


def attend(qkv, mask):
    mask2 = jnp.concatenate([mask, mask], axis=1)
    probs, mixed = [], []
    for p in range(6):
        q2, k2, v2 = qkv(p * 128), qkv(768 + p * 128), qkv(1536 + p * 128)
        s = jnp.where(mask2, nt(k2, split_heads(q2)), NEG)
        top = jnp.max(s, axis=0, keepdims=True)
        e = jnp.exp2((s - top) * (SCALE * LOG2E))
        w = (e * (1.0 / jnp.sum(e, axis=0, keepdims=True))).astype(bf)
        probs.append(w)
        mixed.append(tn(stack_lanes(w), split_heads(v2)).astype(bf))
    return probs, mixed


def attend_back(qkv, w, do2, p):
    q2, k2, v2 = qkv(p * 128), qkv(768 + p * 128), qkv(1536 + p * 128)
    do_bd = split_heads(do2)
    dv = nn(w, do_bd)
    dp = nt(v2, do_bd)
    pf = w.astype(f32)
    pd = pf * dp
    inner = jnp.sum(pd, axis=0, keepdims=True)
    draw = ((pd - pf * inner) * SCALE).astype(bf)
    dq = tn(stack_lanes(draw), split_heads(k2))
    dk = nn(draw, split_heads(q2))
    return dq.astype(bf), dk.astype(bf), dv.astype(bf)


def gelu_both(t):
    t2 = t * t
    th = jnp.tanh(t * (GC + (GC * GK) * t2))
    half = 0.5 + 0.5 * th
    a = t * half
    slope = half + (0.5 * t) * (1.0 - th * th) * (GC + (3.0 * GC * GK) * t2)
    return a, slope


FC = 768


def kernel_d1(wn, dz, g):
    g[...] = tn(wn[...], dz[...]).astype(g.dtype)


def kernel_e(qkv, probs, do, dqkv):
    for rr in range(TILE // SPAN):
        rows = slice(rr * SPAN, (rr + 1) * SPAN)
        for p in range(6):
            cols = slice(p * 128, (p + 1) * 128)
            dq, dk, dv = attend_back(lambda c: qkv[rows, c : c + 128], probs[rr, p], do[rows, cols], p)
            dqkv[rows, p * 128 : p * 128 + 128] = dq
            dqkv[rows, 768 + p * 128 : 768 + p * 128 + 128] = dk
            dqkv[rows, 1536 + p * 128 : 1536 + p * 128 + 128] = dv


def kernel_f(x, dqkv, dh, gain, w_qkv, dx_out):
    n, r = moments(x[...].astype(f32))
    du = nt(dqkv[...], w_qkv[...])
    dx_out[...] = (dh[...] + norm_back(du, n, r, gain[...])).astype(bf)


def whole(shape):
    return pl.BlockSpec(shape, lambda i: (0,) * len(shape), pipeline_mode=pl.Buffered(1))


def rows_of(cols, tile=TILE):
    return pl.BlockSpec((tile, cols), lambda i: (i, 0))


def call(body, name, grid, in_specs, out_specs, out_shape, flops, nbytes, scratch=()):
    return pl.pallas_call(
        body,
        name=name,
        grid=grid,
        in_specs=in_specs,
        out_specs=out_specs,
        out_shape=out_shape,
        scratch_shapes=scratch,
        cost_estimate=pl.CostEstimate(flops=flops, bytes_accessed=nbytes, transcendentals=0),
        compiler_params=pltpu.CompilerParams(vmem_limit_bytes=VMEM),
    )


def sds(*shape, dtype=bf):
    return jax.ShapeDtypeStruct(shape, dtype)


def weight_grad(left, right, name, tile, out=bf, by="right"):
    T, M = left.shape
    N = right.shape[1]
    if by == "right":
        ins = [whole((T, M)), pl.BlockSpec((T, tile), lambda i: (0, i))]
        outs = pl.BlockSpec((M, tile), lambda i: (0, i))
        grid = (N // tile,)
    else:
        ins = [pl.BlockSpec((T, tile), lambda i: (0, i)), whole((T, N))]
        outs = pl.BlockSpec((tile, N), lambda i: (i, 0))
        grid = (M // tile,)
    return call(kernel_d1, name, grid, ins, outs, sds(M, N, dtype=out), 2 * T * M * N, 2 * (T * M + T * N + M * N))(left, right)


def attention_back(qkv, probs, do):
    T, D = do.shape
    per = TILE // SPAN
    return call(
        kernel_e, "attention_backward", (T // TILE,),
        [rows_of(3 * D), pl.BlockSpec((per, 6, SPAN, 2 * SPAN), lambda i: (i, 0, 0, 0)), rows_of(D)],
        rows_of(3 * D), sds(T, 3 * D), 8 * T * D * D, 30 << 20,
    )(qkv, probs, do)


def input_grad(x, dqkv, dh, g1, w_qkv):
    T, D = x.shape
    return call(
        kernel_f, "input_grad", (T // TILE,),
        [rows_of(D), rows_of(3 * D), rows_of(D), whole((1, D)), whole(w_qkv.shape)],
        rows_of(D), sds(T, D),
        6 * T * D * D, 30 << 20,
    )(x, dqkv, dh, g1, w_qkv)


MESH = pl.DeviceIdType.MESH
MESSAGES = {
    "c0": (1, 0, None), "x0": (2, 0, None), "y0": (4, 0, None),
    "xc": (1, 2, None), "yc": (1, 4, None), "xf": (4, 2, 0), "yf": (2, 4, 1),
    "dA": (1, 6, 0), "dB": (1, 6, 1),
}
ORDER = list(MESSAGES)


def halves(n):
    left = (n // 256) * 128
    return (left, n - left)


class Gather:
    def __init__(self, shard, full, send, recv, local, me, rep):
        self.shard, self.full, self.send, self.recv, self.local, self.me, self.rep = shard, full, send, recv, local, me, rep

    def copy(self, name):
        k = ORDER.index(name)
        partner, whose, part = MESSAGES[name]
        piece = self.me ^ whose
        src, dst = self.full.at[piece], self.full.at[piece]
        if whose == 0:
            src = self.shard
        if part is not None:
            left, right = halves(self.full.shape[2])
            cols = pl.ds(0, left) if part == 0 else pl.ds(left, right)
            src, dst = src.at[:, cols], dst.at[:, cols]
        return pltpu.make_async_remote_copy(
            src_ref=src, dst_ref=dst, send_sem=self.send.at[k], recv_sem=self.recv.at[k],
            device_id=(self.rep, self.me ^ partner), device_id_type=MESH,
        )

    def own(self):
        return pltpu.make_async_copy(self.shard, self.full.at[self.me], self.local)

    def start(self, *names):
        for name in names:
            self.copy(name).start()

    def arrived(self, *names):
        for name in names:
            self.copy(name).wait_recv()

    def begin(self):
        self.start("x0", "y0", "c0")
        self.own().start()

    def relay(self):
        self.arrived("x0")
        self.start("xf", "xc")
        self.arrived("y0")
        self.start("yf", "yc")

    def last(self):
        self.arrived("xf")
        self.start("dA")
        self.arrived("yf")
        self.start("dB")

    def complete(self):
        self.own().wait()
        self.arrived("c0", "xc", "yc", "dA", "dB")

    def finish(self):
        for name in ORDER:
            self.copy(name).wait_send()


class Local:
    def __init__(self, whole_ref, full, local):
        self.copy = pltpu.make_async_copy(whole_ref, full, local)

    def begin(self):
        self.copy.start()

    def complete(self):
        self.copy.wait()

    def relay(self):
        pass

    last = finish = relay


def flat(t):
    return t.reshape(t.shape[0] * t.shape[1], t.shape[2])


def kernel_one(
    remote, lengths, x, dy, q_in, o_in, i_in, t_in,
    qkv_out, probs_out, o_out, u_out, y_out, wn_out, za_out, dh_out, do_out, gains_out, gwo_out, wq_out,
    wq, wo, wi, wt, mixed_all, gwo, gains, send, recv, local, wq_sem,
):
    step = pl.program_id(0)
    tiles = pl.num_programs(0) // 2
    D = x.shape[1]
    refs = ((q_in, wq), (o_in, wo), (i_in, wi), (t_in, wt))
    if remote:
        me, rep = lax.axis_index("fsdp"), lax.axis_index("rep")
        gq, go, gi, gt = (Gather(s, f, send.at[k], recv.at[k], local.at[k], me, rep) for k, (s, f) in enumerate(refs))
    else:
        gq, go, gi, gt = (Local(s, f, local.at[k]) for k, (s, f) in enumerate(refs))
    export = pltpu.make_async_copy(wq, wq_out, wq_sem)

    @pl.when(step == 0)
    def _():
        if remote:
            barrier = pltpu.get_barrier_semaphore()
            for partner in (1, 2, 4):
                pl.semaphore_signal(barrier, inc=1, device_id=(rep, me ^ partner), device_id_type=MESH)
            pl.semaphore_wait(barrier, 3)
        gq.begin()
        gq.relay()
        go.begin()
        gi.begin()
        gq.last()
        gq.complete()
        export.start()
        gains[...] = flat(wq[:, :, 3 * D :]).astype(f32).T[:8]
        gains_out[...] = gains[...]

    @pl.when(step == 1)
    def _():
        go.relay()

    @pl.when(step == 3)
    def _():
        go.last()

    @pl.when(step == 5)
    def _():
        gi.relay()
        gt.begin()

    @pl.when(step == 7)
    def _():
        gi.last()

    @pl.when(step < tiles)
    def _():
        n, _ = moments(x[...].astype(f32))
        u = (n * gains[0:1]).astype(bf)
        u_out[...] = u
        qkv_out[...] = nn(u, flat(wq[:, :, : 3 * D])).astype(bf)
        for rr in range(TILE // SPAN):
            rows = slice(rr * SPAN, (rr + 1) * SPAN)
            mask = permitted(lengths, step * (TILE // SPAN) + rr)
            probs, mixed = attend(lambda c: qkv_out[rows, c : c + 128], mask)
            for p in range(6):
                probs_out[rr, p] = probs[p]
                o_out[rows, p * 128 : (p + 1) * 128] = mixed[p]
        mixed_all[step] = o_out[...]

    @pl.when(step == tiles)
    def _():
        go.complete()
        gi.complete()
        gt.relay()
        gt.last()
        gt.complete()

    @pl.when(step >= tiles)
    def _():
        o = mixed_all[step - tiles]
        h = x[...].astype(f32) + nn(o, flat(wo[...]))
        n, r = moments(h)
        g = gains[1:2]
        wn = (n * g).astype(bf)
        wn_out[...] = wn
        dm = dy[...]
        y = h
        dw = None
        per = FC // wt.shape[1]
        for j in range(wi.shape[2] // FC):
            cols = slice(j * FC, (j + 1) * FC)
            w_in, w_out = flat(wi[:, :, cols]), flat(wt[j * per : (j + 1) * per])
            a, slope = gelu_both(nn(wn, w_in))
            a = a.astype(bf)
            za_out[1, :, cols] = a
            y = y + nn(a, w_out)
            dz = (nt(dm, w_out) * slope).astype(bf)
            za_out[0, :, cols] = dz
            t = nt(dz, w_in)
            dw = t if dw is None else dw + t
        y_out[...] = y.astype(bf)
        dh = dm.astype(f32) + norm_back(dw, n, r, g)
        dh_out[...] = dh
        dt = dh.astype(bf)
        do_out[...] = nt(dt, flat(wo[...])).astype(bf)
        gw = tn(o, dt)

        @pl.when(step == tiles)
        def _():
            gwo[...] = gw

        @pl.when(step > tiles)
        def _():
            gwo[...] += gw

    @pl.when(step == 2 * tiles - 1)
    def _():
        gwo_out[...] = gwo[...].astype(bf)
        export.wait()
        for g in (gq, go, gi, gt):
            g.finish()


def forward_and_mlp(remote, x, lengths, dy, packed, w_ao, w_in, w_out):
    T, D = x.shape
    tiles = T // TILE
    per = TILE // SPAN
    F = w_in.shape[-1]
    rows = D // 8
    early = lambda *shape: pl.BlockSpec(shape, lambda i: (jnp.minimum(i, tiles - 1),) + (0,) * (len(shape) - 1))
    late = lambda *shape: pl.BlockSpec(shape, lambda i: (jnp.maximum(i - tiles, 0),) + (0,) * (len(shape) - 1))
    both = lambda *shape: pl.BlockSpec(shape, lambda i: (lax.rem(i, tiles),) + (0,) * (len(shape) - 1))
    fixed = lambda *shape: pl.BlockSpec(shape, lambda i: (0,) * len(shape))
    hbm = pl.BlockSpec(memory_space=pl.ANY)
    return pl.pallas_call(
        functools.partial(kernel_one, remote),
        name="forward_and_mlp",
        grid=(2 * tiles,),
        in_specs=[pl.BlockSpec(memory_space=pltpu.SMEM), both(TILE, D), late(TILE, D), hbm, hbm, hbm, hbm],
        out_specs=[
            early(TILE, 3 * D), early(per, 6, SPAN, 2 * SPAN), early(TILE, D), early(TILE, D),
            late(TILE, D), late(TILE, D), pl.BlockSpec((2, TILE, F), lambda i: (0, jnp.maximum(i - tiles, 0), 0)),
            late(TILE, D), late(TILE, D), fixed(8, D), fixed(D, D), hbm,
        ],
        out_shape=[
            sds(T, 3 * D), sds(T // SPAN, 6, SPAN, 2 * SPAN), sds(T, D), sds(T, D),
            sds(T, D), sds(T, D), sds(2, T, F), sds(T, D, dtype=f32), sds(T, D), sds(8, D, dtype=f32), sds(D, D), sds(8, rows, packed.shape[-1]),
        ],
        scratch_shapes=[
            pltpu.VMEM((8, rows, packed.shape[-1]), bf), pltpu.VMEM((8, rows, D), bf), pltpu.VMEM((8, rows, F), bf),
            pltpu.VMEM((8, F // 8, D), bf), pltpu.VMEM((tiles, TILE, D), bf), pltpu.VMEM((D, D), f32), pltpu.VMEM((8, D), f32),
            pltpu.SemaphoreType.DMA((4, len(ORDER))), pltpu.SemaphoreType.DMA((4, len(ORDER))), pltpu.SemaphoreType.DMA((4,)),
            pltpu.SemaphoreType.DMA,
        ],
        cost_estimate=pl.CostEstimate(flops=12 * T * D * D + 8 * T * D * F + 6 * T * D * D, bytes_accessed=90 << 20, transcendentals=0),
        compiler_params=pltpu.CompilerParams(
            vmem_limit_bytes=VMEM, has_side_effects=remote, collective_id=1 if remote else None
        ),
    )(lengths, x, dy, packed, w_ao, w_in, w_out)


def pack(w_qkv, gain_attn, gain_mlp):
    gains = jnp.stack([gain_attn, gain_mlp], axis=1)
    return jnp.concatenate([w_qkv, jnp.pad(gains, ((0, 0), (0, 126)))], axis=1)


CHUNK = 96
WIDE = 768
RING = 6
N_CHUNKS = 12
SLAB = 16


def add_rows(pairs):
    for target, other in pairs:
        def slab(k, carry, target=target, other=other):
            rows = pl.ds(pl.multiple_of(k * SLAB, SLAB), SLAB)
            target[rows, :] = (target[rows, :].astype(f32) + other[rows, :].astype(f32)).astype(bf)
            return carry

        lax.fori_loop(0, target.shape[0] // SLAB, slab, 0)


class Reduce:
    def __init__(self, k, grads, bufs, send, recv, place):
        self.k, self.g = k, grads
        self.first, self.x2, self.y2, self.y3, self.x3, self.half, self.quarter, self.out = bufs
        self.send, self.recv = send, recv
        self.y, self.x, self.c, self.me, self.rep = place

    def copy(self, m):
        k, g, y, x, c, rep = self.k, self.g, self.y, self.x, self.c, self.rep
        mid = WIDE // 2
        left, right = pl.ds(0, mid), pl.ds(mid, mid)
        own = g.at[y, x, c]
        low, high = rep % 2, rep // 2
        half = CHUNK // 2
        keep = pl.ds(pl.multiple_of(low * half, half), half)
        give = pl.ds(pl.multiple_of((1 - low) * half, half), half)
        keep_cols = pl.ds(pl.multiple_of(high * mid, mid), mid)
        give_cols = pl.ds(pl.multiple_of((1 - high) * mid, mid), mid)
        src, dst, rep_to, me_to = {
            "s1": lambda: (g.at[:, :, 1 - c], self.first.at[k % RING], 0, 1),
            "s2x": lambda: (g.at[:, 1 - x, c, :, left], self.x2.at[k % RING], 0, 2),
            "s2y": lambda: (g.at[1 - y, :, c, :, right], self.y2.at[k % RING], 0, 4),
            "s3y": lambda: (g.at[1 - y, x, c, :, left], self.y3.at[k], 0, 4),
            "s3x": lambda: (g.at[y, 1 - x, c, :, right], self.x3.at[k], 0, 2),
            "z1": lambda: (own.at[give], self.half.at[k], 1, 0),
            "z2": lambda: (own.at[keep, give_cols], self.quarter.at[k], 2, 0),
            "z3": lambda: (self.out.at[k, keep, keep_cols], self.out.at[k, keep, keep_cols], 2, 0),
            "z4": lambda: (self.out.at[k, keep], self.out.at[k, keep], 1, 0),
        }[m]()
        n = REDUCE.index(m)
        return pltpu.make_async_remote_copy(
            src_ref=src, dst_ref=dst, send_sem=self.send.at[k, n], recv_sem=self.recv.at[k, n],
            device_id=(rep ^ rep_to, self.me ^ me_to), device_id_type=MESH,
        )

    def start(self, *names):
        for m in names:
            self.copy(m).start()

    def arrived(self, *names):
        for m in names:
            self.copy(m).wait_recv()

    def stage(self, n):
        k, g, y, x, c = self.k, self.g, self.y, self.x, self.c
        mid = WIDE // 2
        left, right = pl.ds(0, mid), pl.ds(mid, mid)
        low, high = self.rep % 2, self.rep // 2
        half = CHUNK // 2
        keep = pl.ds(pl.multiple_of(low * half, half), half)
        keep_cols = pl.ds(pl.multiple_of(high * mid, mid), mid)
        if n == 1:
            self.start("s1")
        elif n == 2:
            self.arrived("s1")
            add_rows([(g.at[b, a, c], self.first.at[k % RING, b, a]) for b in range(2) for a in range(2)])
            self.start("s2x", "s2y")
        elif n == 3:
            self.arrived("s2x", "s2y")
            add_rows([(g.at[b, x, c, :, left], self.x2.at[k % RING, b]) for b in range(2)])
            add_rows([(g.at[y, a, c, :, right], self.y2.at[k % RING, a]) for a in range(2)])
            self.start("s3y", "s3x")
        elif n == 4:
            self.arrived("s3y", "s3x")
            add_rows([(g.at[y, x, c, :, left], self.y3.at[k]), (g.at[y, x, c, :, right], self.x3.at[k])])
            self.start("z1")
        elif n == 5:
            self.arrived("z1")
            add_rows([(g.at[y, x, c, keep], self.half.at[k])])
            self.start("z2")
        elif n == 6:
            self.arrived("z2")
            own = g.at[y, x, c, keep, keep_cols]
            self.out[k, keep, keep_cols] = (own[...].astype(f32) + self.quarter[k].astype(f32)).astype(bf)
            self.start("z3")
        elif n == 7:
            self.arrived("z3")
            self.start("z4")
        elif n == 8:
            self.arrived("z4")

    def sent(self):
        for m in REDUCE:
            self.copy(m).wait_send()


REDUCE = ["s1", "s2x", "s2y", "s3y", "s3x", "z1", "z2", "z3", "z4"]
P_IN, P_OUT, P_ATT, P_QKV = 0, 4, 8, 16
P_DX = 19
SLOT = [0, 1, 2, 3, 4, 5, 6, 7, 8, 0, 1, 2]
FIRST = [0, 1, 2, 4, 5, 8, 9, 11, 13, 17, 18, 19]
GAPS = [0, 1, 3, 5, 6, 7, 8, 9]


def schedule():
    acts = {}
    for k in range(N_CHUNKS):
        for n, gap in enumerate(GAPS):
            acts.setdefault(FIRST[k] + gap, []).append((k, n + 1))
    return acts


def kernel_two(
    gwo_in, wn, dm, u, wq, gains, za, qkv, probs, do, x, dh,
    dx_out, out_hbm,
    out, big_a, big_b, wq_s, dqkv, grads, first, x2, y2, y3, x3, half, quarter, send, recv, local,
):
    step = pl.program_id(0)
    T, D = big_a.shape
    steps = P_DX + T // TILE
    me, rep = lax.axis_index("fsdp"), lax.axis_index("rep")
    place = (me // 4, (me // 2) % 2, me % 2, me, rep)
    bufs = (first, x2, y2, y3, x3, half, quarter, out)
    chunks = [Reduce(k, grads.at[SLOT[k]], bufs, send, recv, place) for k in range(N_CHUNKS)]
    load_gwo = pltpu.make_async_copy(gwo_in, grads.at[0], local.at[0])
    load_wn = pltpu.make_async_copy(wn, big_a, local.at[1])
    load_dm = pltpu.make_async_copy(dm, big_b, local.at[2])
    load_u = pltpu.make_async_copy(u, big_a, local.at[3])
    load_wq = pltpu.make_async_copy(wq, wq_s, local.at[4])
    store_out = pltpu.make_async_copy(out, out_hbm, local.at[5])

    @pl.when(step == 0)
    def _():
        load_wn.start()
        load_gwo.start()
        load_dm.start()
        load_wq.start()
        barrier = pltpu.get_barrier_semaphore()
        for to in ((rep, me ^ 1), (rep, me ^ 2), (rep, me ^ 4), (rep ^ 1, me), (rep ^ 2, me)):
            pl.semaphore_signal(barrier, inc=1, device_id=to, device_id_type=MESH)
        pl.semaphore_wait(barrier, 5)
        load_gwo.wait()

    acts = schedule()
    for at in range(steps):
        if at in acts:
            @pl.when(step == at)
            def _(at=at):
                for k, n in sorted(acts[at], key=lambda kn: -kn[1]):
                    chunks[k].stage(n)

    @pl.when(step == 0)
    def _():
        load_wn.wait()

    @pl.when(step < P_OUT)
    def _():
        g = tn(big_a[...], za[0]).astype(bf)
        grads[1 + step] = g.reshape(2, 2, 2, CHUNK, WIDE)

    @pl.when(step == P_OUT)
    def _():
        load_u.start()
        load_dm.wait()

    @pl.when((step >= P_OUT) & (step < P_ATT))
    def _():
        j = step - P_OUT
        g = tn(za[0], big_b[...]).astype(bf).reshape(2, 4, CHUNK, WIDE)
        for part in range(4):
            grads[5 + part, j // 2, j % 2] = g[:, part]

    @pl.when((step >= P_ATT) & (step < P_QKV))
    def _():
        t = step - P_ATT
        for rr in range(TILE // SPAN):
            rows = slice(rr * SPAN, (rr + 1) * SPAN)
            for p in range(6):
                cols = slice(p * 128, (p + 1) * 128)
                back = attend_back(lambda c: qkv[rows, c : c + 128], probs[rr, p], do[rows, cols], p)
                for j in range(3):
                    dqkv[j, t, rows, cols] = back[j]

    @pl.when(step == P_QKV)
    def _():
        load_u.wait()
        load_wq.wait()
        for k in range(3):
            chunks[k].sent()

    @pl.when((step >= P_QKV) & (step < P_DX))
    def _():
        j = step - P_QKV
        g = tn(big_a[...], dqkv[j].reshape(T, D)).astype(bf)
        grads[j] = g.reshape(2, 2, 2, CHUNK, WIDE)

    @pl.when(step >= P_DX)
    def _():
        t = step - P_DX
        n, r = moments(x[...].astype(f32))
        du = nt(jnp.concatenate([dqkv[j, t] for j in range(3)], axis=1), flat(wq_s[:, :, : 3 * D]))
        dx_out[...] = (dh[...] + norm_back(du, n, r, gains[0:1])).astype(bf)

    @pl.when(step == steps - 1)
    def _():
        for at in sorted(acts):
            if at >= steps:
                for k, n in sorted(acts[at], key=lambda kn: -kn[1]):
                    chunks[k].stage(n)
        for k in range(3, N_CHUNKS):
            chunks[k].sent()
        store_out.start()
        store_out.wait()


def gradients(gwo, wn, dy, u, wq, gains, za, qkv, probs, do, x, dh):
    T, D = x.shape
    tiles = T // TILE
    per = TILE // SPAN
    steps = P_DX + tiles
    hbm = pl.BlockSpec(memory_space=pl.ANY)

    def tile_from(start, *shape):
        return pl.BlockSpec(shape, lambda i: (jnp.clip(i - start, 0, tiles - 1),) + (0,) * (len(shape) - 1))

    return pl.pallas_call(
        kernel_two,
        name="gradients",
        grid=(steps,),
        in_specs=[
            hbm, hbm, hbm, hbm, hbm, pl.BlockSpec((8, D), lambda i: (0, 0)),
            pl.BlockSpec((1, T, WIDE), lambda i: (jnp.where(i < P_OUT, 0, 1), 0, jnp.where(i < P_OUT, i, jnp.minimum(i - P_OUT, 3)))),
            tile_from(P_ATT, TILE, 3 * D), tile_from(P_ATT, per, 6, SPAN, 2 * SPAN), tile_from(P_ATT, TILE, D),
            tile_from(P_DX, TILE, D), tile_from(P_DX, TILE, D),
        ],
        out_specs=[tile_from(P_DX, TILE, D), hbm],
        out_shape=[sds(T, D), sds(N_CHUNKS, CHUNK, WIDE)],
        scratch_shapes=[
            pltpu.VMEM((N_CHUNKS, CHUNK, WIDE), bf),
            pltpu.VMEM((T, D), bf), pltpu.VMEM((T, D), bf), pltpu.VMEM(wq.shape, bf), pltpu.VMEM((3, tiles, TILE, D), bf),
            pltpu.VMEM((9, 2, 2, 2, CHUNK, WIDE), bf), pltpu.VMEM((RING, 2, 2, CHUNK, WIDE), bf),
            pltpu.VMEM((RING, 2, CHUNK, WIDE // 2), bf), pltpu.VMEM((RING, 2, CHUNK, WIDE // 2), bf),
            pltpu.VMEM((N_CHUNKS, CHUNK, WIDE // 2), bf), pltpu.VMEM((N_CHUNKS, CHUNK, WIDE // 2), bf),
            pltpu.VMEM((N_CHUNKS, CHUNK // 2, WIDE), bf), pltpu.VMEM((N_CHUNKS, CHUNK // 2, WIDE // 2), bf),
            pltpu.SemaphoreType.DMA((N_CHUNKS, len(REDUCE))), pltpu.SemaphoreType.DMA((N_CHUNKS, len(REDUCE))),
            pltpu.SemaphoreType.DMA((6,)),
        ],
        cost_estimate=pl.CostEstimate(flops=8 * T * D * D + 4 * T * D * 4 * D + 20 * T * D * D, bytes_accessed=90 << 20, transcendentals=0),
        compiler_params=pltpu.CompilerParams(vmem_limit_bytes=VMEM, has_side_effects=True, collective_id=2),
    )(gwo.reshape(2, 2, 2, CHUNK, WIDE), wn, dy, u, wq, gains, za, qkv, probs, do, x, dh)


def shards(x, lengths, segments, gain_attn, w_qkv, w_attn_out, gain_mlp, w_mlp_in, w_mlp_out, dy):
    D = x.shape[1]
    remote = lax.axis_size("fsdp") == 8 and lax.axis_size("rep") == 4
    weights = (pack(w_qkv, gain_attn, gain_mlp), w_attn_out, w_mlp_in, w_mlp_out)
    if not remote:
        weights = tuple(lax.all_gather(v, "fsdp", axis=0, tiled=True) for v in weights)
        weights = tuple(v.reshape(8, v.shape[0] // 8, v.shape[1]) for v in weights)
    qkv, probs, o, u, y, wn, za, dh, do, gains, gwo, wq = forward_and_mlp(remote, x, lengths, dy, *weights)
    if remote:
        dx, sums = gradients(gwo, wn, dy, u, wq, gains, za, qkv, probs, do, x, dh)
        sums = sums.astype(f32)
        wide = lambda v: v.transpose(1, 0, 2).reshape(v.shape[1], -1)
        gwo, gwi, gwt, gq = sums[0], wide(sums[1:5]), sums[5:9].reshape(-1, D), wide(sums[9:12])
    else:
        g1 = gains[0:1]
        scatter = lambda v: lax.psum_scatter(v, "fsdp", scatter_dimension=0, tiled=True)
        gwt = scatter(weight_grad(za[1], dy, "mlp_out_grad", 768, bf, "left"))
        gwi = scatter(weight_grad(wn, za[0], "mlp_in_grad", 768))
        gwo = scatter(gwo)
        dqkv = attention_back(qkv, probs, do)
        gq = scatter(weight_grad(u, dqkv, "qkv_grad", 768))
        dx = input_grad(x, dqkv, dh, g1, wq.reshape(D, wq.shape[2])[:, : 3 * D])
        gwt, gwi, gwo, gq = lax.psum((gwt, gwi, gwo, gq), "rep")
        gwt, gwi, gwo, gq = (v.astype(f32) for v in (gwt, gwi, gwo, gq))
    gg1 = jnp.sum(w_qkv.astype(f32) * gq, axis=1) / gain_attn.astype(f32)
    gg2 = jnp.sum(w_mlp_in.astype(f32) * gwi, axis=1) / gain_mlp.astype(f32)
    return y, dx, gg1, gq, gwo, gg2, gwi, gwt


def solution(mesh):
    tokens, cut, vec = P(("rep", "fsdp"), None), P("fsdp", None), P("fsdp")
    return jax.shard_map(
        shards,
        mesh=mesh,
        in_specs=(tokens, tokens, P(("rep", "fsdp")), vec, cut, cut, vec, cut, cut, tokens),
        out_specs=(tokens, tokens, vec, cut, cut, vec, cut, cut),
        check_vma=False,
    )
```

```python
import functools, math
import jax, jax.numpy as jnp
from jax import lax
from jax.experimental import pallas as pl
from jax.experimental.pallas import tpu as pltpu
from jax.sharding import PartitionSpec as P
bf = jnp.bfloat16
f32 = jnp.float32
EPS = 1e-05
NEG = -1e30
SPAN = 128
TILE = 256
VMEM = 63 * 1024 * 1024
SCALE = 64 ** -0.5
LOG2E = math.log2(math.e)
GC = math.sqrt(2.0 / math.pi)
GK = 0.044715


def nn(a, b):
    return lax.dot_general(a, b, (((1,), (0,)), ((), ())), preferred_element_type=f32)


def nt(a, b):
    return lax.dot_general(a, b, (((1,), (1,)), ((), ())), preferred_element_type=f32)


def tn(a, b):
    return lax.dot_general(a, b, (((0,), (0,)), ((), ())), preferred_element_type=f32)


def moments(v):
    c = v - jnp.mean(v, axis=-1, keepdims=True)
    r = lax.rsqrt(jnp.mean(c * c, axis=-1, keepdims=True) + EPS)
    return c * r, r


def norm_back(e, n, r, g):
    s = e * g
    inner = s - jnp.mean(s, axis=-1, keepdims=True) - n * jnp.mean(s * n, axis=-1, keepdims=True)
    return inner * r


def split_heads(t):
    low = lax.broadcasted_iota(jnp.int32, t.shape, 1) < 64
    zero = jnp.zeros_like(t)
    return jnp.concatenate([jnp.where(low, t, zero), jnp.where(low, zero, t)], axis=0)


def stack_lanes(t):
    return jnp.concatenate([t[:, :SPAN], t[:, SPAN:]], axis=0)


def permitted(lengths, row):
    ends = []
    total = 0
    for k in range(4):
        total = total + lengths[row, k]
        ends.append(total)
    key = lax.broadcasted_iota(jnp.int32, (SPAN, SPAN), 0)
    query = lax.broadcasted_iota(jnp.int32, (SPAN, SPAN), 1)
    one, zero = jnp.int32(1), jnp.int32(0)
    seg_key = sum(jnp.where(key >= e, one, zero) for e in ends)
    seg_query = sum(jnp.where(query >= e, one, zero) for e in ends)
    return (seg_key == seg_query) & ((key < total) | (key == query))


def attend(qkv, mask):
    mask2 = jnp.concatenate([mask, mask], axis=1)
    probs, mixed = [], []
    for p in range(6):
        q2, k2, v2 = qkv(p * 128), qkv(768 + p * 128), qkv(1536 + p * 128)
        s = jnp.where(mask2, nt(k2, split_heads(q2)), NEG)
        top = jnp.max(s, axis=0, keepdims=True)
        e = jnp.exp2((s - top) * (SCALE * LOG2E))
        w = (e * (1.0 / jnp.sum(e, axis=0, keepdims=True))).astype(bf)
        probs.append(w)
        mixed.append(tn(stack_lanes(w), split_heads(v2)).astype(bf))
    return probs, mixed


def attend_back(q2, k2, v2, w, do2):
    do_bd = split_heads(do2)
    dv = nn(w, do_bd)
    dp = nt(v2, do_bd)
    pf = w.astype(f32)
    pd = pf * dp
    inner = jnp.sum(pd, axis=0, keepdims=True)
    draw = ((pd - pf * inner) * SCALE).astype(bf)
    dq = tn(stack_lanes(draw), split_heads(k2))
    dk = nn(draw, split_heads(q2))
    return dq.astype(bf), dk.astype(bf), dv.astype(bf)


def gelu(t):
    return t * (0.5 + 0.5 * jnp.tanh(t * (GC + (GC * GK) * (t * t))))


def gelu_slope(t):
    t2 = t * t
    s = 0.5 + 0.5 * jnp.tanh(t * (GC + (GC * GK) * t2))
    a = t * s
    return s + (a - a * s) * (2.0 * GC + (6.0 * GC * GK) * t2)


FC = 768


def kernel_d1(wn, dz, g):
    g[...] = tn(wn[...], dz[...]).astype(g.dtype)


def kernel_e(qkv, probs, do, dqkv):
    for rr in range(TILE // SPAN):
        rows = slice(rr * SPAN, (rr + 1) * SPAN)
        for p in range(6):
            cols = slice(p * 128, (p + 1) * 128)
            q2, k2, v2 = (qkv[rows, j * 768 + p * 128 : j * 768 + p * 128 + 128] for j in range(3))
            dq, dk, dv = attend_back(q2, k2, v2, probs[rr, p], do[rows, cols])
            dqkv[rows, p * 128 : p * 128 + 128] = dq
            dqkv[rows, 768 + p * 128 : 768 + p * 128 + 128] = dk
            dqkv[rows, 1536 + p * 128 : 1536 + p * 128 + 128] = dv


def kernel_f(x, dqkv, dh, gain, w_qkv, dx_out):
    n, r = moments(x[...].astype(f32))
    du = nt(dqkv[...], w_qkv[...])
    dx_out[...] = (dh[...] + norm_back(du, n, r, gain[...])).astype(bf)


def whole(shape):
    return pl.BlockSpec(shape, lambda i: (0,) * len(shape), pipeline_mode=pl.Buffered(1))


def rows_of(cols, tile=TILE):
    return pl.BlockSpec((tile, cols), lambda i: (i, 0))


def call(body, name, grid, in_specs, out_specs, out_shape, flops, nbytes, scratch=()):
    return pl.pallas_call(
        body,
        name=name,
        grid=grid,
        in_specs=in_specs,
        out_specs=out_specs,
        out_shape=out_shape,
        scratch_shapes=scratch,
        cost_estimate=pl.CostEstimate(flops=flops, bytes_accessed=nbytes, transcendentals=0),
        compiler_params=pltpu.CompilerParams(vmem_limit_bytes=VMEM),
    )


def sds(*shape, dtype=bf):
    return jax.ShapeDtypeStruct(shape, dtype)


def weight_grad(left, right, name, tile, out=bf, by="right"):
    T, M = left.shape
    N = right.shape[1]
    if by == "right":
        ins = [whole((T, M)), pl.BlockSpec((T, tile), lambda i: (0, i))]
        outs = pl.BlockSpec((M, tile), lambda i: (0, i))
        grid = (N // tile,)
    else:
        ins = [pl.BlockSpec((T, tile), lambda i: (0, i)), whole((T, N))]
        outs = pl.BlockSpec((tile, N), lambda i: (i, 0))
        grid = (M // tile,)
    return call(kernel_d1, name, grid, ins, outs, sds(M, N, dtype=out), 2 * T * M * N, 2 * (T * M + T * N + M * N))(left, right)


def attention_back(qkv, probs, do):
    T, D = do.shape
    per = TILE // SPAN
    return call(
        kernel_e, "attention_backward", (T // TILE,),
        [rows_of(3 * D), pl.BlockSpec((per, 6, SPAN, 2 * SPAN), lambda i: (i, 0, 0, 0)), rows_of(D)],
        rows_of(3 * D), sds(T, 3 * D), 8 * T * D * D, 30 << 20,
    )(qkv, probs, do)


def input_grad(x, dqkv, dh, g1, w_qkv):
    T, D = x.shape
    return call(
        kernel_f, "input_grad", (T // TILE,),
        [rows_of(D), rows_of(3 * D), rows_of(D), whole((1, D)), whole(w_qkv.shape)],
        rows_of(D), sds(T, D),
        6 * T * D * D, 30 << 20,
    )(x, dqkv, dh, g1, w_qkv)


MESH = pl.DeviceIdType.MESH
D_MODEL = 768
P_B = 3
EARLY = 6
MESSAGES = {
    "x0s": (0, 2, 0, "mine", None), "y0s": (0, 4, 0, "mine", None), "x0c": (0, 2, 0, "middle", None), "y0c": (0, 4, 0, "middle", None),
    "c0": (0, 1, 0, "all", None),
    "xf": (0, 4, 2, "mine", "x0s"), "xz": (1, 0, 2, "mine", "x0s"), "xcs": (0, 1, 2, "mine", "x0s"),
    "yz": (1, 0, 4, "mine", "y0s"), "ycs": (0, 1, 4, "mine", "y0s"),
    "xcc": (0, 1, 2, "middle", "x0c"), "yf": (0, 2, 4, "middle", "y0c"), "ycc": (0, 1, 4, "middle", "y0c"),
    "dz": (1, 0, 6, "mine", "xf"), "dcs": (0, 1, 6, "mine", "xf"), "dcc": (0, 1, 6, "middle", "yf"),
    "xcm": (0, 1, 2, "other", "xz"), "ycm": (0, 1, 4, "other", "yz"), "dcm": (0, 1, 6, "other", "dz"),
}
ARRIVALS = [None, "x0s", "y0s", "x0c", "y0c", "xf", "yf", "xz", "yz", "dz"]
RELAYS = {
    0: [0, 10, 1, 2, 20, 3, 4, 11, 12, 7, 13, 14, 8, 21, 5, 17, 30, 23, 22, 18, 6, 24, 27, 16, 15, 9, 40, 31, 25, 28, 33, 32],
    1: [19, 26, 34, 37, 41, 42, 29, 50, 60, 43, 44, 38, 35, 70],
    2: [36, 45, 47, 51, 52, 48, 80],
    3: [53, 54, 39, 61, 62, 63, 64, 49, 90],
    4: [46, 72, 57, 71, 74, 58],
    5: [73, 55, 67, 81, 82],
    6: [68, 83, 84, 78, 100, 56, 65],
    7: [77, 66, 92, 59, 110],
    8: [91, 94, 87, 93, 75, 88],
    9: [76, 85, 69, 86, 102],
    10: [98, 101, 104, 97, 103],
    11: [112, 79, 111, 114, 89],
    12: [113, 95, 108, 96, 105, 107, 106],
    13: [115, 118, 116, 117],
    14: [99, 109],
    15: [119],
}


class Gather:
    def __init__(self, shard, piece, send, recv, local, me, rep):
        self.shard, self.piece, self.send, self.recv, self.me, self.rep = shard, piece, send, recv, me, rep
        self.own = pltpu.make_async_copy(shard, piece(me), local)

    def copy(self, name):
        rep_to, me_to, whose, what, _ = MESSAGES[name]
        s = ARRIVALS.index(name) if name in ARRIVALS else 0
        third = D_MODEL // 3
        parity = self.rep % 2
        cols = {
            "all": lambda: pl.ds(0, D_MODEL),
            "mine": lambda: pl.ds(pl.multiple_of(parity * 2 * third, 128), third),
            "middle": lambda: pl.ds(third, third),
            "other": lambda: pl.ds(pl.multiple_of((1 - parity) * 2 * third, 128), third),
        }[what]()
        piece = self.piece(self.me ^ whose)
        src = self.shard if whose == 0 else piece
        return pltpu.make_async_remote_copy(
            src_ref=src.at[:, cols], dst_ref=piece.at[:, cols], send_sem=self.send, recv_sem=self.recv.at[s],
            device_id=(self.rep ^ rep_to, self.me ^ me_to), device_id_type=MESH,
        )

    def relay(self, arrival):
        if arrival is None:
            self.own.start()
        else:
            self.copy(arrival).wait_recv()
        for name, message in MESSAGES.items():
            if message[4] == arrival:
                self.copy(name).start()

    def complete(self):
        self.own.wait()
        four = self.piece(pl.ds(0, 4))
        pltpu.make_async_copy(four, four, self.recv.at[0]).wait()

    def finish(self):
        seven = self.piece(pl.ds(0, 7))
        pltpu.make_async_copy(seven, seven, self.send).wait()


class Local:
    def __init__(self, shard, place, local):
        self.own = pltpu.make_async_copy(shard, place, local)

    def relay(self, arrival):
        if arrival is None:
            self.own.start()

    def complete(self):
        self.own.wait()

    def finish(self):
        pass


def dispatch(step, table):
    keys = sorted(table)
    if len(keys) < 4:
        for k in keys:
            pl.when(step == k)(table[k])
    else:
        middle = keys[len(keys) // 2]
        pl.when(step < middle)(lambda: dispatch(step, {k: table[k] for k in keys if k < middle}))
        pl.when(step >= middle)(lambda: dispatch(step, {k: table[k] for k in keys if k >= middle}))


def flat(t):
    return t.reshape(t.shape[0] * t.shape[1], t.shape[2])


def spread(pieces):
    width = D_MODEL // 8
    lane = lax.broadcasted_iota(jnp.int32, (128, D_MODEL), 0)
    place = lax.broadcasted_iota(jnp.int32, (128, D_MODEL), 1)
    total = jnp.zeros((16, D_MODEL), f32)
    for d in range(8):
        hit = (place == lane + d * width) & (lane < width)
        total = total + nn(pieces[d], jnp.where(hit, 1.0, 0.0).astype(bf))
    return total[:8]


def kernel_one(
    remote, lengths, x, dy, gain_in, q_in, o_in, i_in, t_in,
    qkv_out, probs_out, u_out, y_out, wn_out, za_out, dh_out, do_out, gains_out, gwo_out, wq_out,
    wq, wo, wi, wt, gain_parts, gains, high, low, qa, zs, mixed_all, wn, send, recv, gain_send, gain_recv, local, out_sem, a_sem, dz_sem,
):
    step = pl.program_id(0)
    T, D = high.shape
    tiles = T // TILE
    p_h = P_B + tiles
    p_in, p_back = p_h + 2, p_h + 10
    steps = p_back + tiles
    me, rep = lax.axis_index("fsdp"), lax.axis_index("rep")
    part = lambda j: pl.ds(j * D, D)
    rows_of_part = lambda j: pl.ds(j * 96, 96)
    if remote:
        refs = [(q_in.at[:, part(j)], lambda p, j=j: wq.at[j, p]) for j in range(3)]
        refs += [(o_in, lambda p: wo.at[p])]
        refs += [(i_in.at[:, part(j)], lambda p, j=j: wi.at[j, p]) for j in range(4)]
        refs += [(t_in.at[rows_of_part(j)], lambda p, j=j: wt.at[p, rows_of_part(j)]) for j in range(4)]
        blocks = [Gather(s, f, send.at[k], recv.at[k], local.at[k], me, rep) for k, (s, f) in enumerate(refs)]
    else:
        refs = [(q_in.at[:, :, part(j)], wq.at[j]) for j in range(3)] + [(o_in, wo)]
        refs += [(i_in.at[:, :, part(j)], wi.at[j]) for j in range(4)]
        refs += [(t_in.at[:, rows_of_part(j)], wt.at[:, rows_of_part(j)]) for j in range(4)]
        blocks = [Local(s, f, local.at[k]) for k, (s, f) in enumerate(refs)]

    def gain_copy(d):
        return pltpu.make_async_remote_copy(
            src_ref=gain_in, dst_ref=gain_parts.at[me], send_sem=gain_send.at[d], recv_sem=gain_recv.at[d],
            device_id=(rep, me ^ d), device_id_type=MESH,
        )

    own_gain = pltpu.make_async_copy(gain_in, gain_parts.at[me] if remote else gain_parts, local.at[12])
    load_x = pltpu.make_async_copy(x, high, local.at[13])
    export = pltpu.make_async_copy(wq, wq_out, out_sem.at[0])
    store_u = pltpu.make_async_copy(low, u_out, out_sem.at[1])
    store_wn = pltpu.make_async_copy(wn, wn_out, out_sem.at[2])
    store_gwo = pltpu.make_async_copy(mixed_all.at[pl.ds(0, D)], gwo_out, out_sem.at[3])

    def store_qkv(j):
        cols = pl.ds(pl.multiple_of(j * D, D), D)
        return pltpu.make_async_copy(qa.at[:, cols], qkv_out.at[:, cols], out_sem.at[4 + j])

    def rows_at(t, n):
        return pl.ds(pl.multiple_of(t * n, n), n)

    def store_a(e):
        place = (rows_at(lax.rem(e, 2), T // 2), pl.ds(pl.multiple_of(lax.div(e, 2) * FC, FC), FC))
        return pltpu.make_async_copy(qa.at[place], za_out.at[(1, *place)], a_sem.at[e])

    def store_dz(t):
        return pltpu.make_async_copy(zs.at[rows_at(t, TILE)], za_out.at[0, rows_at(t, TILE)], dz_sem.at[t])

    def relay(code):
        blocks[code // 10].relay(ARRIVALS[code % 10])

    @pl.when(step == 0)
    def _():
        load_x.start()
        if remote:
            barrier = pltpu.get_barrier_semaphore()
            for d in range(1, 8):
                pl.semaphore_signal(barrier, inc=1, device_id=(rep, me ^ d), device_id_type=MESH)
            pl.semaphore_signal(barrier, inc=1, device_id=(rep ^ 1, me), device_id_type=MESH)
            pl.semaphore_wait(barrier, 8)
            for d in range(1, 8):
                gain_copy(d).start()
        own_gain.start()
        for code in RELAYS[0][:EARLY]:
            relay(code)
        own_gain.wait()
        if remote:
            for d in range(1, 8):
                gain_copy(d).wait_recv()
        gains[...] = spread(gain_parts)
        gains_out[...] = gains[...]
        load_x.wait()
        later = RELAYS[0][EARLY:]
        for t in range(max(tiles, len(later))):
            if t < tiles:
                rows = pl.ds(t * TILE, TILE)
                n, _ = moments(high[rows, :].astype(f32))
                low[rows, :] = (n * gains[0:1]).astype(bf)
            if t < len(later):
                relay(later[t])
        store_u.start()
        blocks[0].complete()

    completes = {1: [1], 2: [2], p_h: [3], p_back: [8, 9, 10, 11]}
    completes.update({p_in + 2 * j: [4 + j] for j in range(4)})

    def begin(at):
        for code in RELAYS.get(at, []):
            relay(code)
        for k in completes.get(at, []):
            blocks[k].complete()
        if at == P_B:
            export.start()
        if at == p_h:
            store_u.wait()
        if at == p_in:
            store_wn.start()
            for j in range(3):
                store_qkv(j).wait()

    dispatch(step, {at: functools.partial(begin, at) for at in {*RELAYS, *completes, P_B} - {0}})

    @pl.when(step < P_B)
    def _():
        w = flat(wq[step])
        block = 2 * TILE
        cols = pl.ds(pl.multiple_of(step * D, D), D)
        for t in range(T // block):
            qa[t * block : (t + 1) * block, cols] = nn(low[t * block : (t + 1) * block], w).astype(bf)
        store_qkv(step).start()

    @pl.when((step >= P_B) & (step < p_h))
    def _():
        t = step - P_B
        for rr in range(TILE // SPAN):
            rows = pl.ds(pl.multiple_of(t * TILE + rr * SPAN, SPAN), SPAN)
            mask = permitted(lengths, t * (TILE // SPAN) + rr)
            probs, mixed = attend(lambda c: qa[rows, c : c + 128], mask)
            for p in range(6):
                probs_out[rr, p] = probs[p]
                mixed_all[rows, p * 128 : (p + 1) * 128] = mixed[p]

    @pl.when((step >= p_h) & (step < p_in))
    def _():
        for s in range(tiles // 2):
            rows = rows_at((step - p_h) * (tiles // 2) + s, TILE)
            h = high[rows, :].astype(f32) + nn(mixed_all[rows, :], flat(wo[...]))
            top = h.astype(bf)
            high[rows, :] = top
            low[rows, :] = (h - top.astype(f32)).astype(bf)
            n, _ = moments(h)
            wn[rows, :] = (n * gains[1:2]).astype(bf)

    @pl.when((step >= p_in) & (step < p_back))
    def _():
        e = step - p_in
        j, half = lax.div(e, 2), lax.rem(e, 2)
        cols = pl.ds(pl.multiple_of(j * FC, FC), FC)
        w = flat(wi[j])
        block = 2 * TILE
        for s in range(T // 2 // block):
            rows = rows_at(half * (T // 2 // block) + s, block)
            z = nn(wn[rows, :], w)
            qa[rows, cols] = gelu(z).astype(bf)
            zs[rows, cols] = z.astype(bf)
        store_a(e).start()

    per = FC // wt.shape[1]

    @pl.when(step >= p_back)
    def _():
        t = step - p_back
        rows = rows_at(t, TILE)
        h = high[rows, :].astype(f32) + low[rows, :].astype(f32)
        n, r = moments(h)
        dm = dy[...]
        y = h
        dw = None
        for j in range(wi.shape[0]):
            cols = slice(j * FC, (j + 1) * FC)
            w_out = flat(wt[j * per : (j + 1) * per])
            y = y + nn(qa[rows, cols], w_out)
            dz = (nt(dm, w_out) * gelu_slope(zs[rows, cols].astype(f32))).astype(bf)
            zs[rows, cols] = dz
            add = nt(dz, flat(wi[j]))
            dw = add if dw is None else dw + add
        store_dz(t).start()
        y_out[...] = y.astype(bf)
        dh = dm.astype(f32) + norm_back(dw, n, r, gains[1:2])
        dh_out[...] = dh
        dt = dh.astype(bf)
        high[rows, :] = dt
        do_out[...] = nt(dt, flat(wo[...])).astype(bf)

    @pl.when(step == steps - 1)
    def _():
        gwo = tn(mixed_all[...], high[...]).astype(bf)
        mixed_all[0:D, :] = gwo
        store_gwo.start()
        export.wait()
        store_wn.wait()
        for t in range(tiles):
            store_a(t).wait()
            store_dz(t).wait()
        if remote:
            for d in range(1, 8):
                gain_copy(d).wait_send()
        for b in blocks:
            b.finish()
        store_gwo.wait()


def forward_and_mlp(remote, x, lengths, dy, gain, w_qkv, w_ao, w_in, w_out):
    T, D = x.shape
    tiles = T // TILE
    per = TILE // SPAN
    F = w_in.shape[-1]
    rows = D // 8

    def tile_from(start, *shape):
        return pl.BlockSpec(shape, lambda i: (jnp.clip(i - start, 0, tiles - 1),) + (0,) * (len(shape) - 1))

    p_back = P_B + tiles + 10
    hbm = pl.BlockSpec(memory_space=pl.ANY)

    return pl.pallas_call(
        functools.partial(kernel_one, remote),
        name="forward_and_mlp",
        grid=(p_back + tiles,),
        in_specs=[pl.BlockSpec(memory_space=pltpu.SMEM), hbm, tile_from(p_back, TILE, D), hbm, hbm, hbm, hbm, hbm],
        out_specs=[
            hbm, tile_from(P_B, per, 6, SPAN, 2 * SPAN), hbm, tile_from(p_back, TILE, D), hbm, hbm,
            tile_from(p_back, TILE, D), tile_from(p_back, TILE, D), pl.BlockSpec((8, D), lambda i: (0, 0)), hbm, hbm,
        ],
        out_shape=[
            sds(T, 3 * D), sds(T // SPAN, 6, SPAN, 2 * SPAN), sds(T, D),
            sds(T, D), sds(T, D), sds(2, T, F), sds(T, D, dtype=f32), sds(T, D), sds(8, D, dtype=f32), sds(D, D), sds(3, 8, rows, D),
        ],
        scratch_shapes=[
            pltpu.VMEM((3, 8, rows, D), bf), pltpu.VMEM((8, rows, D), bf), pltpu.VMEM((F // FC, 8, rows, FC), bf),
            pltpu.VMEM((8, F // 8, D), bf), pltpu.VMEM((8, 16, 128), bf), pltpu.VMEM((8, D), f32), pltpu.VMEM((T, D), bf),
            pltpu.VMEM((T, D), bf), pltpu.VMEM((T, F), bf), pltpu.VMEM((T, F), bf), pltpu.VMEM((T, D), bf), pltpu.VMEM((T, D), bf),
            pltpu.SemaphoreType.DMA((12,)), pltpu.SemaphoreType.DMA((12, len(ARRIVALS))), pltpu.SemaphoreType.DMA((8,)), pltpu.SemaphoreType.DMA((8,)),
            pltpu.SemaphoreType.DMA((14,)), pltpu.SemaphoreType.DMA((7,)), pltpu.SemaphoreType.DMA((tiles,)), pltpu.SemaphoreType.DMA((tiles,)),
        ],
        cost_estimate=pl.CostEstimate(flops=12 * T * D * D + 8 * T * D * F + 6 * T * D * D, bytes_accessed=90 << 20, transcendentals=0),
        compiler_params=pltpu.CompilerParams(
            vmem_limit_bytes=VMEM, has_side_effects=remote, collective_id=1 if remote else None
        ),
    )(lengths, x, dy, gain, w_qkv, w_ao, w_in, w_out)


def gain_piece(gain_attn, gain_mlp):
    pair = jnp.stack([gain_attn, gain_mlp])
    return jnp.pad(pair, ((0, 14), (0, 128 - pair.shape[1])))


CHUNK = 96
WIDE = 768
RING = 6
N_WIDE = 12
P_IN, P_OUT, P_ATT = 0, 4, 8
P_DX = P_ATT + 18
REUSE = {P_ATT + 8: 0, P_ATT + 14: 1}
START = [
    [0, 1, 3, 6, 9, 12, 21], [2, 3, 7, 10, 14, 17, 21], [5, 6, 8, 12, 16, 19, 36], [3, 5, 8, 11, 18, 20, 28],
    [4, 6, 10, 13, 19, 22, 26], [10, 12, 15, 17, 20, 23, 41], [8, 10, 13, 16, 21, 25, 28], [11, 15, 18, 21, 23, 27, 40],
    [14, 19, 22, 24, 26, 29, 35], [11, 14, 17, 19, 22, 26, 29], [14, 16, 19, 22, 25, 27, 34], [17, 21, 24, 25, 28, 30, 42],
    [21, 22, 25, 27, 29, 31, 38], [24, 25, 27, 29, 31, 33, 40], [26, 27, 29, 30, 32, 38, 39],
]
RECEIVE = {"s1": 0, "s2x": 1, "s2y": 1, "s3y": 2, "s3x": 2, "z1": 3, "z2": 4, "z3": 3}


def slot_of(k):
    return k if k < 10 else k - 10


class Reduce:
    def __init__(self, n, grads, bufs, send, recv, place):
        self.n = n
        k = self.k = n if n < 9 else 9 + (n - 9) // 2
        self.cols = cols = pl.ds(0, WIDE) if n < 9 else pl.ds((n - 9) % 2 * (WIDE // 2), WIDE // 2)
        first, x2, y2, y3, x3, outer, inner, out = bufs
        r = k % RING
        self.g = grads.at[slot_of(k), :, :, :, :, cols]
        self.first = first.at[r, :, :, :, cols]
        self.x2, self.y2 = x2.at[r, :, :, cols], y2.at[r, :, :, cols]
        self.x3, self.y3 = x3.at[k, :, cols], y3.at[k, :, cols]
        self.outer, self.inner, self.out = outer.at[k, :, cols], inner.at[k, :, cols], out.at[k, :, cols]
        self.send, self.recv = send, recv
        self.y, self.x, self.c, self.me, self.rep = place
        self.is_inner = (self.rep == 1) | (self.rep == 2)

    def copy(self, m):
        g, y, x, c = self.g, self.y, self.x, self.c
        upper, lower = pl.ds(0, CHUNK // 2), pl.ds(CHUNK // 2, CHUNK // 2)
        src, dst, rep_to, me_to = {
            "s1": lambda: (g.at[:, :, 1 - c], self.first, 0, 1),
            "s2x": lambda: (g.at[:, 1 - x, c, upper], self.x2, 0, 2),
            "s2y": lambda: (g.at[1 - y, :, c, lower], self.y2, 0, 4),
            "s3y": lambda: (g.at[1 - y, x, c, upper], self.y3, 0, 4),
            "s3x": lambda: (g.at[y, 1 - x, c, lower], self.x3, 0, 2),
            "z1": lambda: (g.at[y, x, c], self.outer, 1, 0),
            "z2": lambda: (g.at[y, x, c], self.inner, 3, 0),
            "z3": lambda: (self.out, self.out, 1, 0),
        }[m]()
        return pltpu.make_async_remote_copy(
            src_ref=src, dst_ref=dst, send_sem=self.send.at[self.n, int(m == "z3")], recv_sem=self.recv.at[self.n, RECEIVE[m]],
            device_id=(self.rep ^ rep_to, self.me ^ me_to), device_id_type=MESH,
        )

    def start(self, *names):
        for m in names:
            self.copy(m).start()

    def arrived(self, m, ref):
        pltpu.make_async_copy(ref, ref, self.recv.at[self.n, RECEIVE[m]]).wait()

    def stage(self, s):
        g, y, x, c = self.g, self.y, self.x, self.c
        upper, lower = pl.ds(0, CHUNK // 2), pl.ds(CHUNK // 2, CHUNK // 2)
        if s == 1:
            self.start("s1")
        elif s == 2:
            self.arrived("s1", self.first)
            for b in range(2):
                for a in range(2):
                    g[b, a, c] += self.first[b, a]
            self.start("s2x", "s2y")
        elif s == 3:
            self.arrived("s2x", g.at[0, 0])
            for b in range(2):
                g[b, x, c, upper] += self.x2[b]
                g[y, b, c, lower] += self.y2[b]
            self.start("s3y", "s3x")
        elif s == 4:
            self.arrived("s3y", g.at[0, 0, 0])
            g[y, x, c, upper] += self.y3[...]
            g[y, x, c, lower] += self.x3[...]

            @pl.when(jnp.logical_not(self.is_inner))
            def _():
                self.start("z1")
        elif s == 5:
            @pl.when(self.is_inner)
            def _():
                self.arrived("z1", self.outer)
                g[y, x, c] += self.outer[...]
                self.start("z2")
        elif s == 6:
            @pl.when(self.is_inner)
            def _():
                self.arrived("z2", self.inner)
                self.out[...] = g[y, x, c] + self.inner[...]
                self.start("z3")
        elif s == 7:
            @pl.when(jnp.logical_not(self.is_inner))
            def _():
                self.arrived("z3", self.out)

    def sent(self):
        pltpu.make_async_copy(self.g, self.g, self.send.at[self.n, 0]).wait()

    def sum_sent(self):
        @pl.when(self.is_inner)
        def _():
            pltpu.make_async_copy(self.out, self.out, self.send.at[self.n, 1]).wait()


def part_of(e):
    return lax.div(e, 3), jnp.minimum(lax.rem(e, 3), 1), lax.rem(e, 3) == 2


def kernel_two(
    gwo_in, wn, dm, u, wq, gains, za, qs, ks, vs, probs, do, x, dh,
    dx_out, out_hbm,
    out, big_a, big_b, wq_s, dqkv, grads, first, x2, y2, y3, x3, outer, inner, send, recv, local,
):
    step = pl.program_id(0)
    T, D = big_a.shape
    steps = P_DX + T // TILE
    me, rep = lax.axis_index("fsdp"), lax.axis_index("rep")
    place = (me // 4, (me // 2) % 2, me % 2, me, rep)
    bufs = (first, x2, y2, y3, x3, outer, inner, out)
    chunks = [Reduce(n, grads, bufs, send, recv, place) for n in range(len(START))]
    load_gwo = pltpu.make_async_copy(gwo_in, grads.at[0], local.at[0])
    load_wn = pltpu.make_async_copy(wn, big_a, local.at[1])
    load_dm = pltpu.make_async_copy(dm, big_b, local.at[2])
    load_u = pltpu.make_async_copy(u, big_a, local.at[3])
    load_wq = pltpu.make_async_copy(wq, wq_s, local.at[4])
    store_out = pltpu.make_async_copy(out, out_hbm, local.at[5])

    @pl.when(step == 0)
    def _():
        load_wn.start()
        load_gwo.start()
        barrier = pltpu.get_barrier_semaphore()
        for to in ((rep, me ^ 1), (rep, me ^ 2), (rep, me ^ 4), (rep ^ 1, me), (rep ^ 3, me)):
            pl.semaphore_signal(barrier, inc=1, device_id=to, device_id_type=MESH)
        pl.semaphore_wait(barrier, 5)
        load_gwo.wait()

    acts = {}
    for n, starts in enumerate(START):
        for s, at in enumerate(starts):
            acts.setdefault(at, []).append((n, s + 1))

    def act(at):
        for n, s in sorted(acts[at], key=lambda ns: -ns[1]):
            chunks[n].stage(s)

    def begin(at):
        if at in acts:
            act(at)
        if at == 0:
            load_wn.wait()
        if at == 1:
            load_dm.start()
        if at == P_OUT:
            load_u.start()
            load_dm.wait()
        if at == P_OUT + 1:
            load_wq.start()
        if at == P_ATT + 2:
            load_u.wait()
            load_wq.wait()
        if at in REUSE:
            chunks[REUSE[at]].sent()

    dispatch(step, {at: functools.partial(begin, at) for at in {*acts, *REUSE, 0, 1, P_OUT, P_OUT + 1, P_ATT + 2} if at < steps})

    @pl.when(step < P_OUT)
    def _():
        g = tn(big_a[...], za[0]).astype(bf)
        grads[1 + step] = g.reshape(2, 2, 2, CHUNK, WIDE)

    @pl.when((step >= P_OUT) & (step < P_ATT))
    def _():
        j = step - P_OUT
        g = tn(za[0], big_b[...]).astype(bf).reshape(2, 4, CHUNK, WIDE)
        for part in range(4):
            grads[5 + part, j // 2, j % 2] = g[:, part]

    pair, half, product = part_of(step - P_ATT)
    attention = (step >= P_ATT) & (step < P_DX)

    @pl.when(attention & jnp.logical_not(product))
    def _():
        for rr in range(probs.shape[0]):
            rows = slice(rr * SPAN, (rr + 1) * SPAN)
            to = pl.ds(pl.multiple_of((half * probs.shape[0] + rr) * SPAN, SPAN), SPAN)
            back = attend_back(qs[rows], ks[rows], vs[rows], probs[rr, 0], do[rows])
            for j in range(3):
                dqkv[pair, to, j * 128 : (j + 1) * 128] = back[j]

    @pl.when(attention & product)
    def _():
        k = pair // 2
        g = tn(big_a[...], dqkv[pair]).astype(bf)
        cols = pl.ds(pl.multiple_of(lax.rem(pair, 2) * (WIDE // 2), WIDE // 2), WIDE // 2)
        grads[jnp.where(k == 0, 9, k - 1), :, :, :, :, cols] = g.reshape(2, 2, 2, CHUNK, WIDE // 2)

    @pl.when(step >= P_DX)
    def _():
        rows = pl.ds(pl.multiple_of((step - P_DX) * TILE, TILE), TILE)
        n, r = moments(x[...].astype(f32))
        d = jnp.concatenate([dqkv[p, rows, j * 128 : (j + 1) * 128] for j in range(3) for p in range(D // 128)], axis=1)
        du = sum(nt(d[:, j * D : (j + 1) * D], flat(wq_s[j])) for j in range(3))
        dx_out[...] = (dh[...] + norm_back(du, n, r, gains[0:1])).astype(bf)

    @pl.when(step == steps - 1)
    def _():
        for at in sorted(acts):
            if at >= steps:
                act(at)
        store_out.start()
        for n in range(len(START)):
            if n not in REUSE.values():
                chunks[n].sent()
            chunks[n].sum_sent()
        store_out.wait()


def gradients(gwo, wn, dy, u, wq, gains, za, qkv, probs, do, x, dh):
    T, D = x.shape
    tiles = T // TILE
    steps = P_DX + tiles
    pairs = D // 128
    hbm = pl.BlockSpec(memory_space=pl.ANY)

    def tile_from(start, *shape):
        return pl.BlockSpec(shape, lambda i: (jnp.clip(i - start, 0, tiles - 1),) + (0,) * (len(shape) - 1))

    def part(i):
        return part_of(jnp.clip(i - P_ATT, 0, 3 * pairs - 1))[:2]

    def head_cols(which):
        def index(i):
            pair, half = part(i)
            return half, which * pairs + pair

        return pl.BlockSpec((T // 2, 128), index)

    def probs_index(i):
        pair, half = part(i)
        return half, pair, 0, 0

    wide = lambda *shape: pltpu.VMEM(shape + (WIDE,), bf)
    return pl.pallas_call(
        kernel_two,
        name="gradients",
        grid=(steps,),
        in_specs=[
            hbm, hbm, hbm, hbm, hbm, pl.BlockSpec((8, D), lambda i: (0, 0)),
            pl.BlockSpec((1, T, WIDE), lambda i: (jnp.where(i < P_OUT, 0, 1), 0, jnp.where(i < P_OUT, i, jnp.minimum(i - P_OUT, 3)))),
            head_cols(0), head_cols(1), head_cols(2), pl.BlockSpec((T // SPAN // 2, 1, SPAN, 2 * SPAN), probs_index), head_cols(0),
            tile_from(P_DX, TILE, D), tile_from(P_DX, TILE, D),
        ],
        out_specs=[tile_from(P_DX, TILE, D), hbm],
        out_shape=[sds(T, D), sds(N_WIDE, CHUNK, WIDE)],
        scratch_shapes=[
            wide(N_WIDE, CHUNK), pltpu.VMEM((T, D), bf), pltpu.VMEM((T, D), bf), pltpu.VMEM(wq.shape, bf),
            pltpu.VMEM((pairs, T, 3 * 128), bf), wide(10, 2, 2, 2, CHUNK), wide(RING, 2, 2, CHUNK), wide(RING, 2, CHUNK // 2),
            wide(RING, 2, CHUNK // 2), wide(N_WIDE, CHUNK // 2), wide(N_WIDE, CHUNK // 2), wide(N_WIDE, CHUNK), wide(N_WIDE, CHUNK),
            pltpu.SemaphoreType.DMA((len(START), 2)), pltpu.SemaphoreType.DMA((len(START), 5)),
            pltpu.SemaphoreType.DMA((6,)),
        ],
        cost_estimate=pl.CostEstimate(flops=8 * T * D * D + 4 * T * D * 4 * D + 20 * T * D * D, bytes_accessed=90 << 20, transcendentals=0),
        compiler_params=pltpu.CompilerParams(vmem_limit_bytes=VMEM, has_side_effects=True, collective_id=2),
    )(gwo.reshape(2, 2, 2, CHUNK, WIDE), wn, dy, u, wq, gains, za, qkv, qkv, qkv, probs, do, x, dh)


def shards(x, lengths, segments, gain_attn, w_qkv, w_attn_out, gain_mlp, w_mlp_in, w_mlp_out, dy):
    D = x.shape[1]
    remote = lax.axis_size("fsdp") == 8 and lax.axis_size("rep") == 4
    gain = gain_piece(gain_attn, gain_mlp)
    weights = (w_qkv, w_attn_out, w_mlp_in, w_mlp_out)
    if not remote:
        weights = tuple(lax.all_gather(v, "fsdp", axis=0, tiled=True) for v in weights)
        weights = tuple(v.reshape(8, v.shape[0] // 8, v.shape[1]) for v in weights)
        gains = [lax.all_gather(v, "fsdp", axis=0, tiled=True).reshape(8, -1) for v in (gain_attn, gain_mlp)]
        gain = jnp.stack([gain_piece(a, b) for a, b in zip(*gains)])
    qkv, probs, u, y, wn, za, dh, do, gains, gwo, wq = forward_and_mlp(remote, x, lengths, dy, gain, *weights)
    if remote:
        dx, sums = gradients(gwo, wn, dy, u, wq, gains, za, qkv, probs, do, x, dh)
        sums = sums.astype(f32)
        wide = lambda v: v.transpose(1, 0, 2).reshape(v.shape[1], -1)
        gq = sums[9:12].reshape(3, CHUNK, 2, 3, 128).transpose(1, 3, 0, 2, 4).reshape(CHUNK, 3 * D)
        gwo, gwi, gwt = sums[0], wide(sums[1:5]), sums[5:9].reshape(-1, D)
    else:
        scatter = lambda v: lax.psum_scatter(v, "fsdp", scatter_dimension=0, tiled=True)
        gwt = scatter(weight_grad(za[1], dy, "mlp_out_grad", 768, bf, "left"))
        gwi = scatter(weight_grad(wn, za[0], "mlp_in_grad", 768))
        gwo = scatter(gwo)
        dqkv = attention_back(qkv, probs, do)
        gq = scatter(weight_grad(u, dqkv, "qkv_grad", 768))
        dx = input_grad(x, dqkv, dh, gains[0:1], wq.transpose(1, 2, 0, 3).reshape(D, 3 * D))
        gwt, gwi, gwo, gq = lax.psum((gwt, gwi, gwo, gq), "rep")
        gwt, gwi, gwo, gq = (v.astype(f32) for v in (gwt, gwi, gwo, gq))
    gg1 = jnp.sum(w_qkv.astype(f32) * gq, axis=1) / gain_attn.astype(f32)
    gg2 = jnp.sum(w_mlp_in.astype(f32) * gwi, axis=1) / gain_mlp.astype(f32)
    return y, dx, gg1, gq, gwo, gg2, gwi, gwt


def solution(mesh):
    tokens, cut, vec = P(("rep", "fsdp"), None), P("fsdp", None), P("fsdp")
    return jax.shard_map(
        shards,
        mesh=mesh,
        in_specs=(tokens, tokens, P(("rep", "fsdp")), vec, cut, cut, vec, cut, cut, tokens),
        out_specs=(tokens, tokens, vec, cut, cut, vec, cut, cut),
        check_vma=False,
    )
```

```python
import functools, math
import jax, jax.numpy as jnp
from jax import lax
from jax.experimental import pallas as pl
from jax.experimental.pallas import tpu as pltpu
from jax.sharding import PartitionSpec as P
bf = jnp.bfloat16
f32 = jnp.float32
EPS = 1e-05
NEG = -1e30
SPAN = 128
TILE = 256
VMEM = 63 * 1024 * 1024
SCALE = 64 ** -0.5
LOG2E = math.log2(math.e)
GC = math.sqrt(2.0 / math.pi)
GK = 0.044715


def nn(a, b):
    return lax.dot_general(a, b, (((1,), (0,)), ((), ())), preferred_element_type=f32)


def nt(a, b):
    return lax.dot_general(a, b, (((1,), (1,)), ((), ())), preferred_element_type=f32)


def tn(a, b):
    return lax.dot_general(a, b, (((0,), (0,)), ((), ())), preferred_element_type=f32)


def moments(v):
    c = v - jnp.mean(v, axis=-1, keepdims=True)
    r = lax.rsqrt(jnp.mean(c * c, axis=-1, keepdims=True) + EPS)
    return c * r, r


def norm_back(e, n, r, g):
    s = e * g
    inner = s - jnp.mean(s, axis=-1, keepdims=True) - n * jnp.mean(s * n, axis=-1, keepdims=True)
    return inner * r


def split_heads(t):
    low = lax.broadcasted_iota(jnp.int32, t.shape, 1) < 64
    zero = jnp.zeros_like(t)
    return jnp.concatenate([jnp.where(low, t, zero), jnp.where(low, zero, t)], axis=0)


def stack_lanes(t):
    return jnp.concatenate([t[:, :SPAN], t[:, SPAN:]], axis=0)


def permitted(lengths, row):
    ends = []
    total = 0
    for k in range(4):
        total = total + lengths[k, row]
        ends.append(total)
    key = lax.broadcasted_iota(jnp.int32, (SPAN, SPAN), 0)
    query = lax.broadcasted_iota(jnp.int32, (SPAN, SPAN), 1)
    one, zero = jnp.int32(1), jnp.int32(0)
    seg_key = sum(jnp.where(key >= e, one, zero) for e in ends)
    seg_query = sum(jnp.where(query >= e, one, zero) for e in ends)
    return (seg_key == seg_query) & ((key < total) | (key == query))


def attend(qkv, mask):
    mask2 = jnp.concatenate([mask, mask], axis=1)
    probs, mixed = [], []
    for p in range(6):
        q2, k2, v2 = qkv(p * 128), qkv(768 + p * 128), qkv(1536 + p * 128)
        s = jnp.where(mask2, nt(k2, split_heads(q2)), NEG)
        top = jnp.max(s, axis=0, keepdims=True)
        e = jnp.exp2((s - top) * (SCALE * LOG2E))
        w = (e * (1.0 / jnp.sum(e, axis=0, keepdims=True))).astype(bf)
        probs.append(w)
        mixed.append(tn(stack_lanes(w), split_heads(v2)).astype(bf))
    return probs, mixed


def attend_back(q2, k2, v2, w, do2):
    do_bd = split_heads(do2)
    dv = nn(w, do_bd)
    dp = nt(v2, do_bd)
    pf = w.astype(f32)
    pd = pf * dp
    inner = jnp.sum(pd, axis=0, keepdims=True)
    draw = ((pd - pf * inner) * SCALE).astype(bf)
    dq = tn(stack_lanes(draw), split_heads(k2))
    dk = nn(draw, split_heads(q2))
    return dq.astype(bf), dk.astype(bf), dv.astype(bf)


def gelu(t):
    return t * (0.5 + 0.5 * jnp.tanh(t * (GC + (GC * GK) * (t * t))))


def gelu_slope(t):
    t2 = t * t
    s = 0.5 + 0.5 * jnp.tanh(t * (GC + (GC * GK) * t2))
    a = t * s
    return s + (a - a * s) * (2.0 * GC + (6.0 * GC * GK) * t2)


FC = 768


def kernel_d1(wn, dz, g):
    g[...] = tn(wn[...], dz[...]).astype(g.dtype)


def kernel_e(qkv, probs, do, dqkv):
    for rr in range(TILE // SPAN):
        rows = slice(rr * SPAN, (rr + 1) * SPAN)
        for p in range(6):
            cols = slice(p * 128, (p + 1) * 128)
            q2, k2, v2 = (qkv[rows, j * 768 + p * 128 : j * 768 + p * 128 + 128] for j in range(3))
            dq, dk, dv = attend_back(q2, k2, v2, probs[rows, p * 2 * SPAN : (p + 1) * 2 * SPAN], do[rows, cols])
            dqkv[rows, p * 128 : p * 128 + 128] = dq
            dqkv[rows, 768 + p * 128 : 768 + p * 128 + 128] = dk
            dqkv[rows, 1536 + p * 128 : 1536 + p * 128 + 128] = dv


def kernel_f(x, dqkv, dh, gain, w_qkv, dx_out):
    n, r = moments(x[...].astype(f32))
    du = nt(dqkv[...], w_qkv[...])
    dx_out[...] = (dh[...] + norm_back(du, n, r, gain[...])).astype(bf)


def whole(shape):
    return pl.BlockSpec(shape, lambda i: (0,) * len(shape), pipeline_mode=pl.Buffered(1))


def rows_of(cols, tile=TILE):
    return pl.BlockSpec((tile, cols), lambda i: (i, 0))


def call(body, name, grid, in_specs, out_specs, out_shape, flops, nbytes, scratch=()):
    return pl.pallas_call(
        body,
        name=name,
        grid=grid,
        in_specs=in_specs,
        out_specs=out_specs,
        out_shape=out_shape,
        scratch_shapes=scratch,
        cost_estimate=pl.CostEstimate(flops=flops, bytes_accessed=nbytes, transcendentals=0),
        compiler_params=pltpu.CompilerParams(vmem_limit_bytes=VMEM),
    )


def sds(*shape, dtype=bf):
    return jax.ShapeDtypeStruct(shape, dtype)


def weight_grad(left, right, name, tile, out=bf, by="right"):
    T, M = left.shape
    N = right.shape[1]
    if by == "right":
        ins = [whole((T, M)), pl.BlockSpec((T, tile), lambda i: (0, i))]
        outs = pl.BlockSpec((M, tile), lambda i: (0, i))
        grid = (N // tile,)
    else:
        ins = [pl.BlockSpec((T, tile), lambda i: (0, i)), whole((T, N))]
        outs = pl.BlockSpec((tile, N), lambda i: (i, 0))
        grid = (M // tile,)
    return call(kernel_d1, name, grid, ins, outs, sds(M, N, dtype=out), 2 * T * M * N, 2 * (T * M + T * N + M * N))(left, right)


def attention_back(qkv, probs, do):
    T, D = do.shape
    return call(
        kernel_e, "attention_backward", (T // TILE,),
        [rows_of(3 * D), rows_of(2 * D), rows_of(D)],
        rows_of(3 * D), sds(T, 3 * D), 8 * T * D * D, 30 << 20,
    )(qkv, probs, do)


def input_grad(x, dqkv, dh, g1, w_qkv):
    T, D = x.shape
    return call(
        kernel_f, "input_grad", (T // TILE,),
        [rows_of(D), rows_of(3 * D), rows_of(D), whole((1, D)), whole(w_qkv.shape)],
        rows_of(D), sds(T, D),
        6 * T * D * D, 30 << 20,
    )(x, dqkv, dh, g1, w_qkv)


MESH = pl.DeviceIdType.MESH
D_MODEL = 768
P_B = 3
EARLY = 6
MESSAGES = {
    "x0s": (0, 2, 0, "mine", None), "y0s": (0, 4, 0, "mine", None), "x0c": (0, 2, 0, "middle", None), "y0c": (0, 4, 0, "middle", None),
    "c0": (0, 1, 0, "all", None),
    "xf": (0, 4, 2, "mine", "x0s"), "xz": (1, 0, 2, "mine", "x0s"), "xcs": (0, 1, 2, "mine", "x0s"),
    "yz": (1, 0, 4, "mine", "y0s"), "ycs": (0, 1, 4, "mine", "y0s"),
    "xcc": (0, 1, 2, "middle", "x0c"), "yf": (0, 2, 4, "middle", "y0c"), "ycc": (0, 1, 4, "middle", "y0c"),
    "dz": (1, 0, 6, "mine", "xf"), "dcs": (0, 1, 6, "mine", "xf"), "dcc": (0, 1, 6, "middle", "yf"),
    "xcm": (0, 1, 2, "other", "xz"), "ycm": (0, 1, 4, "other", "yz"), "dcm": (0, 1, 6, "other", "dz"),
}
ARRIVALS = [None, "x0s", "y0s", "x0c", "y0c", "xf", "yf", "xz", "yz", "dz"]
RELAYS = {
    0: [0, 10, 1, 2, 20, 3, 4, 11, 12, 7, 13, 14, 8, 21, 5, 17, 30, 23, 22, 18, 6, 24, 27, 16, 15, 9, 40, 31, 25, 28, 33, 32],
    1: [19, 26, 34, 37, 41, 42, 29, 50, 60, 43, 44, 38, 35, 70],
    2: [36, 45, 47, 51, 52, 48, 80],
    3: [53, 54, 39, 61, 62, 63, 64, 49, 90],
    4: [46, 72, 57, 71, 74, 58],
    5: [73, 55, 67, 81, 82],
    6: [68, 83, 84, 78, 100, 56, 65],
    7: [77, 66, 92, 59, 110],
    8: [91, 94, 87, 93, 75, 88],
    9: [76, 85, 69, 86, 102],
    10: [98, 101, 104, 97, 103],
    11: [112, 79, 111, 114, 89],
    12: [113, 95, 108, 96, 105, 107, 106],
    13: [115, 118, 116, 117],
    14: [99, 109],
    15: [119],
}


class Gather:
    def __init__(self, shard, piece, send, recv, local, me, rep):
        self.shard, self.piece, self.send, self.recv, self.me, self.rep = shard, piece, send, recv, me, rep
        self.own = pltpu.make_async_copy(shard, piece(me), local)

    def copy(self, name):
        rep_to, me_to, whose, what, _ = MESSAGES[name]
        s = ARRIVALS.index(name) if name in ARRIVALS else 0
        third = D_MODEL // 3
        parity = self.rep % 2
        cols = {
            "all": lambda: pl.ds(0, D_MODEL),
            "mine": lambda: pl.ds(pl.multiple_of(parity * 2 * third, 128), third),
            "middle": lambda: pl.ds(third, third),
            "other": lambda: pl.ds(pl.multiple_of((1 - parity) * 2 * third, 128), third),
        }[what]()
        piece = self.piece(self.me ^ whose)
        src = self.shard if whose == 0 else piece
        return pltpu.make_async_remote_copy(
            src_ref=src.at[:, cols], dst_ref=piece.at[:, cols], send_sem=self.send, recv_sem=self.recv.at[s],
            device_id=(self.rep ^ rep_to, self.me ^ me_to), device_id_type=MESH,
        )

    def relay(self, arrival):
        if arrival is None:
            self.own.start()
        else:
            self.copy(arrival).wait_recv()
        for name, message in MESSAGES.items():
            if message[4] == arrival:
                self.copy(name).start()

    def complete(self):
        self.own.wait()
        four = self.piece(pl.ds(0, 4))
        pltpu.make_async_copy(four, four, self.recv.at[0]).wait()

    def finish(self):
        seven = self.piece(pl.ds(0, 7))
        pltpu.make_async_copy(seven, seven, self.send).wait()


class Local:
    def __init__(self, shard, place, local):
        self.own = pltpu.make_async_copy(shard, place, local)

    def relay(self, arrival):
        if arrival is None:
            self.own.start()

    def complete(self):
        self.own.wait()

    def finish(self):
        pass


def dispatch(step, table):
    keys = sorted(table)
    if len(keys) < 4:
        for k in keys:
            pl.when(step == k)(table[k])
    else:
        middle = keys[len(keys) // 2]
        pl.when(step < middle)(lambda: dispatch(step, {k: table[k] for k in keys if k < middle}))
        pl.when(step >= middle)(lambda: dispatch(step, {k: table[k] for k in keys if k >= middle}))


def flat(t):
    return t.reshape(t.shape[0] * t.shape[1], t.shape[2])


def gain_rows(ga, gm):
    n = ga.shape[1]
    row = lax.broadcasted_iota(jnp.int32, (16, n), 0)
    pair = jnp.where(row == 0, ga.astype(f32), jnp.where(row == 1, gm.astype(f32), 0.0))
    return jnp.concatenate([pair, jnp.zeros((16, 128 - n), f32)], axis=1).astype(bf)


def spread(pieces):
    width = D_MODEL // 8
    lane = lax.broadcasted_iota(jnp.int32, (128, D_MODEL), 0)
    place = lax.broadcasted_iota(jnp.int32, (128, D_MODEL), 1)
    total = jnp.zeros((16, D_MODEL), f32)
    for d in range(8):
        hit = (place == lane + d * width) & (lane < width)
        total = total + nn(pieces[d], jnp.where(hit, 1.0, 0.0).astype(bf))
    return total[:8]


def kernel_one(
    remote, lengths, x, dy, ga, gm, q_in, o_in, i_in, t_in,
    qkv_out, probs_out, u_out, h_out, wn_out, za_out, dh_out, do_out, gains_out, gwo_out, wq_out, wt_out,
    wq, wo, wi, wt, gain_piece, gain_parts, gains, high, low, qa, zs, mixed_all, wn, send, recv, gain_send, gain_recv, local, out_sem, a_sem, dz_sem,
):
    step = pl.program_id(0)
    T, D = high.shape
    tiles = T // TILE
    p_h = P_B + tiles
    p_in, p_back = p_h + 2, p_h + 10
    steps = p_back + tiles
    me, rep = lax.axis_index("fsdp"), lax.axis_index("rep")
    part = lambda j: pl.ds(j * D, D)
    rows_of_part = lambda j: pl.ds(j * 96, 96)
    if remote:
        refs = [(q_in.at[:, part(j)], lambda p, j=j: wq.at[j, p]) for j in range(3)]
        refs += [(o_in, lambda p: wo.at[p])]
        refs += [(i_in.at[:, part(j)], lambda p, j=j: wi.at[j, p]) for j in range(4)]
        refs += [(t_in.at[rows_of_part(j)], lambda p, j=j: wt.at[p, rows_of_part(j)]) for j in range(4)]
        blocks = [Gather(s, f, send.at[k], recv.at[k], local.at[k], me, rep) for k, (s, f) in enumerate(refs)]
    else:
        refs = [(q_in.at[:, :, part(j)], wq.at[j]) for j in range(3)] + [(o_in, wo)]
        refs += [(i_in.at[:, :, part(j)], wi.at[j]) for j in range(4)]
        refs += [(t_in.at[:, rows_of_part(j)], wt.at[:, rows_of_part(j)]) for j in range(4)]
        blocks = [Local(s, f, local.at[k]) for k, (s, f) in enumerate(refs)]

    def gain_copy(d):
        return pltpu.make_async_remote_copy(
            src_ref=gain_piece, dst_ref=gain_parts.at[me], send_sem=gain_send.at[d], recv_sem=gain_recv.at[d],
            device_id=(rep, me ^ d), device_id_type=MESH,
        )

    load_x = pltpu.make_async_copy(x, high, local.at[13])
    export = pltpu.make_async_copy(wq, wq_out, out_sem.at[0])
    store_u = pltpu.make_async_copy(low, u_out, out_sem.at[1])
    store_wn = pltpu.make_async_copy(wn, wn_out, out_sem.at[2])
    store_h = [pltpu.make_async_copy(v, h_out.at[k], out_sem.at[7 + k]) for k, v in enumerate((high, low))]
    export_wt = pltpu.make_async_copy(wt, wt_out, out_sem.at[9])
    store_gwo = pltpu.make_async_copy(mixed_all.at[pl.ds(0, D)], gwo_out, out_sem.at[3])

    def store_qkv(j):
        cols = pl.ds(pl.multiple_of(j * D, D), D)
        return pltpu.make_async_copy(qa.at[:, cols], qkv_out.at[:, cols], out_sem.at[4 + j])

    def rows_at(t, n):
        return pl.ds(pl.multiple_of(t * n, n), n)

    def store_a(e):
        place = (rows_at(lax.rem(e, 2), T // 2), pl.ds(pl.multiple_of(lax.div(e, 2) * FC, FC), FC))
        return pltpu.make_async_copy(qa.at[place], za_out.at[(1, *place)], a_sem.at[e])

    def store_dz(t):
        return pltpu.make_async_copy(zs.at[rows_at(t, TILE)], za_out.at[0, rows_at(t, TILE)], dz_sem.at[t])

    def relay(code):
        blocks[code // 10].relay(ARRIVALS[code % 10])

    @pl.when(step == 0)
    def _():
        load_x.start()
        if remote:
            gain_piece[...] = gain_rows(ga[...], gm[...])
            barrier = pltpu.get_barrier_semaphore()
            for d in range(1, 8):
                pl.semaphore_signal(barrier, inc=1, device_id=(rep, me ^ d), device_id_type=MESH)
            pl.semaphore_signal(barrier, inc=1, device_id=(rep ^ 1, me), device_id_type=MESH)
            pl.semaphore_wait(barrier, 8)
            for d in range(1, 8):
                gain_copy(d).start()
        for code in RELAYS[0][:EARLY]:
            relay(code)
        if remote:
            gain_parts[me] = gain_piece[...]
            for d in range(1, 8):
                gain_copy(d).wait_recv()
        else:
            for d in range(8):
                gain_parts[d] = gain_rows(ga[d : d + 1], gm[d : d + 1])
        gains[...] = spread(gain_parts)
        gains_out[...] = gains[...]
        load_x.wait()
        later = RELAYS[0][EARLY:]
        for t in range(max(tiles, len(later))):
            if t < tiles:
                rows = pl.ds(t * TILE, TILE)
                n, _ = moments(high[rows, :].astype(f32))
                low[rows, :] = (n * gains[0:1]).astype(bf)
            if t < len(later):
                relay(later[t])
        store_u.start()
        blocks[0].complete()

    completes = {1: [1], 2: [2], p_h: [3], p_back: [8, 9, 10, 11]}
    completes.update({p_in + 2 * j: [4 + j] for j in range(4)})

    def begin(at):
        for code in RELAYS.get(at, []):
            relay(code)
        for k in completes.get(at, []):
            blocks[k].complete()
        if at == P_B:
            export.start()
        if at == p_h:
            store_u.wait()
        if at == p_back:
            export_wt.start()
            for store in store_h:
                store.wait()
        if at == p_in:
            store_wn.start()
            for store in store_h:
                store.start()
            for j in range(3):
                store_qkv(j).wait()

    dispatch(step, {at: functools.partial(begin, at) for at in {*RELAYS, *completes, P_B} - {0}})

    @pl.when(step < P_B)
    def _():
        w = flat(wq[step])
        block = 2 * TILE
        cols = pl.ds(pl.multiple_of(step * D, D), D)
        for t in range(T // block):
            qa[t * block : (t + 1) * block, cols] = nn(low[t * block : (t + 1) * block], w).astype(bf)
        store_qkv(step).start()

    @pl.when((step >= P_B) & (step < p_h))
    def _():
        t = step - P_B
        for rr in range(TILE // SPAN):
            rows = pl.ds(pl.multiple_of(t * TILE + rr * SPAN, SPAN), SPAN)
            mask = permitted(lengths, t * (TILE // SPAN) + rr)
            probs, mixed = attend(lambda c: qa[rows, c : c + 128], mask)
            for p in range(6):
                probs_out[rr * SPAN : (rr + 1) * SPAN, p * 2 * SPAN : (p + 1) * 2 * SPAN] = probs[p]
                mixed_all[rows, p * 128 : (p + 1) * 128] = mixed[p]

    @pl.when((step >= p_h) & (step < p_in))
    def _():
        for s in range(tiles // 2):
            rows = rows_at((step - p_h) * (tiles // 2) + s, TILE)
            h = high[rows, :].astype(f32) + nn(mixed_all[rows, :], flat(wo[...]))
            top = h.astype(bf)
            high[rows, :] = top
            low[rows, :] = (h - top.astype(f32)).astype(bf)
            n, _ = moments(h)
            wn[rows, :] = (n * gains[1:2]).astype(bf)

    @pl.when((step >= p_in) & (step < p_back))
    def _():
        e = step - p_in
        j, half = lax.div(e, 2), lax.rem(e, 2)
        cols = pl.ds(pl.multiple_of(j * FC, FC), FC)
        w = flat(wi[j])
        block = 2 * TILE
        for s in range(T // 2 // block):
            rows = rows_at(half * (T // 2 // block) + s, block)
            z = nn(wn[rows, :], w)
            qa[rows, cols] = gelu(z).astype(bf)
            zs[rows, cols] = z.astype(bf)
        store_a(e).start()

    per = FC // wt.shape[1]

    @pl.when(step >= p_back)
    def _():
        t = step - p_back
        rows = rows_at(t, TILE)
        h = high[rows, :].astype(f32) + low[rows, :].astype(f32)
        n, r = moments(h)
        dm = dy[...]
        dw = None
        for j in range(wi.shape[0]):
            cols = slice(j * FC, (j + 1) * FC)
            w_out = flat(wt[j * per : (j + 1) * per])
            dz = (nt(dm, w_out) * gelu_slope(zs[rows, cols].astype(f32))).astype(bf)
            zs[rows, cols] = dz
            add = nt(dz, flat(wi[j]))
            dw = add if dw is None else dw + add
        store_dz(t).start()
        dt = (dm.astype(f32) + norm_back(dw, n, r, gains[1:2])).astype(bf)
        dh_out[...] = dt
        high[rows, :] = dt
        do_out[...] = nt(dt, flat(wo[...])).astype(bf)

    @pl.when(step == steps - 1)
    def _():
        gwo = tn(mixed_all[...], high[...]).astype(bf)
        mixed_all[0:D, :] = gwo
        store_gwo.start()
        export.wait()
        export_wt.wait()
        store_wn.wait()
        for t in range(tiles):
            store_a(t).wait()
            store_dz(t).wait()
        if remote:
            for d in range(1, 8):
                gain_copy(d).wait_send()
        for b in blocks:
            b.finish()
        store_gwo.wait()


def forward_and_mlp(remote, x, lengths, dy, ga, gm, w_qkv, w_ao, w_in, w_out):
    T, D = x.shape
    tiles = T // TILE
    F = w_in.shape[-1]
    rows = D // 8

    def tile_from(start, *shape):
        return pl.BlockSpec(shape, lambda i: (jnp.clip(i - start, 0, tiles - 1),) + (0,) * (len(shape) - 1))

    p_back = P_B + tiles + 10
    whole = pl.BlockSpec(ga.shape, lambda i: (0, 0))
    hbm = pl.BlockSpec(memory_space=pl.ANY)

    return pl.pallas_call(
        functools.partial(kernel_one, remote),
        name="forward_and_mlp",
        grid=(p_back + tiles,),
        in_specs=[pl.BlockSpec(memory_space=pltpu.SMEM), hbm, tile_from(p_back, TILE, D), whole, whole, hbm, hbm, hbm, hbm],
        out_specs=[
            hbm, tile_from(P_B, TILE, 2 * D), hbm, hbm, hbm, hbm,
            tile_from(p_back, TILE, D), tile_from(p_back, TILE, D), pl.BlockSpec((8, D), lambda i: (0, 0)), hbm, hbm, hbm,
        ],
        out_shape=[
            sds(T, 3 * D), sds(T, 2 * D), sds(T, D),
            sds(2, T, D), sds(T, D), sds(2, T, F), sds(T, D), sds(T, D), sds(8, D, dtype=f32), sds(D, D), sds(3, 8, rows, D), sds(8, F // 8, D),
        ],
        scratch_shapes=[
            pltpu.VMEM((3, 8, rows, D), bf), pltpu.VMEM((8, rows, D), bf), pltpu.VMEM((F // FC, 8, rows, FC), bf),
            pltpu.VMEM((8, F // 8, D), bf), pltpu.VMEM((16, 128), bf), pltpu.VMEM((8, 16, 128), bf), pltpu.VMEM((8, D), f32), pltpu.VMEM((T, D), bf),
            pltpu.VMEM((T, D), bf), pltpu.VMEM((T, F), bf), pltpu.VMEM((T, F), bf), pltpu.VMEM((T, D), bf), pltpu.VMEM((T, D), bf),
            pltpu.SemaphoreType.DMA((12,)), pltpu.SemaphoreType.DMA((12, len(ARRIVALS))), pltpu.SemaphoreType.DMA((8,)), pltpu.SemaphoreType.DMA((8,)),
            pltpu.SemaphoreType.DMA((14,)), pltpu.SemaphoreType.DMA((10,)), pltpu.SemaphoreType.DMA((tiles,)), pltpu.SemaphoreType.DMA((tiles,)),
        ],
        cost_estimate=pl.CostEstimate(flops=12 * T * D * D + 8 * T * D * F + 6 * T * D * D, bytes_accessed=90 << 20, transcendentals=0),
        compiler_params=pltpu.CompilerParams(
            vmem_limit_bytes=VMEM, has_side_effects=remote, collective_id=1 if remote else None
        ),
    )(lengths.T, x, dy, ga, gm, w_qkv, w_ao, w_in, w_out)


CHUNK = 96
WIDE = 768
RING = 6
N_WIDE = 12
P_IN, P_OUT, P_ATT = 0, 4, 8
P_DX = P_ATT + 9
P_Y = P_DX + 4
STEPS = P_Y + 4
BLOCK = 512
REUSE = {P_ATT + 5: [0], P_ATT + 8: [1], P_DX + 2: [2, 3, 4, 5]}
START = [
    [1, 2, 5, 7, 10, 13, 15], [1, 3, 7, 9, 12, 14, 19], [2, 4, 7, 9, 12, 15, 25], [3, 5, 8, 10, 13, 16, 20],
    [6, 8, 10, 12, 14, 16, 26], [8, 9, 12, 14, 16, 18, 27], [8, 11, 13, 15, 17, 19, 29], [11, 12, 15, 17, 19, 21, 24],
    [8, 10, 13, 16, 18, 20, 25], [12, 14, 16, 18, 20, 22, 28], [15, 16, 19, 20, 22, 23, 32], [17, 18, 20, 21, 22, 24, 28],
]
RECEIVE = {"s1": 0, "s2x": 1, "s2y": 1, "s3y": 2, "s3x": 2, "z1": 3, "z2": 4, "z3": 3}


def slot_of(k):
    return k if k < 10 else k - 10


class Reduce:
    def __init__(self, k, grads, bufs, send, recv, place):
        self.n = k
        first, x2, y2, y3, x3, outer, inner, out = bufs
        r = k % RING
        self.g = grads.at[slot_of(k)]
        self.first, self.x2, self.y2 = first.at[r], x2.at[r], y2.at[r]
        self.x3, self.y3, self.outer, self.inner, self.out = x3.at[k], y3.at[k], outer.at[k], inner.at[k], out.at[k]
        self.send, self.recv = send, recv
        self.y, self.x, self.c, self.me, self.rep = place
        self.is_inner = (self.rep == 1) | (self.rep == 2)

    def copy(self, m):
        g, y, x, c = self.g, self.y, self.x, self.c
        upper, lower = pl.ds(0, CHUNK // 2), pl.ds(CHUNK // 2, CHUNK // 2)
        src, dst, rep_to, me_to = {
            "s1": lambda: (g.at[:, :, 1 - c], self.first, 0, 1),
            "s2x": lambda: (g.at[:, 1 - x, c, upper], self.x2, 0, 2),
            "s2y": lambda: (g.at[1 - y, :, c, lower], self.y2, 0, 4),
            "s3y": lambda: (g.at[1 - y, x, c, upper], self.y3, 0, 4),
            "s3x": lambda: (g.at[y, 1 - x, c, lower], self.x3, 0, 2),
            "z1": lambda: (g.at[y, x, c], self.outer, 1, 0),
            "z2": lambda: (g.at[y, x, c], self.inner, 3, 0),
            "z3": lambda: (self.out, self.out, 1, 0),
        }[m]()
        return pltpu.make_async_remote_copy(
            src_ref=src, dst_ref=dst, send_sem=self.send.at[self.n, int(m == "z3")], recv_sem=self.recv.at[self.n, RECEIVE[m]],
            device_id=(self.rep ^ rep_to, self.me ^ me_to), device_id_type=MESH,
        )

    def start(self, *names):
        for m in names:
            self.copy(m).start()

    def arrived(self, m, ref):
        pltpu.make_async_copy(ref, ref, self.recv.at[self.n, RECEIVE[m]]).wait()

    def stage(self, s):
        g, y, x, c = self.g, self.y, self.x, self.c
        upper, lower = pl.ds(0, CHUNK // 2), pl.ds(CHUNK // 2, CHUNK // 2)
        if s == 1:
            self.start("s1")
        elif s == 2:
            self.arrived("s1", self.first)
            for b in range(2):
                for a in range(2):
                    g[b, a, c] += self.first[b, a]
            self.start("s2x", "s2y")
        elif s == 3:
            self.arrived("s2x", g.at[0, 0])
            for b in range(2):
                g[b, x, c, upper] += self.x2[b]
                g[y, b, c, lower] += self.y2[b]
            self.start("s3y", "s3x")
        elif s == 4:
            self.arrived("s3y", g.at[0, 0, 0])
            g[y, x, c, upper] += self.y3[...]
            g[y, x, c, lower] += self.x3[...]

            @pl.when(jnp.logical_not(self.is_inner))
            def _():
                self.start("z1")
        elif s == 5:
            @pl.when(self.is_inner)
            def _():
                self.arrived("z1", self.outer)
                g[y, x, c] += self.outer[...]
                self.start("z2")
        elif s == 6:
            @pl.when(self.is_inner)
            def _():
                self.arrived("z2", self.inner)
                self.out[...] = g[y, x, c] + self.inner[...]
                self.start("z3")
        elif s == 7:
            @pl.when(jnp.logical_not(self.is_inner))
            def _():
                self.arrived("z3", self.out)

    def sent(self):
        pltpu.make_async_copy(self.g, self.g, self.send.at[self.n, 0]).wait()

    def sum_sent(self):
        @pl.when(self.is_inner)
        def _():
            pltpu.make_async_copy(self.out, self.out, self.send.at[self.n, 1]).wait()


def part_of(e):
    return 2 * lax.div(e, 3) + jnp.minimum(lax.rem(e, 3), 1), lax.rem(e, 3) == 2


def kernel_two(
    gwo_in, wn, dm, u, wq, wt, gains, za, qkv, probs, do, x, dh, h,
    dx_out, y_out, out_hbm,
    out, big_a, big_b, wq_s, dqkv, grads, first, x2, y2, y3, x3, outer, inner, stream, halves, result,
    send, recv, local, load_sem, store_sem,
):
    step = pl.program_id(0)
    T, D = big_a.shape
    me, rep = lax.axis_index("fsdp"), lax.axis_index("rep")
    place = (me // 4, (me // 2) % 2, me % 2, me, rep)
    bufs = (first, x2, y2, y3, x3, outer, inner, out)
    chunks = [Reduce(n, grads, bufs, send, recv, place) for n in range(len(START))]
    load_gwo = pltpu.make_async_copy(gwo_in, grads.at[0], local.at[0])
    load_wn = pltpu.make_async_copy(wn, big_a, local.at[1])
    load_dm = pltpu.make_async_copy(dm, big_b, local.at[2])
    load_u = pltpu.make_async_copy(u, big_a, local.at[3])
    load_wq = pltpu.make_async_copy(wq, wq_s, local.at[4])
    store_out = pltpu.make_async_copy(out, out_hbm, local.at[5])
    load_wt = pltpu.make_async_copy(wt, grads.at[pl.ds(2, 4)], local.at[6])

    def loads(at):
        s = at % 2
        to = stream.at[s]
        if at < P_ATT:
            pairs = [(za.at[at // 4, :, pl.ds(at % 4 * WIDE, WIDE)], to)]
        elif at < P_DX:
            e = at - P_ATT
            if e % 3 == 2:
                return []
            p = e // 3 * 2 + e % 3
            pairs = [(qkv.at[:, pl.ds(j * D + p * 128, 128)], to.at[:, pl.ds(j * 128, 128)]) for j in range(3)]
            pairs.append((do.at[:, pl.ds(p * 128, 128)], to.at[:, pl.ds(384, 128)]))
            pairs.append((probs.at[:, pl.ds(p * 256, 256)], to.at[:, pl.ds(512, 256)]))
        elif at < P_Y:
            rows = pl.ds((at - P_DX) * BLOCK, BLOCK)
            pairs = [(x.at[rows], to.at[pl.ds(0, BLOCK)]), (dh.at[rows], to.at[pl.ds(BLOCK, BLOCK)])]
        else:
            rows = pl.ds((at - P_Y) * BLOCK, BLOCK)
            pairs = [(za.at[1, rows, pl.ds(j * WIDE, WIDE)], to.at[pl.ds(j * BLOCK, BLOCK)]) for j in range(4)]
            pairs.append((h.at[:, rows], halves.at[s]))
        return [pltpu.make_async_copy(src, dst, load_sem.at[s, k]) for k, (src, dst) in enumerate(pairs)]

    def store(at):
        to, t = (dx_out, at - P_DX) if at < P_Y else (y_out, at - P_Y)
        return pltpu.make_async_copy(result.at[at % 2], to.at[pl.ds(t * BLOCK, BLOCK)], store_sem.at[at % 2])

    acts = {}
    for n, starts in enumerate(START):
        for s, at in enumerate(starts):
            acts.setdefault(at, []).append((n, s + 1))

    def act(at):
        for n, s in sorted(acts[at], key=lambda ns: -ns[1]):
            chunks[n].stage(s)

    def begin(at):
        if at == 0:
            load_wn.start()
            for load in loads(0):
                load.start()
            barrier = pltpu.get_barrier_semaphore()
            for to in ((rep, me ^ 1), (rep, me ^ 2), (rep, me ^ 4), (rep ^ 1, me), (rep ^ 3, me)):
                pl.semaphore_signal(barrier, inc=1, device_id=to, device_id_type=MESH)
            pl.semaphore_wait(barrier, 5)
            load_wn.wait()
        for load in loads(at):
            load.wait()
        if at == 0:
            load_gwo.start()
        if at + 1 < STEPS:
            for load in loads(at + 1):
                load.start()
        if at == 1:
            load_dm.start()
            load_gwo.wait()
        if at in acts:
            act(at)
        if at == P_OUT:
            load_u.start()
            load_dm.wait()
        if at == P_OUT + 1:
            load_wq.start()
        if at == P_ATT + 2:
            load_u.wait()
            load_wq.wait()
        for k in REUSE.get(at, []):
            chunks[k].sent()
        if at == P_DX + 2:
            load_wt.start()
        if at == P_Y:
            load_wt.wait()
        if at >= P_DX + 2:
            store(at - 2).wait()

    dispatch(step, {at: functools.partial(begin, at) for at in range(STEPS)})

    slot = lax.rem(step, 2)

    @pl.when(step < P_OUT)
    def _():
        g = tn(big_a[...], stream[slot]).astype(bf)
        grads[1 + step] = g.reshape(2, 2, 2, CHUNK, WIDE)

    @pl.when((step >= P_OUT) & (step < P_ATT))
    def _():
        j = step - P_OUT
        g = tn(stream[slot], big_b[...]).astype(bf).reshape(2, 4, CHUNK, WIDE)
        for part in range(4):
            grads[5 + part, j // 2, j % 2] = g[:, part]

    pair, product = part_of(step - P_ATT)
    attention = (step >= P_ATT) & (step < P_DX)

    @pl.when(attention & jnp.logical_not(product))
    def _():
        for rr in range(T // SPAN):
            rows = slice(rr * SPAN, (rr + 1) * SPAN)
            q2, k2, v2, do2 = (stream[slot, rows, j * 128 : (j + 1) * 128] for j in range(4))
            back = attend_back(q2, k2, v2, stream[slot, rows, 512:768], do2)
            for j in range(3):
                to_cols = pl.ds(pl.multiple_of(lax.rem(pair, 2) * (WIDE // 2) + j * 128, 128), 128)
                dqkv[lax.div(pair, 2), rows, to_cols] = back[j]

    @pl.when(attention & product)
    def _():
        k = lax.div(pair, 2)
        g = tn(big_a[...], dqkv[k]).astype(bf)
        grads[jnp.where(k == 0, 9, k - 1)] = g.reshape(2, 2, 2, CHUNK, WIDE)

    @pl.when((step >= P_DX) & (step < P_Y))
    def _():
        for part in range(BLOCK // TILE):
            here = slice(part * TILE, (part + 1) * TILE)
            rows = pl.ds(pl.multiple_of((step - P_DX) * BLOCK + part * TILE, TILE), TILE)
            n, r = moments(stream[slot, here].astype(f32))
            du = 0.0
            for j in range(3):
                at = [(p // 2, (p % 2) * (WIDE // 2) + j * 128) for p in range(D // 128)]
                du = du + nt(jnp.concatenate([dqkv[k, rows, c : c + 128] for k, c in at], axis=1), flat(wq_s[j]))
            dt = stream[slot, BLOCK + part * TILE : BLOCK + (part + 1) * TILE].astype(f32)
            result[slot, here] = (dt + norm_back(du, n, r, gains[0:1])).astype(bf)
        for at in range(P_DX, P_Y):
            @pl.when(step == at)
            def _(at=at):
                store(at).start()

    @pl.when(step >= P_Y)
    def _():
        y = halves[slot, 0].astype(f32) + halves[slot, 1].astype(f32)
        for j in range(4):
            y = y + nn(stream[slot, j * BLOCK : (j + 1) * BLOCK], grads[2 + j].reshape(WIDE, WIDE))
        result[slot] = y.astype(bf)
        for at in range(P_Y, STEPS):
            @pl.when(step == at)
            def _(at=at):
                store(at).start()

    @pl.when(step == STEPS - 1)
    def _():
        for at in sorted(acts):
            if at >= STEPS:
                act(at)
        store_out.start()
        for n in range(len(START)):
            if n not in sum(REUSE.values(), []):
                chunks[n].sent()
            chunks[n].sum_sent()
        for at in (STEPS - 2, STEPS - 1):
            store(at).wait()
        store_out.wait()


def gradients(gwo, wn, dy, u, wq, wt, gains, za, qkv, probs, do, x, dh, h):
    T, D = x.shape
    hbm = pl.BlockSpec(memory_space=pl.ANY)
    wide = lambda *shape: pltpu.VMEM(shape + (WIDE,), bf)
    return pl.pallas_call(
        kernel_two,
        name="gradients",
        grid=(STEPS,),
        in_specs=[hbm] * 6 + [pl.BlockSpec((8, D), lambda i: (0, 0))] + [hbm] * 7,
        out_specs=[hbm] * 3,
        out_shape=[sds(T, D), sds(T, D), sds(N_WIDE, CHUNK, WIDE)],
        scratch_shapes=[
            wide(N_WIDE, CHUNK), wide(T), wide(T), pltpu.VMEM(wq.shape, bf), wide(3, T),
            wide(10, 2, 2, 2, CHUNK), wide(RING, 2, 2, CHUNK), wide(RING, 2, CHUNK // 2),
            wide(RING, 2, CHUNK // 2), wide(N_WIDE, CHUNK // 2), wide(N_WIDE, CHUNK // 2), wide(N_WIDE, CHUNK), wide(N_WIDE, CHUNK),
            wide(2, T), wide(2, 2, BLOCK), wide(2, BLOCK),
            pltpu.SemaphoreType.DMA((len(START), 2)), pltpu.SemaphoreType.DMA((len(START), 5)), pltpu.SemaphoreType.DMA((7,)),
            pltpu.SemaphoreType.DMA((2, 5)), pltpu.SemaphoreType.DMA((2,)),
        ],
        cost_estimate=pl.CostEstimate(flops=8 * T * D * D + 4 * T * D * 4 * D + 20 * T * D * D, bytes_accessed=90 << 20, transcendentals=0),
        compiler_params=pltpu.CompilerParams(vmem_limit_bytes=VMEM, has_side_effects=True, collective_id=2),
    )(gwo.reshape(2, 2, 2, CHUNK, WIDE), wn, dy, u, wq, wt.reshape(4, 2, 2, 2, CHUNK, WIDE), gains, za, qkv, probs, do, x, dh, h)


def kernel_finish(sums, wq, wi, ga, gm, y, dx, y_out, dx_out, gq, gwo, gwi, gwt, gg1, gg2, hold, sem):
    parts = sem.shape[2]
    n = y.shape[0] // parts
    moves = []
    for p in range(parts):
        for k, (src, dst) in enumerate(((y, y_out), (dx, dx_out))):
            rows = pl.ds(p * n, n)
            there = pltpu.make_async_copy(src.at[rows], hold.at[k, rows], sem.at[0, k, p])
            moves.append((there, pltpu.make_async_copy(hold.at[k, rows], dst.at[rows], sem.at[1, k, p])))
            there.start()
    D = gwo.shape[1]
    gwo[...] = sums[0].astype(f32)
    for j in range(4):
        gwi[:, j * D : (j + 1) * D] = sums[1 + j].astype(f32)
        gwt[j * CHUNK : (j + 1) * CHUNK, :] = sums[5 + j].astype(f32)
    for pair in range(D // 128):
        for j in range(3):
            cols = (pair % 2) * (WIDE // 2) + j * 128
            gq[:, j * D + pair * 128 : j * D + pair * 128 + 128] = sums[9 + pair // 2, :, cols : cols + 128].astype(f32)
    for there, out in moves:
        there.wait()
        out.start()
    for grad, w, gain, out in ((gq, wq, ga, gg1), (gwi, wi, gm, gg2)):
        acc = jnp.zeros((CHUNK, 128), f32)
        for c in range(0, w.shape[1], 128):
            acc = acc + w[:, c : c + 128].astype(f32) * grad[:, c : c + 128]
        out[...] = jnp.sum(acc.T, axis=0, keepdims=True) / gain[...].astype(f32)
    for _, out in moves:
        out.wait()


def finish(sums, w_qkv, w_mlp_in, gain_attn, gain_mlp, y, dx):
    rows, D = w_qkv.shape[0], w_qkv.shape[1] // 3
    vmem, hbm = pl.BlockSpec(memory_space=pltpu.VMEM), pl.BlockSpec(memory_space=pl.ANY)
    fs = functools.partial(sds, dtype=f32)
    y, dx, gq, gwo, gwi, gwt, gg1, gg2 = pl.pallas_call(
        kernel_finish,
        name="finish",
        in_specs=[vmem] * 5 + [hbm] * 2,
        out_specs=[hbm] * 2 + [vmem] * 6,
        out_shape=[sds(*y.shape), sds(*dx.shape), fs(rows, 3 * D), fs(rows, D), fs(rows, 4 * D), fs(4 * rows, D), fs(1, rows), fs(1, rows)],
        scratch_shapes=[pltpu.VMEM((2, *y.shape), bf), pltpu.SemaphoreType.DMA((2, 2, 4))],
        cost_estimate=pl.CostEstimate(flops=1 << 20, bytes_accessed=20 << 20, transcendentals=0),
        compiler_params=pltpu.CompilerParams(vmem_limit_bytes=VMEM),
    )(sums, w_qkv, w_mlp_in, gain_attn.reshape(1, rows), gain_mlp.reshape(1, rows), y, dx)
    return y, dx, gg1.reshape(rows), gq, gwo, gg2.reshape(rows), gwi, gwt


def shards(x, lengths, segments, gain_attn, w_qkv, w_attn_out, gain_mlp, w_mlp_in, w_mlp_out, dy):
    D = x.shape[1]
    remote = lax.axis_size("fsdp") == 8 and lax.axis_size("rep") == 4
    ga, gm = gain_attn.reshape(1, -1), gain_mlp.reshape(1, -1)
    weights = (w_qkv, w_attn_out, w_mlp_in, w_mlp_out)
    if not remote:
        weights = tuple(lax.all_gather(v, "fsdp", axis=0, tiled=True) for v in weights)
        weights = tuple(v.reshape(8, v.shape[0] // 8, v.shape[1]) for v in weights)
        ga, gm = (lax.all_gather(v, "fsdp", axis=0, tiled=True).reshape(8, -1) for v in (gain_attn, gain_mlp))
    qkv, probs, u, h, wn, za, dh, do, gains, gwo, wq, wt = forward_and_mlp(remote, x, lengths, dy, ga, gm, *weights)
    if remote:
        dx, y, sums = gradients(gwo, wn, dy, u, wq, wt, gains, za, qkv, probs, do, x, dh, h)
        return finish(sums, w_qkv, w_mlp_in, gain_attn, gain_mlp, y, dx)
    scatter = lambda v: lax.psum_scatter(v, "fsdp", scatter_dimension=0, tiled=True)
    gwt = scatter(weight_grad(za[1], dy, "mlp_out_grad", 768, bf, "left"))
    gwi = scatter(weight_grad(wn, za[0], "mlp_in_grad", 768))
    gwo = scatter(gwo)
    dqkv = attention_back(qkv, probs, do)
    gq = scatter(weight_grad(u, dqkv, "qkv_grad", 768))
    dx = input_grad(x, dqkv, dh.astype(f32), gains[0:1], wq.transpose(1, 2, 0, 3).reshape(D, 3 * D))
    y = jnp.sum(h.astype(f32), axis=0) + jnp.dot(za[1], wt.reshape(-1, D), preferred_element_type=f32)
    y = y.astype(bf)
    gwt, gwi, gwo, gq = lax.psum((gwt, gwi, gwo, gq), "rep")
    gwt, gwi, gwo, gq = (v.astype(f32) for v in (gwt, gwi, gwo, gq))
    gg1 = jnp.sum(w_qkv.astype(f32) * gq, axis=1) / gain_attn.astype(f32)
    gg2 = jnp.sum(w_mlp_in.astype(f32) * gwi, axis=1) / gain_mlp.astype(f32)
    return y, dx, gg1, gq, gwo, gg2, gwi, gwt


def solution(mesh):
    tokens, cut, vec = P(("rep", "fsdp"), None), P("fsdp", None), P("fsdp")
    return jax.shard_map(
        shards,
        mesh=mesh,
        in_specs=(tokens, tokens, P(("rep", "fsdp")), vec, cut, cut, vec, cut, cut, tokens),
        out_specs=(tokens, tokens, vec, cut, cut, vec, cut, cut),
        check_vma=False,
    )
```

```python
import functools, math
import jax, jax.numpy as jnp
from jax import lax
from jax.experimental import pallas as pl
from jax.experimental.pallas import tpu as pltpu
from jax.sharding import PartitionSpec as P
bf = jnp.bfloat16
f32 = jnp.float32
EPS = 1e-05
NEG = -1e30
SPAN = 128
TILE = 256
VMEM = 63 * 1024 * 1024
SCALE = 64 ** -0.5
LOG2E = math.log2(math.e)
GC = math.sqrt(2.0 / math.pi)
GK = 0.044715


def nn(a, b):
    return lax.dot_general(a, b, (((1,), (0,)), ((), ())), preferred_element_type=f32)


def nt(a, b):
    return lax.dot_general(a, b, (((1,), (1,)), ((), ())), preferred_element_type=f32)


def tn(a, b):
    return lax.dot_general(a, b, (((0,), (0,)), ((), ())), preferred_element_type=f32)


def moments(v):
    c = v - jnp.mean(v, axis=-1, keepdims=True)
    r = lax.rsqrt(jnp.mean(c * c, axis=-1, keepdims=True) + EPS)
    return c * r, r


def norm_back(e, n, r, g):
    s = e * g
    inner = s - jnp.mean(s, axis=-1, keepdims=True) - n * jnp.mean(s * n, axis=-1, keepdims=True)
    return inner * r


def split_heads(t):
    low = lax.broadcasted_iota(jnp.int32, t.shape, 1) < 64
    zero = jnp.zeros_like(t)
    return jnp.concatenate([jnp.where(low, t, zero), jnp.where(low, zero, t)], axis=0)


def stack_lanes(t):
    return jnp.concatenate([t[:, :SPAN], t[:, SPAN:]], axis=0)


def permitted(lengths, row):
    ends = []
    total = 0
    for k in range(4):
        total = total + lengths[k, row]
        ends.append(total)
    key = lax.broadcasted_iota(jnp.int32, (SPAN, SPAN), 0)
    query = lax.broadcasted_iota(jnp.int32, (SPAN, SPAN), 1)
    one, zero = jnp.int32(1), jnp.int32(0)
    seg_key = sum(jnp.where(key >= e, one, zero) for e in ends)
    seg_query = sum(jnp.where(query >= e, one, zero) for e in ends)
    return (seg_key == seg_query) & ((key < total) | (key == query))


def attend(qkv, mask):
    mask2 = jnp.concatenate([mask, mask], axis=1)
    probs, mixed = [], []
    for p in range(6):
        q2, k2, v2 = qkv(p * 128), qkv(768 + p * 128), qkv(1536 + p * 128)
        s = jnp.where(mask2, nt(k2, split_heads(q2)), NEG)
        top = jnp.max(s, axis=0, keepdims=True)
        e = jnp.exp2((s - top) * (SCALE * LOG2E))
        w = (e * (1.0 / jnp.sum(e, axis=0, keepdims=True))).astype(bf)
        probs.append(w)
        mixed.append(tn(stack_lanes(w), split_heads(v2)).astype(bf))
    return probs, mixed


def attend_back(q2, k2, v2, w, do2):
    do_bd = split_heads(do2)
    dv = nn(w, do_bd)
    dp = nt(v2, do_bd)
    pf = w.astype(f32)
    pd = pf * dp
    inner = jnp.sum(pd, axis=0, keepdims=True)
    draw = ((pd - pf * inner) * SCALE).astype(bf)
    dq = tn(stack_lanes(draw), split_heads(k2))
    dk = nn(draw, split_heads(q2))
    return dq.astype(bf), dk.astype(bf), dv.astype(bf)


def gelu(t):
    return t * (0.5 + 0.5 * jnp.tanh(t * (GC + (GC * GK) * (t * t))))


def gelu_slope(t):
    t2 = t * t
    s = 0.5 + 0.5 * jnp.tanh(t * (GC + (GC * GK) * t2))
    a = t * s
    return s + (a - a * s) * (2.0 * GC + (6.0 * GC * GK) * t2)


FC = 768


def kernel_d1(wn, dz, g):
    g[...] = tn(wn[...], dz[...]).astype(g.dtype)


def kernel_e(qkv, probs, do, dqkv):
    for rr in range(TILE // SPAN):
        rows = slice(rr * SPAN, (rr + 1) * SPAN)
        for p in range(6):
            cols = slice(p * 128, (p + 1) * 128)
            q2, k2, v2 = (qkv[rows, j * 768 + p * 128 : j * 768 + p * 128 + 128] for j in range(3))
            dq, dk, dv = attend_back(q2, k2, v2, probs[rows, p * 2 * SPAN : (p + 1) * 2 * SPAN], do[rows, cols])
            dqkv[rows, p * 128 : p * 128 + 128] = dq
            dqkv[rows, 768 + p * 128 : 768 + p * 128 + 128] = dk
            dqkv[rows, 1536 + p * 128 : 1536 + p * 128 + 128] = dv


def kernel_f(x, dqkv, dh, gain, w_qkv, dx_out):
    n, r = moments(x[...].astype(f32))
    du = nt(dqkv[...], w_qkv[...])
    dx_out[...] = (dh[...] + norm_back(du, n, r, gain[...])).astype(bf)


def whole(shape):
    return pl.BlockSpec(shape, lambda i: (0,) * len(shape), pipeline_mode=pl.Buffered(1))


def rows_of(cols, tile=TILE):
    return pl.BlockSpec((tile, cols), lambda i: (i, 0))


def call(body, name, grid, in_specs, out_specs, out_shape, flops, nbytes, scratch=()):
    return pl.pallas_call(
        body,
        name=name,
        grid=grid,
        in_specs=in_specs,
        out_specs=out_specs,
        out_shape=out_shape,
        scratch_shapes=scratch,
        cost_estimate=pl.CostEstimate(flops=flops, bytes_accessed=nbytes, transcendentals=0),
        compiler_params=pltpu.CompilerParams(vmem_limit_bytes=VMEM),
    )


def sds(*shape, dtype=bf):
    return jax.ShapeDtypeStruct(shape, dtype)


def weight_grad(left, right, name, tile, out=bf, by="right"):
    T, M = left.shape
    N = right.shape[1]
    if by == "right":
        ins = [whole((T, M)), pl.BlockSpec((T, tile), lambda i: (0, i))]
        outs = pl.BlockSpec((M, tile), lambda i: (0, i))
        grid = (N // tile,)
    else:
        ins = [pl.BlockSpec((T, tile), lambda i: (0, i)), whole((T, N))]
        outs = pl.BlockSpec((tile, N), lambda i: (i, 0))
        grid = (M // tile,)
    return call(kernel_d1, name, grid, ins, outs, sds(M, N, dtype=out), 2 * T * M * N, 2 * (T * M + T * N + M * N))(left, right)


def attention_back(qkv, probs, do):
    T, D = do.shape
    return call(
        kernel_e, "attention_backward", (T // TILE,),
        [rows_of(3 * D), rows_of(2 * D), rows_of(D)],
        rows_of(3 * D), sds(T, 3 * D), 8 * T * D * D, 30 << 20,
    )(qkv, probs, do)


def input_grad(x, dqkv, dh, g1, w_qkv):
    T, D = x.shape
    return call(
        kernel_f, "input_grad", (T // TILE,),
        [rows_of(D), rows_of(3 * D), rows_of(D), whole((1, D)), whole(w_qkv.shape)],
        rows_of(D), sds(T, D),
        6 * T * D * D, 30 << 20,
    )(x, dqkv, dh, g1, w_qkv)


MESH = pl.DeviceIdType.MESH
D_MODEL = 768
P_B = 3
BACK = 256
EARLY = 6
MESSAGES = {
    "x0s": (0, 2, 0, "mine", None), "y0s": (0, 4, 0, "mine", None), "x0c": (0, 2, 0, "middle", None), "y0c": (0, 4, 0, "middle", None),
    "c0": (0, 1, 0, "all", None),
    "xf": (0, 4, 2, "mine", "x0s"), "xz": (1, 0, 2, "mine", "x0s"), "xcs": (0, 1, 2, "mine", "x0s"),
    "yz": (1, 0, 4, "mine", "y0s"), "ycs": (0, 1, 4, "mine", "y0s"),
    "xcc": (0, 1, 2, "middle", "x0c"), "yf": (0, 2, 4, "middle", "y0c"), "ycc": (0, 1, 4, "middle", "y0c"),
    "dz": (1, 0, 6, "mine", "xf"), "dcs": (0, 1, 6, "mine", "xf"), "dcc": (0, 1, 6, "middle", "yf"),
    "xcm": (0, 1, 2, "other", "xz"), "ycm": (0, 1, 4, "other", "yz"), "dcm": (0, 1, 6, "other", "dz"),
}
ARRIVALS = [None, "x0s", "y0s", "x0c", "y0c", "xf", "yf", "xz", "yz", "dz"]
RELAYS = {
    0: [0, 10, 1, 2, 20, 3, 4, 11, 12, 13, 14, 7, 21, 5, 8, 30, 23, 22, 17, 6, 24, 18, 16, 15, 40, 27, 31, 25, 9, 33, 32, 50, 28, 26, 34, 19],
    1: [41, 42, 37, 43, 44, 29, 60, 70],
    2: [51, 35, 38, 53, 52, 36, 54, 80],
    3: [47, 45, 46, 48, 62, 61, 64, 63, 90],
    4: [57, 72, 71, 100, 39, 74],
    5: [73, 58, 55, 56],
    6: [49, 82, 81, 68, 110, 84, 83],
    7: [67, 65, 66],
    8: [78, 92, 91, 77, 94],
    9: [93, 59, 75, 101],
    10: [88, 102, 103, 87],
    11: [104, 76, 69, 85, 111],
    12: [98, 112, 113, 97, 114, 86],
    13: [79, 95, 96, 107, 105, 106],
    14: [108, 115, 89, 116],
    15: [117, 118],
    16: [99, 109],
    17: [119],
}


class Gather:
    def __init__(self, shard, piece, send, recv, local, me, rep):
        self.shard, self.piece, self.send, self.recv, self.me, self.rep = shard, piece, send, recv, me, rep
        self.own = pltpu.make_async_copy(shard, piece(me), local)

    def copy(self, name):
        rep_to, me_to, whose, what, _ = MESSAGES[name]
        s = ARRIVALS.index(name) if name in ARRIVALS else 0
        third = D_MODEL // 3
        parity = self.rep % 2
        cols = {
            "all": lambda: pl.ds(0, D_MODEL),
            "mine": lambda: pl.ds(pl.multiple_of(parity * 2 * third, 128), third),
            "middle": lambda: pl.ds(third, third),
            "other": lambda: pl.ds(pl.multiple_of((1 - parity) * 2 * third, 128), third),
        }[what]()
        piece = self.piece(self.me ^ whose)
        src = self.shard if whose == 0 else piece
        return pltpu.make_async_remote_copy(
            src_ref=src.at[:, cols], dst_ref=piece.at[:, cols], send_sem=self.send, recv_sem=self.recv.at[s],
            device_id=(self.rep ^ rep_to, self.me ^ me_to), device_id_type=MESH,
        )

    def relay(self, arrival):
        if arrival is None:
            self.own.start()
        else:
            self.copy(arrival).wait_recv()
        for name, message in MESSAGES.items():
            if message[4] == arrival:
                self.copy(name).start()

    def complete(self):
        self.own.wait()
        four = self.piece(pl.ds(0, 4))
        pltpu.make_async_copy(four, four, self.recv.at[0]).wait()

    def finish(self):
        seven = self.piece(pl.ds(0, 7))
        pltpu.make_async_copy(seven, seven, self.send).wait()


class Local:
    def __init__(self, shard, place, local):
        self.own = pltpu.make_async_copy(shard, place, local)

    def relay(self, arrival):
        if arrival is None:
            self.own.start()

    def complete(self):
        self.own.wait()

    def finish(self):
        pass


def dispatch(step, table):
    keys = sorted(table)
    if len(keys) < 4:
        for k in keys:
            pl.when(step == k)(table[k])
    else:
        middle = keys[len(keys) // 2]
        pl.when(step < middle)(lambda: dispatch(step, {k: table[k] for k in keys if k < middle}))
        pl.when(step >= middle)(lambda: dispatch(step, {k: table[k] for k in keys if k >= middle}))


def flat(t):
    return t.reshape(t.shape[0] * t.shape[1], t.shape[2])


def gain_rows(ga, gm):
    n = ga.shape[1]
    row = lax.broadcasted_iota(jnp.int32, (16, n), 0)
    pair = jnp.where(row == 0, ga.astype(f32), jnp.where(row == 1, gm.astype(f32), 0.0))
    return jnp.concatenate([pair, jnp.zeros((16, 128 - n), f32)], axis=1).astype(bf)


def spread(pieces):
    width = D_MODEL // 8
    lane = lax.broadcasted_iota(jnp.int32, (128, D_MODEL), 0)
    place = lax.broadcasted_iota(jnp.int32, (128, D_MODEL), 1)
    total = jnp.zeros((16, D_MODEL), f32)
    for d in range(8):
        hit = (place == lane + d * width) & (lane < width)
        total = total + nn(pieces[d], jnp.where(hit, 1.0, 0.0).astype(bf))
    return total[:8]


def kernel_one(
    remote, lengths, x, dy, ga, gm, q_in, o_in, i_in, t_in,
    qkv_out, probs_out, u_out, h_out, wn_out, za_out, dh_out, do_out, gains_out, gwo_out, wq_out, wt_out,
    wq, wo, wi, wt, gain_piece, gain_parts, gains, high, low, qa, zs, mixed_all, wn, send, recv, gain_send, gain_recv, local, out_sem, a_sem, dz_sem,
):
    step = pl.program_id(0)
    T, D = high.shape
    tiles = T // TILE
    p_h = P_B + tiles
    p_in, p_back = p_h + 2, p_h + 10
    steps = p_back + T // BACK
    me, rep = lax.axis_index("fsdp"), lax.axis_index("rep")
    part = lambda j: pl.ds(j * D, D)
    rows_of_part = lambda j: pl.ds(j * 96, 96)
    if remote:
        refs = [(q_in.at[:, part(j)], lambda p, j=j: wq.at[j, p]) for j in range(3)]
        refs += [(o_in, lambda p: wo.at[p])]
        refs += [(i_in.at[:, part(j)], lambda p, j=j: wi.at[j, p]) for j in range(4)]
        refs += [(t_in.at[rows_of_part(j)], lambda p, j=j: wt.at[p, rows_of_part(j)]) for j in range(4)]
        blocks = [Gather(s, f, send.at[k], recv.at[k], local.at[k], me, rep) for k, (s, f) in enumerate(refs)]
    else:
        refs = [(q_in.at[:, :, part(j)], wq.at[j]) for j in range(3)] + [(o_in, wo)]
        refs += [(i_in.at[:, :, part(j)], wi.at[j]) for j in range(4)]
        refs += [(t_in.at[:, rows_of_part(j)], wt.at[:, rows_of_part(j)]) for j in range(4)]
        blocks = [Local(s, f, local.at[k]) for k, (s, f) in enumerate(refs)]

    def gain_copy(d):
        return pltpu.make_async_remote_copy(
            src_ref=gain_piece, dst_ref=gain_parts.at[me], send_sem=gain_send.at[d], recv_sem=gain_recv.at[d],
            device_id=(rep, me ^ d), device_id_type=MESH,
        )

    load_x = pltpu.make_async_copy(x, high, local.at[13])
    export = pltpu.make_async_copy(wq, wq_out, out_sem.at[0])
    store_u = pltpu.make_async_copy(low, u_out, out_sem.at[1])
    store_wn = pltpu.make_async_copy(wn, wn_out, out_sem.at[2])
    store_h = [pltpu.make_async_copy(v, h_out.at[k], out_sem.at[7 + k]) for k, v in enumerate((high, low))]
    export_wt = pltpu.make_async_copy(wt, wt_out, out_sem.at[9])
    store_gwo = pltpu.make_async_copy(mixed_all.at[pl.ds(0, D)], gwo_out, out_sem.at[3])

    def store_qkv(j):
        cols = pl.ds(pl.multiple_of(j * D, D), D)
        return pltpu.make_async_copy(qa.at[:, cols], qkv_out.at[:, cols], out_sem.at[4 + j])

    def rows_at(t, n):
        return pl.ds(pl.multiple_of(t * n, n), n)

    def store_a(e):
        place = (rows_at(lax.rem(e, 2), T // 2), pl.ds(pl.multiple_of(lax.div(e, 2) * FC, FC), FC))
        return pltpu.make_async_copy(qa.at[place], za_out.at[(1, *place)], a_sem.at[e])

    def store_dz(t):
        return pltpu.make_async_copy(zs.at[rows_at(t, BACK)], za_out.at[0, rows_at(t, BACK)], dz_sem.at[t])

    def relay(code):
        blocks[code // 10].relay(ARRIVALS[code % 10])

    @pl.when(step == 0)
    def _():
        load_x.start()
        if remote:
            gain_piece[...] = gain_rows(ga[...], gm[...])
            barrier = pltpu.get_barrier_semaphore()
            for d in range(1, 8):
                pl.semaphore_signal(barrier, inc=1, device_id=(rep, me ^ d), device_id_type=MESH)
            pl.semaphore_signal(barrier, inc=1, device_id=(rep ^ 1, me), device_id_type=MESH)
            pl.semaphore_wait(barrier, 8)
            for d in range(1, 8):
                gain_copy(d).start()
        for code in RELAYS[0][:EARLY]:
            relay(code)
        if remote:
            gain_parts[me] = gain_piece[...]
            for d in range(1, 8):
                gain_copy(d).wait_recv()
        else:
            for d in range(8):
                gain_parts[d] = gain_rows(ga[d : d + 1], gm[d : d + 1])
        gains[...] = spread(gain_parts)
        gains_out[...] = gains[...]
        load_x.wait()
        later = RELAYS[0][EARLY:]
        for t in range(max(tiles, len(later))):
            if t < tiles:
                rows = pl.ds(t * TILE, TILE)
                n, _ = moments(high[rows, :].astype(f32))
                low[rows, :] = (n * gains[0:1]).astype(bf)
            if t < len(later):
                relay(later[t])
        store_u.start()
        blocks[0].complete()

    completes = {1: [1], 2: [2], p_h: [3], p_back: [8, 9, 10, 11]}
    completes.update({p_in + 2 * j: [4 + j] for j in range(4)})

    def begin(at):
        for code in RELAYS.get(at, []):
            relay(code)
        for k in completes.get(at, []):
            blocks[k].complete()
        if at == P_B:
            export.start()
        if at == p_h:
            store_u.wait()
        if at == p_back:
            export_wt.start()
            for store in store_h:
                store.wait()
        if at == p_in:
            store_wn.start()
            for store in store_h:
                store.start()
            for j in range(3):
                store_qkv(j).wait()

    dispatch(step, {at: functools.partial(begin, at) for at in {*RELAYS, *completes, P_B} - {0}})

    @pl.when(step < P_B)
    def _():
        w = flat(wq[step])
        block = 2 * TILE
        cols = pl.ds(pl.multiple_of(step * D, D), D)
        for t in range(T // block):
            qa[t * block : (t + 1) * block, cols] = nn(low[t * block : (t + 1) * block], w).astype(bf)
        store_qkv(step).start()

    @pl.when((step >= P_B) & (step < p_h))
    def _():
        t = step - P_B
        for rr in range(TILE // SPAN):
            rows = pl.ds(pl.multiple_of(t * TILE + rr * SPAN, SPAN), SPAN)
            mask = permitted(lengths, t * (TILE // SPAN) + rr)
            probs, mixed = attend(lambda c: qa[rows, c : c + 128], mask)
            for p in range(6):
                probs_out[rr * SPAN : (rr + 1) * SPAN, p * 2 * SPAN : (p + 1) * 2 * SPAN] = probs[p]
                mixed_all[rows, p * 128 : (p + 1) * 128] = mixed[p]

    @pl.when((step >= p_h) & (step < p_in))
    def _():
        for s in range(tiles // 2):
            rows = rows_at((step - p_h) * (tiles // 2) + s, TILE)
            h = high[rows, :].astype(f32) + nn(mixed_all[rows, :], flat(wo[...]))
            top = h.astype(bf)
            high[rows, :] = top
            low[rows, :] = (h - top.astype(f32)).astype(bf)
            n, _ = moments(h)
            wn[rows, :] = (n * gains[1:2]).astype(bf)

    @pl.when((step >= p_in) & (step < p_back))
    def _():
        e = step - p_in
        j, half = lax.div(e, 2), lax.rem(e, 2)
        cols = pl.ds(pl.multiple_of(j * FC, FC), FC)
        w = flat(wi[j])
        block = TILE
        for s in range(T // 2 // block):
            rows = rows_at(half * (T // 2 // block) + s, block)
            z = nn(wn[rows, :], w)
            qa[rows, cols] = gelu(z).astype(bf)
            zs[rows, cols] = z.astype(bf)
        store_a(e).start()

    per = FC // wt.shape[1]

    @pl.when(step >= p_back)
    def _():
        t = step - p_back
        rows = rows_at(t, BACK)
        h = high[rows, :].astype(f32) + low[rows, :].astype(f32)
        n, r = moments(h)
        dm = dy[...]
        dw = None
        for j in range(wi.shape[0]):
            cols = slice(j * FC, (j + 1) * FC)
            w_out = flat(wt[j * per : (j + 1) * per])
            dz = (nt(dm, w_out) * gelu_slope(zs[rows, cols].astype(f32))).astype(bf)
            zs[rows, cols] = dz
            add = nt(dz, flat(wi[j]))
            dw = add if dw is None else dw + add
        store_dz(t).start()
        dt = (dm.astype(f32) + norm_back(dw, n, r, gains[1:2])).astype(bf)
        dh_out[...] = dt
        high[rows, :] = dt
        do_out[...] = nt(dt, flat(wo[...])).astype(bf)

    @pl.when(step == steps - 1)
    def _():
        gwo = tn(mixed_all[...], high[...]).astype(bf)
        mixed_all[0:D, :] = gwo
        store_gwo.start()
        export.wait()
        export_wt.wait()
        store_wn.wait()
        for t in range(8):
            store_a(t).wait()
        for t in range(T // BACK):
            store_dz(t).wait()
        if remote:
            for d in range(1, 8):
                gain_copy(d).wait_send()
        for b in blocks:
            b.finish()
        store_gwo.wait()


def forward_and_mlp(remote, x, lengths, dy, ga, gm, w_qkv, w_ao, w_in, w_out):
    T, D = x.shape
    tiles = T // TILE
    F = w_in.shape[-1]
    rows = D // 8

    def tile_from(start, *shape):
        return pl.BlockSpec(shape, lambda i: (jnp.clip(i - start, 0, tiles - 1),) + (0,) * (len(shape) - 1))

    p_back = P_B + tiles + 10
    back_rows = pl.BlockSpec((BACK, D), lambda i: (jnp.clip(i - p_back, 0, T // BACK - 1), 0))
    whole = pl.BlockSpec(ga.shape, lambda i: (0, 0))
    hbm = pl.BlockSpec(memory_space=pl.ANY)

    return pl.pallas_call(
        functools.partial(kernel_one, remote),
        name="forward_and_mlp",
        grid=(p_back + T // BACK,),
        in_specs=[pl.BlockSpec(memory_space=pltpu.SMEM), hbm, back_rows, whole, whole, hbm, hbm, hbm, hbm],
        out_specs=[
            hbm, tile_from(P_B, TILE, 2 * D), hbm, hbm, hbm, hbm,
            back_rows, back_rows, pl.BlockSpec((8, D), lambda i: (0, 0)), hbm, hbm, hbm,
        ],
        out_shape=[
            sds(T, 3 * D), sds(T, 2 * D), sds(T, D),
            sds(2, T, D), sds(T, D), sds(2, T, F), sds(T, D), sds(T, D), sds(8, D, dtype=f32), sds(D, D), sds(3, 8, rows, D), sds(8, F // 8, D),
        ],
        scratch_shapes=[
            pltpu.VMEM((3, 8, rows, D), bf), pltpu.VMEM((8, rows, D), bf), pltpu.VMEM((F // FC, 8, rows, FC), bf),
            pltpu.VMEM((8, F // 8, D), bf), pltpu.VMEM((16, 128), bf), pltpu.VMEM((8, 16, 128), bf), pltpu.VMEM((8, D), f32), pltpu.VMEM((T, D), bf),
            pltpu.VMEM((T, D), bf), pltpu.VMEM((T, F), bf), pltpu.VMEM((T, F), bf), pltpu.VMEM((T, D), bf), pltpu.VMEM((T, D), bf),
            pltpu.SemaphoreType.DMA((12,)), pltpu.SemaphoreType.DMA((12, len(ARRIVALS))), pltpu.SemaphoreType.DMA((8,)), pltpu.SemaphoreType.DMA((8,)),
            pltpu.SemaphoreType.DMA((14,)), pltpu.SemaphoreType.DMA((10,)), pltpu.SemaphoreType.DMA((tiles,)), pltpu.SemaphoreType.DMA((tiles,)),
        ],
        cost_estimate=pl.CostEstimate(flops=12 * T * D * D + 8 * T * D * F + 6 * T * D * D, bytes_accessed=90 << 20, transcendentals=0),
        compiler_params=pltpu.CompilerParams(
            vmem_limit_bytes=VMEM, has_side_effects=remote, collective_id=1 if remote else None
        ),
    )(lengths.T, x, dy, ga, gm, w_qkv, w_ao, w_in, w_out)


CHUNK = 96
WIDE = 768
RING = 6
N_WIDE = 12
P_IN, P_OUT, P_ATT = 0, 4, 8
P_DX = P_ATT + 9
P_Y = P_DX + 4
STEPS = P_Y + 4
BLOCK = 512
REUSE = {P_ATT + 5: [0], P_ATT + 8: [1], P_DX + 2: [2, 3, 4, 5]}
START = [
    [1, 2, 5, 7, 9, 13, 15], [1, 3, 6, 11, 13, 15, 25], [2, 4, 6, 8, 10, 13, 16], [3, 6, 9, 10, 12, 14, 28],
    [5, 8, 10, 12, 14, 16, 23], [8, 9, 11, 13, 15, 16, 23], [8, 10, 13, 15, 16, 18, 22], [8, 13, 15, 16, 18, 20, 30],
    [11, 12, 15, 17, 19, 21, 25], [12, 13, 16, 18, 20, 22, 32], [12, 14, 16, 18, 20, 22, 24], [14, 15, 18, 19, 21, 23, 26],
    [14, 16, 19, 20, 22, 23, 27], [17, 18, 20, 21, 23, 24, 29], [17, 19, 21, 22, 23, 24, 27],
]
RECEIVE = {"s1": 0, "s2x": 1, "s2y": 1, "s3y": 2, "s3x": 2, "z1": 3, "z2": 4, "z3": 3}


def slot_of(k):
    return k if k < 10 else k - 10


class Reduce:
    def __init__(self, n, grads, bufs, send, recv, place):
        self.n = n
        k = n if n < 9 else 9 + (n - 9) // 2
        cols = pl.ds(0, WIDE) if n < 9 else pl.ds((n - 9) % 2 * (WIDE // 2), WIDE // 2)
        first, x2, y2, y3, x3, outer, inner, out = bufs
        r = k % RING
        self.g = grads.at[slot_of(k), :, :, :, :, cols]
        self.first = first.at[r, :, :, :, cols]
        self.x2, self.y2 = x2.at[r, :, :, cols], y2.at[r, :, :, cols]
        self.x3, self.y3 = x3.at[k, :, cols], y3.at[k, :, cols]
        self.outer, self.inner, self.out = outer.at[k, :, cols], inner.at[k, :, cols], out.at[k, :, cols]
        self.send, self.recv = send, recv
        self.y, self.x, self.c, self.me, self.rep = place
        self.is_inner = (self.rep == 1) | (self.rep == 2)

    def copy(self, m):
        g, y, x, c = self.g, self.y, self.x, self.c
        upper, lower = pl.ds(0, CHUNK // 2), pl.ds(CHUNK // 2, CHUNK // 2)
        src, dst, rep_to, me_to = {
            "s1": lambda: (g.at[:, :, 1 - c], self.first, 0, 1),
            "s2x": lambda: (g.at[:, 1 - x, c, upper], self.x2, 0, 2),
            "s2y": lambda: (g.at[1 - y, :, c, lower], self.y2, 0, 4),
            "s3y": lambda: (g.at[1 - y, x, c, upper], self.y3, 0, 4),
            "s3x": lambda: (g.at[y, 1 - x, c, lower], self.x3, 0, 2),
            "z1": lambda: (g.at[y, x, c], self.outer, 1, 0),
            "z2": lambda: (g.at[y, x, c], self.inner, 3, 0),
            "z3": lambda: (self.out, self.out, 1, 0),
        }[m]()
        return pltpu.make_async_remote_copy(
            src_ref=src, dst_ref=dst, send_sem=self.send.at[self.n, int(m == "z3")], recv_sem=self.recv.at[self.n, RECEIVE[m]],
            device_id=(self.rep ^ rep_to, self.me ^ me_to), device_id_type=MESH,
        )

    def start(self, *names):
        for m in names:
            self.copy(m).start()

    def arrived(self, m, ref):
        pltpu.make_async_copy(ref, ref, self.recv.at[self.n, RECEIVE[m]]).wait()

    def stage(self, s):
        g, y, x, c = self.g, self.y, self.x, self.c
        upper, lower = pl.ds(0, CHUNK // 2), pl.ds(CHUNK // 2, CHUNK // 2)
        if s == 1:
            self.start("s1")
        elif s == 2:
            self.arrived("s1", self.first)
            for b in range(2):
                for a in range(2):
                    g[b, a, c] += self.first[b, a]
            self.start("s2x", "s2y")
        elif s == 3:
            self.arrived("s2x", g.at[0, 0])
            for b in range(2):
                g[b, x, c, upper] += self.x2[b]
                g[y, b, c, lower] += self.y2[b]
            self.start("s3y", "s3x")
        elif s == 4:
            self.arrived("s3y", g.at[0, 0, 0])
            g[y, x, c, upper] += self.y3[...]
            g[y, x, c, lower] += self.x3[...]

            @pl.when(jnp.logical_not(self.is_inner))
            def _():
                self.start("z1")
        elif s == 5:
            @pl.when(self.is_inner)
            def _():
                self.arrived("z1", self.outer)
                g[y, x, c] += self.outer[...]
                self.start("z2")
        elif s == 6:
            @pl.when(self.is_inner)
            def _():
                self.arrived("z2", self.inner)
                self.out[...] = g[y, x, c] + self.inner[...]
                self.start("z3")
        elif s == 7:
            @pl.when(jnp.logical_not(self.is_inner))
            def _():
                self.arrived("z3", self.out)

    def sent(self):
        pltpu.make_async_copy(self.g, self.g, self.send.at[self.n, 0]).wait()

    def sum_sent(self):
        @pl.when(self.is_inner)
        def _():
            pltpu.make_async_copy(self.out, self.out, self.send.at[self.n, 1]).wait()


def part_of(e):
    return 2 * lax.div(e, 3) + jnp.minimum(lax.rem(e, 3), 1), lax.rem(e, 3) == 2


def kernel_two(
    gwo_in, wn, dm, u, wq, wt, gains, za, qkv, probs, do, x, dh, h,
    dx_out, y_out, out_hbm,
    out, big_a, big_b, wq_s, dqkv, grads, first, x2, y2, y3, x3, outer, inner, stream, halves, result,
    send, recv, local, load_sem, store_sem,
):
    step = pl.program_id(0)
    T, D = big_a.shape
    me, rep = lax.axis_index("fsdp"), lax.axis_index("rep")
    place = (me // 4, (me // 2) % 2, me % 2, me, rep)
    bufs = (first, x2, y2, y3, x3, outer, inner, out)
    chunks = [Reduce(n, grads, bufs, send, recv, place) for n in range(len(START))]
    load_gwo = pltpu.make_async_copy(gwo_in, grads.at[0], local.at[0])
    load_wn = pltpu.make_async_copy(wn, big_a, local.at[1])
    load_dm = pltpu.make_async_copy(dm, big_b, local.at[2])
    load_u = pltpu.make_async_copy(u, big_a, local.at[3])
    load_wq = pltpu.make_async_copy(wq, wq_s, local.at[4])
    store_out = pltpu.make_async_copy(out, out_hbm, local.at[5])
    load_wt = pltpu.make_async_copy(wt, grads.at[pl.ds(2, 4)], local.at[6])

    def loads(at):
        s = at % 2
        to = stream.at[s]
        if at < P_ATT:
            pairs = [(za.at[at // 4, :, pl.ds(at % 4 * WIDE, WIDE)], to)]
        elif at < P_DX:
            e = at - P_ATT
            if e % 3 == 2:
                return []
            p = e // 3 * 2 + e % 3
            pairs = [(qkv.at[:, pl.ds(j * D + p * 128, 128)], to.at[:, pl.ds(j * 128, 128)]) for j in range(3)]
            pairs.append((do.at[:, pl.ds(p * 128, 128)], to.at[:, pl.ds(384, 128)]))
            pairs.append((probs.at[:, pl.ds(p * 256, 256)], to.at[:, pl.ds(512, 256)]))
        elif at < P_Y:
            rows = pl.ds((at - P_DX) * BLOCK, BLOCK)
            pairs = [(x.at[rows], to.at[pl.ds(0, BLOCK)]), (dh.at[rows], to.at[pl.ds(BLOCK, BLOCK)])]
        else:
            rows = pl.ds((at - P_Y) * BLOCK, BLOCK)
            pairs = [(za.at[1, rows, pl.ds(j * WIDE, WIDE)], to.at[pl.ds(j * BLOCK, BLOCK)]) for j in range(4)]
            pairs.append((h.at[:, rows], halves.at[s]))
        return [pltpu.make_async_copy(src, dst, load_sem.at[s, k]) for k, (src, dst) in enumerate(pairs)]

    def store(at):
        to, t = (dx_out, at - P_DX) if at < P_Y else (y_out, at - P_Y)
        return pltpu.make_async_copy(result.at[at % 2], to.at[pl.ds(t * BLOCK, BLOCK)], store_sem.at[at % 2])

    acts = {}
    for n, starts in enumerate(START):
        for s, at in enumerate(starts):
            acts.setdefault(at, []).append((n, s + 1))

    def act(at):
        for n, s in sorted(acts[at], key=lambda ns: -ns[1]):
            chunks[n].stage(s)

    def begin(at):
        if at == 0:
            load_wn.start()
            for load in loads(0):
                load.start()
            barrier = pltpu.get_barrier_semaphore()
            for to in ((rep, me ^ 1), (rep, me ^ 2), (rep, me ^ 4), (rep ^ 1, me), (rep ^ 3, me)):
                pl.semaphore_signal(barrier, inc=1, device_id=to, device_id_type=MESH)
            pl.semaphore_wait(barrier, 5)
            load_wn.wait()
        for load in loads(at):
            load.wait()
        if at == 0:
            load_gwo.start()
        if at + 1 < STEPS:
            for load in loads(at + 1):
                load.start()
        if at == 1:
            load_dm.start()
            load_gwo.wait()
        if at in acts:
            act(at)
        if at == P_OUT:
            load_u.start()
            load_dm.wait()
        if at == P_OUT + 1:
            load_wq.start()
        if at == P_ATT + 2:
            load_u.wait()
            load_wq.wait()
        for k in REUSE.get(at, []):
            chunks[k].sent()
        if at == P_DX + 2:
            load_wt.start()
        if at == P_Y:
            load_wt.wait()
        if at >= P_DX + 2:
            store(at - 2).wait()

    dispatch(step, {at: functools.partial(begin, at) for at in range(STEPS)})

    slot = lax.rem(step, 2)

    @pl.when(step < P_OUT)
    def _():
        g = tn(big_a[...], stream[slot]).astype(bf)
        grads[1 + step] = g.reshape(2, 2, 2, CHUNK, WIDE)

    @pl.when((step >= P_OUT) & (step < P_ATT))
    def _():
        j = step - P_OUT
        g = tn(stream[slot], big_b[...]).astype(bf).reshape(2, 4, CHUNK, WIDE)
        for part in range(4):
            grads[5 + part, j // 2, j % 2] = g[:, part]

    pair, product = part_of(step - P_ATT)
    attention = (step >= P_ATT) & (step < P_DX)

    @pl.when(attention & jnp.logical_not(product))
    def _():
        for rr in range(T // SPAN):
            rows = slice(rr * SPAN, (rr + 1) * SPAN)
            q2, k2, v2, do2 = (stream[slot, rows, j * 128 : (j + 1) * 128] for j in range(4))
            back = attend_back(q2, k2, v2, stream[slot, rows, 512:768], do2)
            for j in range(3):
                to_cols = pl.ds(pl.multiple_of(lax.rem(pair, 2) * (WIDE // 2) + j * 128, 128), 128)
                dqkv[lax.div(pair, 2), rows, to_cols] = back[j]

    @pl.when(attention & product)
    def _():
        k = lax.div(pair, 2)
        g = tn(big_a[...], dqkv[k]).astype(bf)
        grads[jnp.where(k == 0, 9, k - 1)] = g.reshape(2, 2, 2, CHUNK, WIDE)

    @pl.when((step >= P_DX) & (step < P_Y))
    def _():
        for part in range(BLOCK // TILE):
            here = slice(part * TILE, (part + 1) * TILE)
            rows = pl.ds(pl.multiple_of((step - P_DX) * BLOCK + part * TILE, TILE), TILE)
            n, r = moments(stream[slot, here].astype(f32))
            du = 0.0
            for j in range(3):
                at = [(p // 2, (p % 2) * (WIDE // 2) + j * 128) for p in range(D // 128)]
                du = du + nt(jnp.concatenate([dqkv[k, rows, c : c + 128] for k, c in at], axis=1), flat(wq_s[j]))
            dt = stream[slot, BLOCK + part * TILE : BLOCK + (part + 1) * TILE].astype(f32)
            result[slot, here] = (dt + norm_back(du, n, r, gains[0:1])).astype(bf)
        for at in range(P_DX, P_Y):
            @pl.when(step == at)
            def _(at=at):
                store(at).start()

    @pl.when(step >= P_Y)
    def _():
        y = halves[slot, 0].astype(f32) + halves[slot, 1].astype(f32)
        for j in range(4):
            y = y + nn(stream[slot, j * BLOCK : (j + 1) * BLOCK], grads[2 + j].reshape(WIDE, WIDE))
        result[slot] = y.astype(bf)
        for at in range(P_Y, STEPS):
            @pl.when(step == at)
            def _(at=at):
                store(at).start()

    @pl.when(step == STEPS - 1)
    def _():
        for at in sorted(acts):
            if at >= STEPS:
                act(at)
        store_out.start()
        for n in range(len(START)):
            if n not in sum(REUSE.values(), []):
                chunks[n].sent()
            chunks[n].sum_sent()
        for at in (STEPS - 2, STEPS - 1):
            store(at).wait()
        store_out.wait()


def gradients(gwo, wn, dy, u, wq, wt, gains, za, qkv, probs, do, x, dh, h):
    T, D = x.shape
    hbm = pl.BlockSpec(memory_space=pl.ANY)
    wide = lambda *shape: pltpu.VMEM(shape + (WIDE,), bf)
    return pl.pallas_call(
        kernel_two,
        name="gradients",
        grid=(STEPS,),
        in_specs=[hbm] * 6 + [pl.BlockSpec((8, D), lambda i: (0, 0))] + [hbm] * 7,
        out_specs=[hbm] * 3,
        out_shape=[sds(T, D), sds(T, D), sds(N_WIDE, CHUNK, WIDE)],
        scratch_shapes=[
            wide(N_WIDE, CHUNK), wide(T), wide(T), pltpu.VMEM(wq.shape, bf), wide(3, T),
            wide(10, 2, 2, 2, CHUNK), wide(RING, 2, 2, CHUNK), wide(RING, 2, CHUNK // 2),
            wide(RING, 2, CHUNK // 2), wide(N_WIDE, CHUNK // 2), wide(N_WIDE, CHUNK // 2), wide(N_WIDE, CHUNK), wide(N_WIDE, CHUNK),
            wide(2, T), wide(2, 2, BLOCK), wide(2, BLOCK),
            pltpu.SemaphoreType.DMA((len(START), 2)), pltpu.SemaphoreType.DMA((len(START), 5)), pltpu.SemaphoreType.DMA((7,)),
            pltpu.SemaphoreType.DMA((2, 5)), pltpu.SemaphoreType.DMA((2,)),
        ],
        cost_estimate=pl.CostEstimate(flops=8 * T * D * D + 4 * T * D * 4 * D + 20 * T * D * D, bytes_accessed=90 << 20, transcendentals=0),
        compiler_params=pltpu.CompilerParams(vmem_limit_bytes=VMEM, has_side_effects=True, collective_id=2),
    )(gwo.reshape(2, 2, 2, CHUNK, WIDE), wn, dy, u, wq, wt.reshape(4, 2, 2, 2, CHUNK, WIDE), gains, za, qkv, probs, do, x, dh, h)


def kernel_finish(
    sums_in, wq_in, wi_in, ga, gm, y, dx, y_out, dx_out, gq_out, gwo_out, gwi_out, gwt_out, gg1, gg2,
    hold, sums, wq, wi, gq, gwo, gwi, gwt, sem, load_sem, store_sem,
):
    parts = sem.shape[2]
    n = y.shape[0] // parts
    loads = [pltpu.make_async_copy(src, dst, load_sem.at[k]) for k, (src, dst) in enumerate(((sums_in, sums), (wq_in, wq), (wi_in, wi)))]
    moves = []
    for p in range(parts):
        for k, (src, dst) in enumerate(((y, y_out), (dx, dx_out))):
            rows = pl.ds(p * n, n)
            there = pltpu.make_async_copy(src.at[rows], hold.at[k, rows], sem.at[0, k, p])
            moves.append((there, pltpu.make_async_copy(hold.at[k, rows], dst.at[rows], sem.at[1, k, p])))
    for load in loads:
        load.start()
    for there, _ in moves:
        there.start()
    stores = [pltpu.make_async_copy(src, dst, store_sem.at[k]) for k, (src, dst) in enumerate(((gwt, gwt_out), (gwi, gwi_out), (gq, gq_out), (gwo, gwo_out)))]
    D = gwo.shape[1]
    loads[0].wait()
    for j in range(4):
        gwt[j * CHUNK : (j + 1) * CHUNK, :] = sums[5 + j].astype(f32)
    stores[0].start()
    for j in range(4):
        gwi[:, j * D : (j + 1) * D] = sums[1 + j].astype(f32)
    stores[1].start()
    for pair in range(D // 128):
        for j in range(3):
            cols = (pair % 2) * (WIDE // 2) + j * 128
            gq[:, j * D + pair * 128 : j * D + pair * 128 + 128] = sums[9 + pair // 2, :, cols : cols + 128].astype(f32)
    stores[2].start()
    gwo[...] = sums[0].astype(f32)
    stores[3].start()
    for there, out in moves:
        there.wait()
        out.start()
    loads[1].wait()
    loads[2].wait()
    for grad, w, gain, out in ((gq, wq, ga, gg1), (gwi, wi, gm, gg2)):
        acc = jnp.zeros((CHUNK, 128), f32)
        for c in range(0, w.shape[1], 128):
            acc = acc + w[:, c : c + 128].astype(f32) * grad[:, c : c + 128]
        out[...] = jnp.sum(acc.T, axis=0, keepdims=True) / gain[...].astype(f32)
    for store in stores:
        store.wait()
    for _, out in moves:
        out.wait()


def finish(sums, w_qkv, w_mlp_in, gain_attn, gain_mlp, y, dx):
    rows, D = w_qkv.shape[0], w_qkv.shape[1] // 3
    vmem, hbm = pl.BlockSpec(memory_space=pltpu.VMEM), pl.BlockSpec(memory_space=pl.ANY)
    shapes = [(rows, 3 * D), (rows, D), (rows, 4 * D), (4 * rows, D)]
    fs = functools.partial(sds, dtype=f32)
    y, dx, gq, gwo, gwi, gwt, gg1, gg2 = pl.pallas_call(
        kernel_finish,
        name="finish",
        in_specs=[hbm] * 3 + [vmem] * 2 + [hbm] * 2,
        out_specs=[hbm] * 6 + [vmem] * 2,
        out_shape=[sds(*y.shape), sds(*dx.shape), *(fs(*shape) for shape in shapes), fs(1, rows), fs(1, rows)],
        scratch_shapes=[
            pltpu.VMEM((2, *y.shape), bf), pltpu.VMEM(sums.shape, bf), pltpu.VMEM(w_qkv.shape, bf), pltpu.VMEM(w_mlp_in.shape, bf),
            *(pltpu.VMEM(shape, f32) for shape in shapes),
            pltpu.SemaphoreType.DMA((2, 2, 4)), pltpu.SemaphoreType.DMA((3,)), pltpu.SemaphoreType.DMA((4,)),
        ],
        cost_estimate=pl.CostEstimate(flops=1 << 20, bytes_accessed=20 << 20, transcendentals=0),
        compiler_params=pltpu.CompilerParams(vmem_limit_bytes=VMEM),
    )(sums, w_qkv, w_mlp_in, gain_attn.reshape(1, rows), gain_mlp.reshape(1, rows), y, dx)
    return y, dx, gg1.reshape(rows), gq, gwo, gg2.reshape(rows), gwi, gwt


def shards(x, lengths, segments, gain_attn, w_qkv, w_attn_out, gain_mlp, w_mlp_in, w_mlp_out, dy):
    D = x.shape[1]
    remote = lax.axis_size("fsdp") == 8 and lax.axis_size("rep") == 4
    ga, gm = gain_attn.reshape(1, -1), gain_mlp.reshape(1, -1)
    weights = (w_qkv, w_attn_out, w_mlp_in, w_mlp_out)
    if not remote:
        weights = tuple(lax.all_gather(v, "fsdp", axis=0, tiled=True) for v in weights)
        weights = tuple(v.reshape(8, v.shape[0] // 8, v.shape[1]) for v in weights)
        ga, gm = (lax.all_gather(v, "fsdp", axis=0, tiled=True).reshape(8, -1) for v in (gain_attn, gain_mlp))
    qkv, probs, u, h, wn, za, dh, do, gains, gwo, wq, wt = forward_and_mlp(remote, x, lengths, dy, ga, gm, *weights)
    if remote:
        dx, y, sums = gradients(gwo, wn, dy, u, wq, wt, gains, za, qkv, probs, do, x, dh, h)
        return finish(sums, w_qkv, w_mlp_in, gain_attn, gain_mlp, y, dx)
    scatter = lambda v: lax.psum_scatter(v, "fsdp", scatter_dimension=0, tiled=True)
    gwt = scatter(weight_grad(za[1], dy, "mlp_out_grad", 768, bf, "left"))
    gwi = scatter(weight_grad(wn, za[0], "mlp_in_grad", 768))
    gwo = scatter(gwo)
    dqkv = attention_back(qkv, probs, do)
    gq = scatter(weight_grad(u, dqkv, "qkv_grad", 768))
    dx = input_grad(x, dqkv, dh.astype(f32), gains[0:1], wq.transpose(1, 2, 0, 3).reshape(D, 3 * D))
    y = jnp.sum(h.astype(f32), axis=0) + jnp.dot(za[1], wt.reshape(-1, D), preferred_element_type=f32)
    y = y.astype(bf)
    gwt, gwi, gwo, gq = lax.psum((gwt, gwi, gwo, gq), "rep")
    gwt, gwi, gwo, gq = (v.astype(f32) for v in (gwt, gwi, gwo, gq))
    gg1 = jnp.sum(w_qkv.astype(f32) * gq, axis=1) / gain_attn.astype(f32)
    gg2 = jnp.sum(w_mlp_in.astype(f32) * gwi, axis=1) / gain_mlp.astype(f32)
    return y, dx, gg1, gq, gwo, gg2, gwi, gwt


def solution(mesh):
    tokens, cut, vec = P(("rep", "fsdp"), None), P("fsdp", None), P("fsdp")
    return jax.shard_map(
        shards,
        mesh=mesh,
        in_specs=(tokens, tokens, P(("rep", "fsdp")), vec, cut, cut, vec, cut, cut, tokens),
        out_specs=(tokens, tokens, vec, cut, cut, vec, cut, cut),
        check_vma=False,
    )
```

```python
import functools, math
import jax, jax.numpy as jnp
from jax import lax
from jax.experimental import pallas as pl
from jax.experimental.pallas import tpu as pltpu
from jax.sharding import PartitionSpec as P
bf = jnp.bfloat16
f32 = jnp.float32
EPS = 1e-05
NEG = -1e30
SPAN = 128
TILE = 256
VMEM = 63 * 1024 * 1024
SCALE = 64 ** -0.5
LOG2E = math.log2(math.e)
GC = math.sqrt(2.0 / math.pi)
GK = 0.044715


def nn(a, b):
    return lax.dot_general(a, b, (((1,), (0,)), ((), ())), preferred_element_type=f32)


def nt(a, b):
    return lax.dot_general(a, b, (((1,), (1,)), ((), ())), preferred_element_type=f32)


def tn(a, b):
    return lax.dot_general(a, b, (((0,), (0,)), ((), ())), preferred_element_type=f32)


def moments(v):
    c = v - jnp.mean(v, axis=-1, keepdims=True)
    r = lax.rsqrt(jnp.mean(c * c, axis=-1, keepdims=True) + EPS)
    return c * r, r


def norm_back(e, n, r, g):
    s = e * g
    inner = s - jnp.mean(s, axis=-1, keepdims=True) - n * jnp.mean(s * n, axis=-1, keepdims=True)
    return inner * r


def split_heads(t):
    low = lax.broadcasted_iota(jnp.int32, t.shape, 1) < 64
    zero = jnp.zeros_like(t)
    return jnp.concatenate([jnp.where(low, t, zero), jnp.where(low, zero, t)], axis=0)


def stack_lanes(t):
    return jnp.concatenate([t[:, :SPAN], t[:, SPAN:]], axis=0)


def permitted(lengths, row):
    ends = []
    total = 0
    for k in range(4):
        total = total + lengths[k, row]
        ends.append(total)
    key = lax.broadcasted_iota(jnp.int32, (SPAN, SPAN), 0)
    query = lax.broadcasted_iota(jnp.int32, (SPAN, SPAN), 1)
    one, zero = jnp.int32(1), jnp.int32(0)
    seg_key = sum(jnp.where(key >= e, one, zero) for e in ends)
    seg_query = sum(jnp.where(query >= e, one, zero) for e in ends)
    return (seg_key == seg_query) & ((key < total) | (key == query))


def attend(qkv, mask):
    mask2 = jnp.concatenate([mask, mask], axis=1)
    probs, mixed = [], []
    for p in range(6):
        q2, k2, v2 = qkv(p * 128), qkv(768 + p * 128), qkv(1536 + p * 128)
        s = jnp.where(mask2, nt(k2, split_heads(q2)), NEG)
        top = jnp.max(s, axis=0, keepdims=True)
        e = jnp.exp2((s - top) * (SCALE * LOG2E))
        w = (e * (1.0 / jnp.sum(e, axis=0, keepdims=True))).astype(bf)
        probs.append(w)
        mixed.append(tn(stack_lanes(w), split_heads(v2)).astype(bf))
    return probs, mixed


def attend_back(q2, k2, v2, w, do2):
    do_bd = split_heads(do2)
    dv = nn(w, do_bd)
    dp = nt(v2, do_bd)
    pf = w.astype(f32)
    pd = pf * dp
    inner = jnp.sum(pd, axis=0, keepdims=True)
    draw = ((pd - pf * inner) * SCALE).astype(bf)
    dq = tn(stack_lanes(draw), split_heads(k2))
    dk = nn(draw, split_heads(q2))
    return dq.astype(bf), dk.astype(bf), dv.astype(bf)


def gelu(t):
    return t * (0.5 + 0.5 * jnp.tanh(t * (GC + (GC * GK) * (t * t))))


def gelu_slope(t):
    t2 = t * t
    s = 0.5 + 0.5 * jnp.tanh(t * (GC + (GC * GK) * t2))
    a = t * s
    return s + (a - a * s) * (2.0 * GC + (6.0 * GC * GK) * t2)


FC = 768


def kernel_d1(wn, dz, g):
    g[...] = tn(wn[...], dz[...]).astype(g.dtype)


def kernel_e(qkv, probs, do, dqkv):
    for rr in range(TILE // SPAN):
        rows = slice(rr * SPAN, (rr + 1) * SPAN)
        for p in range(6):
            cols = slice(p * 128, (p + 1) * 128)
            q2, k2, v2 = (qkv[rows, j * 768 + p * 128 : j * 768 + p * 128 + 128] for j in range(3))
            dq, dk, dv = attend_back(q2, k2, v2, probs[rows, p * 2 * SPAN : (p + 1) * 2 * SPAN], do[rows, cols])
            dqkv[rows, p * 128 : p * 128 + 128] = dq
            dqkv[rows, 768 + p * 128 : 768 + p * 128 + 128] = dk
            dqkv[rows, 1536 + p * 128 : 1536 + p * 128 + 128] = dv


def kernel_f(x, dqkv, dh, gain, w_qkv, dx_out):
    n, r = moments(x[...].astype(f32))
    du = nt(dqkv[...], w_qkv[...])
    dx_out[...] = (dh[...] + norm_back(du, n, r, gain[...])).astype(bf)


def whole(shape):
    return pl.BlockSpec(shape, lambda i: (0,) * len(shape), pipeline_mode=pl.Buffered(1))


def rows_of(cols, tile=TILE):
    return pl.BlockSpec((tile, cols), lambda i: (i, 0))


def call(body, name, grid, in_specs, out_specs, out_shape, flops, nbytes, scratch=()):
    return pl.pallas_call(
        body,
        name=name,
        grid=grid,
        in_specs=in_specs,
        out_specs=out_specs,
        out_shape=out_shape,
        scratch_shapes=scratch,
        cost_estimate=pl.CostEstimate(flops=flops, bytes_accessed=nbytes, transcendentals=0),
        compiler_params=pltpu.CompilerParams(vmem_limit_bytes=VMEM),
    )


def sds(*shape, dtype=bf):
    return jax.ShapeDtypeStruct(shape, dtype)


def weight_grad(left, right, name, tile, out=bf, by="right"):
    T, M = left.shape
    N = right.shape[1]
    if by == "right":
        ins = [whole((T, M)), pl.BlockSpec((T, tile), lambda i: (0, i))]
        outs = pl.BlockSpec((M, tile), lambda i: (0, i))
        grid = (N // tile,)
    else:
        ins = [pl.BlockSpec((T, tile), lambda i: (0, i)), whole((T, N))]
        outs = pl.BlockSpec((tile, N), lambda i: (i, 0))
        grid = (M // tile,)
    return call(kernel_d1, name, grid, ins, outs, sds(M, N, dtype=out), 2 * T * M * N, 2 * (T * M + T * N + M * N))(left, right)


def attention_back(qkv, probs, do):
    T, D = do.shape
    return call(
        kernel_e, "attention_backward", (T // TILE,),
        [rows_of(3 * D), rows_of(2 * D), rows_of(D)],
        rows_of(3 * D), sds(T, 3 * D), 8 * T * D * D, 30 << 20,
    )(qkv, probs, do)


def input_grad(x, dqkv, dh, g1, w_qkv):
    T, D = x.shape
    return call(
        kernel_f, "input_grad", (T // TILE,),
        [rows_of(D), rows_of(3 * D), rows_of(D), whole((1, D)), whole(w_qkv.shape)],
        rows_of(D), sds(T, D),
        6 * T * D * D, 30 << 20,
    )(x, dqkv, dh, g1, w_qkv)


MESH = pl.DeviceIdType.MESH
D_MODEL = 768
P_B = 3
BACK = 256
EARLY = 6
MESSAGES = {
    "x0s": (0, 2, 0, "mine", None), "y0s": (0, 4, 0, "mine", None), "x0c": (0, 2, 0, "middle", None), "y0c": (0, 4, 0, "middle", None),
    "c0": (0, 1, 0, "all", None),
    "xf": (0, 4, 2, "mine", "x0s"), "xz": (1, 0, 2, "mine", "x0s"), "xcs": (0, 1, 2, "mine", "x0s"),
    "yz": (1, 0, 4, "mine", "y0s"), "ycs": (0, 1, 4, "mine", "y0s"),
    "xcc": (0, 1, 2, "middle", "x0c"), "yf": (0, 2, 4, "middle", "y0c"), "ycc": (0, 1, 4, "middle", "y0c"),
    "dz": (1, 0, 6, "mine", "xf"), "dcs": (0, 1, 6, "mine", "xf"), "dcc": (0, 1, 6, "middle", "yf"),
    "xcm": (0, 1, 2, "other", "xz"), "ycm": (0, 1, 4, "other", "yz"), "dcm": (0, 1, 6, "other", "dz"),
}
ARRIVALS = [None, "x0s", "y0s", "x0c", "y0c", "xf", "yf", "xz", "yz", "dz"]
RELAYS = {
    0: [0, 10, 1, 2, 20, 3, 4, 11, 12, 13, 14, 7, 21, 5, 8, 30, 23, 22, 17, 6, 24, 18, 16, 15, 40, 27, 31, 25, 9, 33, 32, 50, 28, 26, 34, 19],
    1: [41, 42, 37, 43, 44, 29, 60, 70],
    2: [51, 35, 38, 53, 52, 36, 54, 80],
    3: [47, 45, 46, 48, 62, 61, 64, 63, 90],
    4: [57, 72, 71, 100, 39, 74],
    5: [73, 58, 55, 56],
    6: [49, 82, 81, 68, 110, 84, 83],
    7: [67, 65, 66],
    8: [78, 92, 91, 77, 94],
    9: [93, 59, 75, 101],
    10: [88, 102, 103, 87],
    11: [104, 76, 69, 85, 111],
    12: [98, 112, 113, 97, 114, 86],
    13: [79, 95, 96, 107, 105, 106],
    14: [108, 115, 89, 116],
    15: [117, 118],
    16: [99, 109],
    17: [119],
}


class Gather:
    def __init__(self, shard, piece, send, recv, local, me, rep):
        self.shard, self.piece, self.send, self.recv, self.me, self.rep = shard, piece, send, recv, me, rep
        self.own = pltpu.make_async_copy(shard, piece(me), local)

    def copy(self, name):
        rep_to, me_to, whose, what, _ = MESSAGES[name]
        s = ARRIVALS.index(name) if name in ARRIVALS else 0
        third = D_MODEL // 3
        parity = self.rep % 2
        cols = {
            "all": lambda: pl.ds(0, D_MODEL),
            "mine": lambda: pl.ds(pl.multiple_of(parity * 2 * third, 128), third),
            "middle": lambda: pl.ds(third, third),
            "other": lambda: pl.ds(pl.multiple_of((1 - parity) * 2 * third, 128), third),
        }[what]()
        piece = self.piece(self.me ^ whose)
        src = self.shard if whose == 0 else piece
        return pltpu.make_async_remote_copy(
            src_ref=src.at[:, cols], dst_ref=piece.at[:, cols], send_sem=self.send, recv_sem=self.recv.at[s],
            device_id=(self.rep ^ rep_to, self.me ^ me_to), device_id_type=MESH,
        )

    def relay(self, arrival):
        if arrival is None:
            self.own.start()
        else:
            self.copy(arrival).wait_recv()
        for name, message in MESSAGES.items():
            if message[4] == arrival:
                self.copy(name).start()

    def complete(self):
        self.own.wait()
        four = self.piece(pl.ds(0, 4))
        pltpu.make_async_copy(four, four, self.recv.at[0]).wait()

    def finish(self):
        seven = self.piece(pl.ds(0, 7))
        pltpu.make_async_copy(seven, seven, self.send).wait()


class Local:
    def __init__(self, shard, place, local):
        self.own = pltpu.make_async_copy(shard, place, local)

    def relay(self, arrival):
        if arrival is None:
            self.own.start()

    def complete(self):
        self.own.wait()

    def finish(self):
        pass


def dispatch(step, table):
    keys = sorted(table)
    if len(keys) < 4:
        for k in keys:
            pl.when(step == k)(table[k])
    else:
        middle = keys[len(keys) // 2]
        pl.when(step < middle)(lambda: dispatch(step, {k: table[k] for k in keys if k < middle}))
        pl.when(step >= middle)(lambda: dispatch(step, {k: table[k] for k in keys if k >= middle}))


def flat(t):
    return t.reshape(t.shape[0] * t.shape[1], t.shape[2])


def gain_rows(ga, gm):
    n = ga.shape[1]
    row = lax.broadcasted_iota(jnp.int32, (16, n), 0)
    pair = jnp.where(row == 0, ga.astype(f32), jnp.where(row == 1, gm.astype(f32), 0.0))
    return jnp.concatenate([pair, jnp.zeros((16, 128 - n), f32)], axis=1).astype(bf)


def spread(pieces):
    width = D_MODEL // 8
    lane = lax.broadcasted_iota(jnp.int32, (128, D_MODEL), 0)
    place = lax.broadcasted_iota(jnp.int32, (128, D_MODEL), 1)
    total = jnp.zeros((16, D_MODEL), f32)
    for d in range(8):
        hit = (place == lane + d * width) & (lane < width)
        total = total + nn(pieces[d], jnp.where(hit, 1.0, 0.0).astype(bf))
    return total[:8]


def kernel_one(
    remote, lengths, x, dy, ga, gm, q_in, o_in, i_in, t_in,
    qkv_out, probs_out, u_out, h_out, wn_out, za_out, dh_out, do_out, gains_out, gwo_out, wq_out, wt_out,
    wq, wo, wi, wt, gain_piece, gain_parts, gains, high, low, qa, zs, mixed_all, wn, send, recv, gain_send, gain_recv, local, out_sem, a_sem, dz_sem, back_sem,
):
    step = pl.program_id(0)
    T, D = high.shape
    tiles = T // TILE
    p_h = P_B + tiles
    p_in, p_back = p_h + 2, p_h + 10
    steps = p_back + T // BACK
    me, rep = lax.axis_index("fsdp"), lax.axis_index("rep")
    part = lambda j: pl.ds(j * D, D)
    rows_of_part = lambda j: pl.ds(j * 96, 96)
    if remote:
        refs = [(q_in.at[:, part(j)], lambda p, j=j: wq.at[j, p]) for j in range(3)]
        refs += [(o_in, lambda p: wo.at[p])]
        refs += [(i_in.at[:, part(j)], lambda p, j=j: wi.at[j, p]) for j in range(4)]
        refs += [(t_in.at[rows_of_part(j)], lambda p, j=j: wt.at[p, rows_of_part(j)]) for j in range(4)]
        blocks = [Gather(s, f, send.at[k], recv.at[k], local.at[k], me, rep) for k, (s, f) in enumerate(refs)]
    else:
        refs = [(q_in.at[:, :, part(j)], wq.at[j]) for j in range(3)] + [(o_in, wo)]
        refs += [(i_in.at[:, :, part(j)], wi.at[j]) for j in range(4)]
        refs += [(t_in.at[:, rows_of_part(j)], wt.at[:, rows_of_part(j)]) for j in range(4)]
        blocks = [Local(s, f, local.at[k]) for k, (s, f) in enumerate(refs)]

    def gain_copy(d):
        return pltpu.make_async_remote_copy(
            src_ref=gain_piece, dst_ref=gain_parts.at[me], send_sem=gain_send.at[d], recv_sem=gain_recv.at[d],
            device_id=(rep, me ^ d), device_id_type=MESH,
        )

    load_x = pltpu.make_async_copy(x, high, local.at[13])
    export = pltpu.make_async_copy(wq, wq_out, out_sem.at[0])
    store_u = pltpu.make_async_copy(low, u_out, out_sem.at[1])
    store_wn = pltpu.make_async_copy(wn, wn_out, out_sem.at[2])
    store_h = [pltpu.make_async_copy(v, h_out.at[k], out_sem.at[7 + k]) for k, v in enumerate((high, low))]
    export_wt = pltpu.make_async_copy(wt, wt_out, out_sem.at[9])
    store_gwo = pltpu.make_async_copy(mixed_all.at[pl.ds(0, D)], gwo_out, out_sem.at[3])

    def store_qkv(j):
        cols = pl.ds(pl.multiple_of(j * D, D), D)
        return pltpu.make_async_copy(qa.at[:, cols], qkv_out.at[:, cols], out_sem.at[4 + j])

    def rows_at(t, n):
        return pl.ds(pl.multiple_of(t * n, n), n)

    def store_a(e):
        place = (rows_at(lax.rem(e, 2), T // 2), pl.ds(pl.multiple_of(lax.div(e, 2) * FC, FC), FC))
        return pltpu.make_async_copy(qa.at[place], za_out.at[(1, *place)], a_sem.at[e])

    def store_dz(t):
        return pltpu.make_async_copy(zs.at[rows_at(t, BACK)], za_out.at[0, rows_at(t, BACK)], dz_sem.at[t])

    def store_back(t):
        rows = rows_at(t, BACK)
        return [pltpu.make_async_copy(v.at[rows], to.at[rows], back_sem.at[k, t]) for k, (v, to) in enumerate(((high, dh_out), (low, do_out)))]

    def relay(code):
        blocks[code // 10].relay(ARRIVALS[code % 10])

    @pl.when(step == 0)
    def _():
        load_x.start()
        if remote:
            gain_piece[...] = gain_rows(ga[...], gm[...])
            barrier = pltpu.get_barrier_semaphore()
            for d in range(1, 8):
                pl.semaphore_signal(barrier, inc=1, device_id=(rep, me ^ d), device_id_type=MESH)
            pl.semaphore_signal(barrier, inc=1, device_id=(rep ^ 1, me), device_id_type=MESH)
            pl.semaphore_wait(barrier, 8)
            for d in range(1, 8):
                gain_copy(d).start()
        for code in RELAYS[0][:EARLY]:
            relay(code)
        if remote:
            gain_parts[me] = gain_piece[...]
            for d in range(1, 8):
                gain_copy(d).wait_recv()
        else:
            for d in range(8):
                gain_parts[d] = gain_rows(ga[d : d + 1], gm[d : d + 1])
        gains[...] = spread(gain_parts)
        gains_out[...] = gains[...]
        load_x.wait()
        later = RELAYS[0][EARLY:]
        for t in range(max(tiles, len(later))):
            if t < tiles:
                rows = pl.ds(t * TILE, TILE)
                n, _ = moments(high[rows, :].astype(f32))
                low[rows, :] = (n * gains[0:1]).astype(bf)
            if t < len(later):
                relay(later[t])
        store_u.start()
        blocks[0].complete()

    completes = {1: [1], 2: [2], p_h: [3], p_back: [8, 9, 10, 11]}
    completes.update({p_in + 2 * j: [4 + j] for j in range(4)})

    def begin(at):
        for code in RELAYS.get(at, []):
            relay(code)
        for k in completes.get(at, []):
            blocks[k].complete()
        if at == P_B:
            export.start()
        if at == p_h:
            store_u.wait()
        if at == p_back:
            export_wt.start()
            for store in store_h:
                store.wait()
        if at == p_in:
            store_wn.start()
            for store in store_h:
                store.start()
            for j in range(3):
                store_qkv(j).wait()

    dispatch(step, {at: functools.partial(begin, at) for at in {*RELAYS, *completes, P_B} - {0}})

    @pl.when(step < P_B)
    def _():
        w = flat(wq[step])
        block = 2 * TILE
        cols = pl.ds(pl.multiple_of(step * D, D), D)
        for t in range(T // block):
            qa[t * block : (t + 1) * block, cols] = nn(low[t * block : (t + 1) * block], w).astype(bf)
        store_qkv(step).start()

    @pl.when((step >= P_B) & (step < p_h))
    def _():
        t = step - P_B
        for rr in range(TILE // SPAN):
            rows = pl.ds(pl.multiple_of(t * TILE + rr * SPAN, SPAN), SPAN)
            mask = permitted(lengths, t * (TILE // SPAN) + rr)
            probs, mixed = attend(lambda c: qa[rows, c : c + 128], mask)
            for p in range(6):
                probs_out[rr * SPAN : (rr + 1) * SPAN, p * 2 * SPAN : (p + 1) * 2 * SPAN] = probs[p]
                mixed_all[rows, p * 128 : (p + 1) * 128] = mixed[p]

    @pl.when((step >= p_h) & (step < p_in))
    def _():
        for s in range(tiles // 2):
            rows = rows_at((step - p_h) * (tiles // 2) + s, TILE)
            h = high[rows, :].astype(f32) + nn(mixed_all[rows, :], flat(wo[...]))
            top = h.astype(bf)
            high[rows, :] = top
            low[rows, :] = (h - top.astype(f32)).astype(bf)
            n, _ = moments(h)
            wn[rows, :] = (n * gains[1:2]).astype(bf)

    @pl.when((step >= p_in) & (step < p_back))
    def _():
        e = step - p_in
        j, half = lax.div(e, 2), lax.rem(e, 2)
        cols = pl.ds(pl.multiple_of(j * FC, FC), FC)
        w = flat(wi[j])
        block = TILE
        for s in range(T // 2 // block):
            rows = rows_at(half * (T // 2 // block) + s, block)
            z = nn(wn[rows, :], w)
            qa[rows, cols] = gelu(z).astype(bf)
            zs[rows, cols] = z.astype(bf)
        store_a(e).start()

    per = FC // wt.shape[1]

    @pl.when(step >= p_back)
    def _():
        t = step - p_back
        rows = rows_at(t, BACK)
        h = high[rows, :].astype(f32) + low[rows, :].astype(f32)
        n, r = moments(h)
        dm = dy[...]
        dw = None
        for j in range(wi.shape[0]):
            cols = slice(j * FC, (j + 1) * FC)
            w_out = flat(wt[j * per : (j + 1) * per])
            dz = (nt(dm, w_out) * gelu_slope(zs[rows, cols].astype(f32))).astype(bf)
            zs[rows, cols] = dz
            add = nt(dz, flat(wi[j]))
            dw = add if dw is None else dw + add
        store_dz(t).start()
        dt = (dm.astype(f32) + norm_back(dw, n, r, gains[1:2])).astype(bf)
        high[rows, :] = dt
        low[rows, :] = nt(dt, flat(wo[...])).astype(bf)
        for store in store_back(t):
            store.start()

    @pl.when(step == steps - 1)
    def _():
        gwo = tn(mixed_all[...], high[...]).astype(bf)
        mixed_all[0:D, :] = gwo
        store_gwo.start()
        export.wait()
        export_wt.wait()
        store_wn.wait()
        for t in range(8):
            store_a(t).wait()
        for t in range(T // BACK):
            store_dz(t).wait()
            for store in store_back(t):
                store.wait()
        if remote:
            for d in range(1, 8):
                gain_copy(d).wait_send()
        for b in blocks:
            b.finish()
        store_gwo.wait()


def forward_and_mlp(remote, x, lengths, dy, ga, gm, w_qkv, w_ao, w_in, w_out):
    T, D = x.shape
    tiles = T // TILE
    F = w_in.shape[-1]
    rows = D // 8

    def tile_from(start, *shape):
        return pl.BlockSpec(shape, lambda i: (jnp.clip(i - start, 0, tiles - 1),) + (0,) * (len(shape) - 1))

    p_back = P_B + tiles + 10
    back_rows = pl.BlockSpec((BACK, D), lambda i: (jnp.clip(i - p_back, 0, T // BACK - 1), 0))
    whole = pl.BlockSpec(ga.shape, lambda i: (0, 0))
    hbm = pl.BlockSpec(memory_space=pl.ANY)

    return pl.pallas_call(
        functools.partial(kernel_one, remote),
        name="forward_and_mlp",
        grid=(p_back + T // BACK,),
        in_specs=[pl.BlockSpec(memory_space=pltpu.SMEM), hbm, back_rows, whole, whole, hbm, hbm, hbm, hbm],
        out_specs=[
            hbm, tile_from(P_B, TILE, 2 * D), hbm, hbm, hbm, hbm,
            hbm, hbm, pl.BlockSpec((8, D), lambda i: (0, 0)), hbm, hbm, hbm,
        ],
        out_shape=[
            sds(T, 3 * D), sds(T, 2 * D), sds(T, D),
            sds(2, T, D), sds(T, D), sds(2, T, F), sds(T, D), sds(T, D), sds(8, D, dtype=f32), sds(D, D), sds(3, 8, rows, D), sds(8, F // 8, D),
        ],
        scratch_shapes=[
            pltpu.VMEM((3, 8, rows, D), bf), pltpu.VMEM((8, rows, D), bf), pltpu.VMEM((F // FC, 8, rows, FC), bf),
            pltpu.VMEM((8, F // 8, D), bf), pltpu.VMEM((16, 128), bf), pltpu.VMEM((8, 16, 128), bf), pltpu.VMEM((8, D), f32), pltpu.VMEM((T, D), bf),
            pltpu.VMEM((T, D), bf), pltpu.VMEM((T, F), bf), pltpu.VMEM((T, F), bf), pltpu.VMEM((T, D), bf), pltpu.VMEM((T, D), bf),
            pltpu.SemaphoreType.DMA((12,)), pltpu.SemaphoreType.DMA((12, len(ARRIVALS))), pltpu.SemaphoreType.DMA((8,)), pltpu.SemaphoreType.DMA((8,)),
            pltpu.SemaphoreType.DMA((14,)), pltpu.SemaphoreType.DMA((10,)), pltpu.SemaphoreType.DMA((tiles,)), pltpu.SemaphoreType.DMA((T // BACK,)), pltpu.SemaphoreType.DMA((2, T // BACK)),
        ],
        cost_estimate=pl.CostEstimate(flops=12 * T * D * D + 8 * T * D * F + 6 * T * D * D, bytes_accessed=90 << 20, transcendentals=0),
        compiler_params=pltpu.CompilerParams(
            vmem_limit_bytes=VMEM, has_side_effects=remote, collective_id=1 if remote else None
        ),
    )(lengths.T, x, dy, ga, gm, w_qkv, w_ao, w_in, w_out)


CHUNK = 96
WIDE = 768
RING = 6
N_WIDE = 12
P_IN, P_OUT, P_ATT = 0, 4, 8
P_DX = P_ATT + 9
P_Y = P_DX + 4
STEPS = P_Y + 4
BLOCK = 512
REUSE = {P_ATT + 5: [0], P_ATT + 8: [1], P_DX + 2: [2, 3, 4, 5]}
START = [
    [1, 2, 5, 7, 9, 13, 15], [1, 3, 6, 11, 13, 15, 25], [2, 4, 6, 8, 10, 13, 16], [3, 6, 9, 10, 12, 14, 28],
    [5, 8, 10, 12, 14, 16, 23], [8, 9, 11, 13, 15, 16, 23], [8, 10, 13, 15, 16, 18, 22], [8, 13, 15, 16, 18, 20, 30],
    [11, 12, 15, 17, 19, 21, 25], [12, 13, 16, 18, 20, 22, 32], [12, 14, 16, 18, 20, 22, 24], [14, 15, 18, 19, 21, 23, 26],
    [14, 16, 19, 20, 22, 23, 27], [17, 18, 20, 21, 23, 24, 29], [17, 19, 21, 22, 23, 24, 27],
]
RECEIVE = {"s1": 0, "s2x": 1, "s2y": 1, "s3y": 2, "s3x": 2, "z1": 3, "z2": 4, "z3": 3}


def slot_of(k):
    return k if k < 10 else k - 10


class Reduce:
    def __init__(self, n, grads, bufs, send, recv, place):
        self.n = n
        k = n if n < 9 else 9 + (n - 9) // 2
        cols = pl.ds(0, WIDE) if n < 9 else pl.ds((n - 9) % 2 * (WIDE // 2), WIDE // 2)
        first, x2, y2, y3, x3, outer, inner, out = bufs
        r = k % RING
        self.g = grads.at[slot_of(k), :, :, :, :, cols]
        self.first = first.at[r, :, :, :, cols]
        self.x2, self.y2 = x2.at[r, :, :, cols], y2.at[r, :, :, cols]
        self.x3, self.y3 = x3.at[k, :, cols], y3.at[k, :, cols]
        self.outer, self.inner, self.out = outer.at[k, :, cols], inner.at[k, :, cols], out.at[k, :, cols]
        self.send, self.recv = send, recv
        self.y, self.x, self.c, self.me, self.rep = place
        self.is_inner = (self.rep == 1) | (self.rep == 2)

    def copy(self, m):
        g, y, x, c = self.g, self.y, self.x, self.c
        upper, lower = pl.ds(0, CHUNK // 2), pl.ds(CHUNK // 2, CHUNK // 2)
        src, dst, rep_to, me_to = {
            "s1": lambda: (g.at[:, :, 1 - c], self.first, 0, 1),
            "s2x": lambda: (g.at[:, 1 - x, c, upper], self.x2, 0, 2),
            "s2y": lambda: (g.at[1 - y, :, c, lower], self.y2, 0, 4),
            "s3y": lambda: (g.at[1 - y, x, c, upper], self.y3, 0, 4),
            "s3x": lambda: (g.at[y, 1 - x, c, lower], self.x3, 0, 2),
            "z1": lambda: (g.at[y, x, c], self.outer, 1, 0),
            "z2": lambda: (g.at[y, x, c], self.inner, 3, 0),
            "z3": lambda: (self.out, self.out, 1, 0),
        }[m]()
        return pltpu.make_async_remote_copy(
            src_ref=src, dst_ref=dst, send_sem=self.send.at[self.n, int(m == "z3")], recv_sem=self.recv.at[self.n, RECEIVE[m]],
            device_id=(self.rep ^ rep_to, self.me ^ me_to), device_id_type=MESH,
        )

    def start(self, *names):
        for m in names:
            self.copy(m).start()

    def arrived(self, m, ref):
        pltpu.make_async_copy(ref, ref, self.recv.at[self.n, RECEIVE[m]]).wait()

    def stage(self, s):
        g, y, x, c = self.g, self.y, self.x, self.c
        upper, lower = pl.ds(0, CHUNK // 2), pl.ds(CHUNK // 2, CHUNK // 2)
        if s == 1:
            self.start("s1")
        elif s == 2:
            self.arrived("s1", self.first)
            for b in range(2):
                for a in range(2):
                    g[b, a, c] += self.first[b, a]
            self.start("s2x", "s2y")
        elif s == 3:
            self.arrived("s2x", g.at[0, 0])
            for b in range(2):
                g[b, x, c, upper] += self.x2[b]
                g[y, b, c, lower] += self.y2[b]
            self.start("s3y", "s3x")
        elif s == 4:
            self.arrived("s3y", g.at[0, 0, 0])
            g[y, x, c, upper] += self.y3[...]
            g[y, x, c, lower] += self.x3[...]

            @pl.when(jnp.logical_not(self.is_inner))
            def _():
                self.start("z1")
        elif s == 5:
            @pl.when(self.is_inner)
            def _():
                self.arrived("z1", self.outer)
                g[y, x, c] += self.outer[...]
                self.start("z2")
        elif s == 6:
            @pl.when(self.is_inner)
            def _():
                self.arrived("z2", self.inner)
                self.out[...] = g[y, x, c] + self.inner[...]
                self.start("z3")
        elif s == 7:
            @pl.when(jnp.logical_not(self.is_inner))
            def _():
                self.arrived("z3", self.out)

    def sent(self):
        pltpu.make_async_copy(self.g, self.g, self.send.at[self.n, 0]).wait()

    def sum_sent(self):
        @pl.when(self.is_inner)
        def _():
            pltpu.make_async_copy(self.out, self.out, self.send.at[self.n, 1]).wait()


def part_of(e):
    return 2 * lax.div(e, 3) + jnp.minimum(lax.rem(e, 3), 1), lax.rem(e, 3) == 2


def kernel_two(
    gwo_in, wn, dm, u, wq, wt, gains, za, qkv, probs, do, x, dh, h,
    dx_out, y_out, out_hbm,
    out, big_a, big_b, wq_s, dqkv, grads, first, x2, y2, y3, x3, outer, inner, stream, halves, result,
    send, recv, local, load_sem, store_sem,
):
    step = pl.program_id(0)
    T, D = big_a.shape
    me, rep = lax.axis_index("fsdp"), lax.axis_index("rep")
    place = (me // 4, (me // 2) % 2, me % 2, me, rep)
    bufs = (first, x2, y2, y3, x3, outer, inner, out)
    chunks = [Reduce(n, grads, bufs, send, recv, place) for n in range(len(START))]
    load_gwo = pltpu.make_async_copy(gwo_in, grads.at[0], local.at[0])
    load_wn = pltpu.make_async_copy(wn, big_a, local.at[1])
    load_dm = pltpu.make_async_copy(dm, big_b, local.at[2])
    load_u = pltpu.make_async_copy(u, big_a, local.at[3])
    load_wq = pltpu.make_async_copy(wq, wq_s, local.at[4])
    store_out = pltpu.make_async_copy(out, out_hbm, local.at[5])
    load_wt = pltpu.make_async_copy(wt, grads.at[pl.ds(2, 4)], local.at[6])

    def loads(at):
        s = at % 2
        to = stream.at[s]
        if at < P_ATT:
            pairs = [(za.at[at // 4, :, pl.ds(at % 4 * WIDE, WIDE)], to)]
        elif at < P_DX:
            e = at - P_ATT
            if e % 3 == 2:
                return []
            p = e // 3 * 2 + e % 3
            pairs = [(qkv.at[:, pl.ds(j * D + p * 128, 128)], to.at[:, pl.ds(j * 128, 128)]) for j in range(3)]
            pairs.append((do.at[:, pl.ds(p * 128, 128)], to.at[:, pl.ds(384, 128)]))
            pairs.append((probs.at[:, pl.ds(p * 256, 256)], to.at[:, pl.ds(512, 256)]))
        elif at < P_Y:
            rows = pl.ds((at - P_DX) * BLOCK, BLOCK)
            pairs = [(x.at[rows], to.at[pl.ds(0, BLOCK)]), (dh.at[rows], to.at[pl.ds(BLOCK, BLOCK)])]
        else:
            rows = pl.ds((at - P_Y) * BLOCK, BLOCK)
            pairs = [(za.at[1, rows, pl.ds(j * WIDE, WIDE)], to.at[pl.ds(j * BLOCK, BLOCK)]) for j in range(4)]
            pairs.append((h.at[:, rows], halves.at[s]))
        return [pltpu.make_async_copy(src, dst, load_sem.at[s, k]) for k, (src, dst) in enumerate(pairs)]

    def store(at):
        to, t = (dx_out, at - P_DX) if at < P_Y else (y_out, at - P_Y)
        return pltpu.make_async_copy(result.at[at % 2], to.at[pl.ds(t * BLOCK, BLOCK)], store_sem.at[at % 2])

    acts = {}
    for n, starts in enumerate(START):
        for s, at in enumerate(starts):
            acts.setdefault(at, []).append((n, s + 1))

    def act(at):
        for n, s in sorted(acts[at], key=lambda ns: -ns[1]):
            chunks[n].stage(s)

    def begin(at):
        if at == 0:
            load_wn.start()
            for load in loads(0):
                load.start()
            barrier = pltpu.get_barrier_semaphore()
            for to in ((rep, me ^ 1), (rep, me ^ 2), (rep, me ^ 4), (rep ^ 1, me), (rep ^ 3, me)):
                pl.semaphore_signal(barrier, inc=1, device_id=to, device_id_type=MESH)
            pl.semaphore_wait(barrier, 5)
            load_wn.wait()
        for load in loads(at):
            load.wait()
        if at == 0:
            load_gwo.start()
        if at + 1 < STEPS:
            for load in loads(at + 1):
                load.start()
        if at == 1:
            load_dm.start()
            load_gwo.wait()
        if at in acts:
            act(at)
        if at == P_OUT:
            load_u.start()
            load_dm.wait()
        if at == P_OUT + 1:
            load_wq.start()
        if at == P_ATT + 2:
            load_u.wait()
            load_wq.wait()
        for k in REUSE.get(at, []):
            chunks[k].sent()
        if at == P_DX + 2:
            load_wt.start()
        if at == P_Y:
            load_wt.wait()
        if at >= P_DX + 2:
            store(at - 2).wait()

    dispatch(step, {at: functools.partial(begin, at) for at in range(STEPS)})

    slot = lax.rem(step, 2)

    @pl.when(step < P_OUT)
    def _():
        g = tn(big_a[...], stream[slot]).astype(bf)
        grads[1 + step] = g.reshape(2, 2, 2, CHUNK, WIDE)

    @pl.when((step >= P_OUT) & (step < P_ATT))
    def _():
        j = step - P_OUT
        g = tn(stream[slot], big_b[...]).astype(bf).reshape(2, 4, CHUNK, WIDE)
        for part in range(4):
            grads[5 + part, j // 2, j % 2] = g[:, part]

    pair, product = part_of(step - P_ATT)
    attention = (step >= P_ATT) & (step < P_DX)

    @pl.when(attention & jnp.logical_not(product))
    def _():
        for rr in range(T // SPAN):
            rows = slice(rr * SPAN, (rr + 1) * SPAN)
            q2, k2, v2, do2 = (stream[slot, rows, j * 128 : (j + 1) * 128] for j in range(4))
            back = attend_back(q2, k2, v2, stream[slot, rows, 512:768], do2)
            for j in range(3):
                to_cols = pl.ds(pl.multiple_of(lax.rem(pair, 2) * (WIDE // 2) + j * 128, 128), 128)
                dqkv[lax.div(pair, 2), rows, to_cols] = back[j]

    @pl.when(attention & product)
    def _():
        k = lax.div(pair, 2)
        g = tn(big_a[...], dqkv[k]).astype(bf)
        grads[jnp.where(k == 0, 9, k - 1)] = g.reshape(2, 2, 2, CHUNK, WIDE)

    @pl.when((step >= P_DX) & (step < P_Y))
    def _():
        for part in range(BLOCK // TILE):
            here = slice(part * TILE, (part + 1) * TILE)
            rows = pl.ds(pl.multiple_of((step - P_DX) * BLOCK + part * TILE, TILE), TILE)
            n, r = moments(stream[slot, here].astype(f32))
            du = 0.0
            for j in range(3):
                at = [(p // 2, (p % 2) * (WIDE // 2) + j * 128) for p in range(D // 128)]
                du = du + nt(jnp.concatenate([dqkv[k, rows, c : c + 128] for k, c in at], axis=1), flat(wq_s[j]))
            dt = stream[slot, BLOCK + part * TILE : BLOCK + (part + 1) * TILE].astype(f32)
            result[slot, here] = (dt + norm_back(du, n, r, gains[0:1])).astype(bf)
        for at in range(P_DX, P_Y):
            @pl.when(step == at)
            def _(at=at):
                store(at).start()

    @pl.when(step >= P_Y)
    def _():
        y = halves[slot, 0].astype(f32) + halves[slot, 1].astype(f32)
        for j in range(4):
            y = y + nn(stream[slot, j * BLOCK : (j + 1) * BLOCK], grads[2 + j].reshape(WIDE, WIDE))
        result[slot] = y.astype(bf)
        for at in range(P_Y, STEPS):
            @pl.when(step == at)
            def _(at=at):
                store(at).start()

    @pl.when(step == STEPS - 1)
    def _():
        for at in sorted(acts):
            if at >= STEPS:
                act(at)
        store_out.start()
        for n in range(len(START)):
            if n not in sum(REUSE.values(), []):
                chunks[n].sent()
            chunks[n].sum_sent()
        for at in (STEPS - 2, STEPS - 1):
            store(at).wait()
        store_out.wait()


def gradients(gwo, wn, dy, u, wq, wt, gains, za, qkv, probs, do, x, dh, h):
    T, D = x.shape
    hbm = pl.BlockSpec(memory_space=pl.ANY)
    wide = lambda *shape: pltpu.VMEM(shape + (WIDE,), bf)
    return pl.pallas_call(
        kernel_two,
        name="gradients",
        grid=(STEPS,),
        in_specs=[hbm] * 6 + [pl.BlockSpec((8, D), lambda i: (0, 0))] + [hbm] * 7,
        out_specs=[hbm] * 3,
        out_shape=[sds(T, D), sds(T, D), sds(N_WIDE, CHUNK, WIDE)],
        scratch_shapes=[
            wide(N_WIDE, CHUNK), wide(T), wide(T), pltpu.VMEM(wq.shape, bf), wide(3, T),
            wide(10, 2, 2, 2, CHUNK), wide(RING, 2, 2, CHUNK), wide(RING, 2, CHUNK // 2),
            wide(RING, 2, CHUNK // 2), wide(N_WIDE, CHUNK // 2), wide(N_WIDE, CHUNK // 2), wide(N_WIDE, CHUNK), wide(N_WIDE, CHUNK),
            wide(2, T), wide(2, 2, BLOCK), wide(2, BLOCK),
            pltpu.SemaphoreType.DMA((len(START), 2)), pltpu.SemaphoreType.DMA((len(START), 5)), pltpu.SemaphoreType.DMA((7,)),
            pltpu.SemaphoreType.DMA((2, 5)), pltpu.SemaphoreType.DMA((2,)),
        ],
        cost_estimate=pl.CostEstimate(flops=8 * T * D * D + 4 * T * D * 4 * D + 20 * T * D * D, bytes_accessed=90 << 20, transcendentals=0),
        compiler_params=pltpu.CompilerParams(vmem_limit_bytes=VMEM, has_side_effects=True, collective_id=2),
    )(gwo.reshape(2, 2, 2, CHUNK, WIDE), wn, dy, u, wq, wt.reshape(4, 2, 2, 2, CHUNK, WIDE), gains, za, qkv, probs, do, x, dh, h)


def kernel_finish(
    sums_in, wq_in, wi_in, ga, gm, y, dx, y_out, dx_out, gq_out, gwo_out, gwi_out, gwt_out, gg1, gg2,
    hold, sums, wq, wi, gq, gwo, gwi, gwt, sem, load_sem, store_sem,
):
    parts = sem.shape[2]
    n = y.shape[0] // parts
    loads = [pltpu.make_async_copy(src, dst, load_sem.at[k]) for k, (src, dst) in enumerate(((sums_in, sums), (wq_in, wq), (wi_in, wi)))]
    moves = []
    for p in range(parts):
        for k, (src, dst) in enumerate(((y, y_out), (dx, dx_out))):
            rows = pl.ds(p * n, n)
            there = pltpu.make_async_copy(src.at[rows], hold.at[k, rows], sem.at[0, k, p])
            moves.append((there, pltpu.make_async_copy(hold.at[k, rows], dst.at[rows], sem.at[1, k, p])))
    for load in loads:
        load.start()
    for there, _ in moves:
        there.start()
    stores = [pltpu.make_async_copy(src, dst, store_sem.at[k]) for k, (src, dst) in enumerate(((gwt, gwt_out), (gwi, gwi_out), (gq, gq_out), (gwo, gwo_out)))]
    D = gwo.shape[1]
    loads[0].wait()
    for j in range(4):
        gwt[j * CHUNK : (j + 1) * CHUNK, :] = sums[5 + j].astype(f32)
    stores[0].start()
    for j in range(4):
        gwi[:, j * D : (j + 1) * D] = sums[1 + j].astype(f32)
    stores[1].start()
    for pair in range(D // 128):
        for j in range(3):
            cols = (pair % 2) * (WIDE // 2) + j * 128
            gq[:, j * D + pair * 128 : j * D + pair * 128 + 128] = sums[9 + pair // 2, :, cols : cols + 128].astype(f32)
    stores[2].start()
    gwo[...] = sums[0].astype(f32)
    stores[3].start()
    for there, out in moves:
        there.wait()
        out.start()
    loads[1].wait()
    loads[2].wait()
    for grad, w, gain, out in ((gq, wq, ga, gg1), (gwi, wi, gm, gg2)):
        acc = jnp.zeros((CHUNK, 128), f32)
        for c in range(0, w.shape[1], 128):
            acc = acc + w[:, c : c + 128].astype(f32) * grad[:, c : c + 128]
        out[...] = jnp.sum(acc.T, axis=0, keepdims=True) / gain[...].astype(f32)
    for store in stores:
        store.wait()
    for _, out in moves:
        out.wait()


def finish(sums, w_qkv, w_mlp_in, gain_attn, gain_mlp, y, dx):
    rows, D = w_qkv.shape[0], w_qkv.shape[1] // 3
    vmem, hbm = pl.BlockSpec(memory_space=pltpu.VMEM), pl.BlockSpec(memory_space=pl.ANY)
    shapes = [(rows, 3 * D), (rows, D), (rows, 4 * D), (4 * rows, D)]
    fs = functools.partial(sds, dtype=f32)
    y, dx, gq, gwo, gwi, gwt, gg1, gg2 = pl.pallas_call(
        kernel_finish,
        name="finish",
        in_specs=[hbm] * 3 + [vmem] * 2 + [hbm] * 2,
        out_specs=[hbm] * 6 + [vmem] * 2,
        out_shape=[sds(*y.shape), sds(*dx.shape), *(fs(*shape) for shape in shapes), fs(1, rows), fs(1, rows)],
        scratch_shapes=[
            pltpu.VMEM((2, *y.shape), bf), pltpu.VMEM(sums.shape, bf), pltpu.VMEM(w_qkv.shape, bf), pltpu.VMEM(w_mlp_in.shape, bf),
            *(pltpu.VMEM(shape, f32) for shape in shapes),
            pltpu.SemaphoreType.DMA((2, 2, 4)), pltpu.SemaphoreType.DMA((3,)), pltpu.SemaphoreType.DMA((4,)),
        ],
        cost_estimate=pl.CostEstimate(flops=1 << 20, bytes_accessed=20 << 20, transcendentals=0),
        compiler_params=pltpu.CompilerParams(vmem_limit_bytes=VMEM),
    )(sums, w_qkv, w_mlp_in, gain_attn.reshape(1, rows), gain_mlp.reshape(1, rows), y, dx)
    return y, dx, gg1.reshape(rows), gq, gwo, gg2.reshape(rows), gwi, gwt


def shards(x, lengths, segments, gain_attn, w_qkv, w_attn_out, gain_mlp, w_mlp_in, w_mlp_out, dy):
    D = x.shape[1]
    remote = lax.axis_size("fsdp") == 8 and lax.axis_size("rep") == 4
    ga, gm = gain_attn.reshape(1, -1), gain_mlp.reshape(1, -1)
    weights = (w_qkv, w_attn_out, w_mlp_in, w_mlp_out)
    if not remote:
        weights = tuple(lax.all_gather(v, "fsdp", axis=0, tiled=True) for v in weights)
        weights = tuple(v.reshape(8, v.shape[0] // 8, v.shape[1]) for v in weights)
        ga, gm = (lax.all_gather(v, "fsdp", axis=0, tiled=True).reshape(8, -1) for v in (gain_attn, gain_mlp))
    qkv, probs, u, h, wn, za, dh, do, gains, gwo, wq, wt = forward_and_mlp(remote, x, lengths, dy, ga, gm, *weights)
    if remote:
        dx, y, sums = gradients(gwo, wn, dy, u, wq, wt, gains, za, qkv, probs, do, x, dh, h)
        return finish(sums, w_qkv, w_mlp_in, gain_attn, gain_mlp, y, dx)
    scatter = lambda v: lax.psum_scatter(v, "fsdp", scatter_dimension=0, tiled=True)
    gwt = scatter(weight_grad(za[1], dy, "mlp_out_grad", 768, bf, "left"))
    gwi = scatter(weight_grad(wn, za[0], "mlp_in_grad", 768))
    gwo = scatter(gwo)
    dqkv = attention_back(qkv, probs, do)
    gq = scatter(weight_grad(u, dqkv, "qkv_grad", 768))
    dx = input_grad(x, dqkv, dh.astype(f32), gains[0:1], wq.transpose(1, 2, 0, 3).reshape(D, 3 * D))
    y = jnp.sum(h.astype(f32), axis=0) + jnp.dot(za[1], wt.reshape(-1, D), preferred_element_type=f32)
    y = y.astype(bf)
    gwt, gwi, gwo, gq = lax.psum((gwt, gwi, gwo, gq), "rep")
    gwt, gwi, gwo, gq = (v.astype(f32) for v in (gwt, gwi, gwo, gq))
    gg1 = jnp.sum(w_qkv.astype(f32) * gq, axis=1) / gain_attn.astype(f32)
    gg2 = jnp.sum(w_mlp_in.astype(f32) * gwi, axis=1) / gain_mlp.astype(f32)
    return y, dx, gg1, gq, gwo, gg2, gwi, gwt


def solution(mesh):
    tokens, cut, vec = P(("rep", "fsdp"), None), P("fsdp", None), P("fsdp")
    return jax.shard_map(
        shards,
        mesh=mesh,
        in_specs=(tokens, tokens, P(("rep", "fsdp")), vec, cut, cut, vec, cut, cut, tokens),
        out_specs=(tokens, tokens, vec, cut, cut, vec, cut, cut),
        check_vma=False,
    )
```
